128 devices in a mesh: dp: 16 (over z_lo, y, core), tensor: 8 (over z_hi, x).
Axes of the slice: x: 4, y: 4, z: 4 (z_hi: 2, z_lo: 2; z = z_hi * 2 + z_lo), core: 2. Of those that a mesh axis runs over, the one named last changes fastest.
Arguments:
- hidden_in: bfloat16 [16, 1024, 2048], P('dp', None, 'tensor'), may hold values from -6 to 6
- cotangent: bfloat16 [16, 1024, 2048], P('dp', None, 'tensor'), may hold values from -6 to 6
- sequence_order: int32 [16], replicated, may hold values from 0 to 15, each once
- seq_lengths: int32 [16], replicated, may hold values from 1 to 1024, 12288 in all
- expert_ids: int32 [16, 1024, 2], replicated, may hold values from 0 to 3, all different within a row
- gate_weights: float32 [16, 1024, 2], replicated, may hold values from 0.2 to 1
- w_query: bfloat16 [2048, 2048], P(None, 'tensor'), may hold values from -0.125 to 0.125
- w_key: bfloat16 [2048, 2048], P(None, 'tensor'), may hold values from -0.125 to 0.125
- w_value: bfloat16 [2048, 2048], P(None, 'tensor'), may hold values from -0.125 to 0.125
- w_output: bfloat16 [2048, 2048], P('tensor'), may hold values from -2 to 2
- gain_attn: float32 [2048], replicated, may hold values from 0.5 to 1.5
- gain_query: float32 [2048], P('tensor'), may hold values from 0.5 to 1.5
- gain_key: float32 [2048], P('tensor'), may hold values from 0.5 to 1.5
- gain_mlp: float32 [2048], replicated, may hold values from 0.5 to 1.5
- w_gate: bfloat16 [4, 2048, 1024], P(None, None, 'tensor'), may hold values from -0.125 to 0.125
- w_up: bfloat16 [4, 2048, 1024], P(None, None, 'tensor'), may hold values from -0.125 to 0.125
- w_down: bfloat16 [4, 1024, 2048], P(None, 'tensor'), may hold values from -0.1875 to 0.1875
Outputs:
- output: bfloat16 [16, 1024, 2048], P('dp', None, 'tensor')
- grad_input: bfloat16 [16, 1024, 2048], P('dp', None, 'tensor')
- grad_w_query: float32 [2048, 2048], P(None, 'tensor')
- grad_w_key: float32 [2048, 2048], P(None, 'tensor')
- grad_w_value: float32 [2048, 2048], P(None, 'tensor')
- grad_w_output: float32 [2048, 2048], P('tensor')
- grad_gain_attn: float32 [2048], replicated
- grad_gain_query: float32 [2048], P('tensor')
- grad_gain_key: float32 [2048], P('tensor')
- grad_gain_mlp: float32 [2048], replicated
- grad_w_gate: float32 [4, 2048, 1024], P(None, None, 'tensor')
- grad_w_up: float32 [4, 2048, 1024], P(None, None, 'tensor')
- grad_w_down: float32 [4, 1024, 2048], P(None, 'tensor')
The draws below stay inside these ranges and needn't reach their ends.
Inputs may be any that keep to these rules, and one draw needn't show every extreme that they name: `sequence_order`: each sequence is named once. `seq_lengths`: some sequence has exactly 1024 tokens; the lengths sum to 12288. `expert_ids`: the 2 experts of a token differ.
All inputs are finite; a program needn't handle non-finite values.
Results may differ from the reference program's by a relative error of at most 0.03.
Values may be sent and summed in bfloat16 or wider, within the bound.
No kernel may reach another device: no remote copies, remote signals or barrier semaphores. Data moves between devices by JAX's collectives and lax.ppermute only.
A program may use at most 320 MiB of HBM per device.

```python
import math
import jax
import jax.numpy as jnp
import numpy as np
from jax import lax

D = 2048
HEADS = 16
HEAD_DIM = 128
FF = 1024
EXPERTS = 4
TOP = 2
LEN = 1024
SEQ_GRP = 1
SEQS = 16
GROUP_TOK = 1024
CAP = 512
QW = 2048
N_DP = 16
N_TENSOR = 8


def block_levels(rng, dims, split, least, largest):
    gain = 1.0
    for dim, shards_of in split:
        steps = jax.random.uniform(jax.random.fold_in(jax.random.fold_in(rng, 6), dim), (shards_of,), jnp.float32, least / len(split), largest / len(split))
        gain = gain * jnp.repeat(jnp.exp(steps), dims[dim] // shards_of).reshape((-1,) + (1,) * (len(dims) - 1 - dim))
    return gain


def choose_distinct(rng, rows, number_of, top, lift):
    order = jax.random.permutation(jax.random.fold_in(rng, 1), number_of)
    pull = order
    for power in range(3):
        pull = pull * pull // number_of
    pull = pull * lift // number_of
    tickets = jax.random.randint(jax.random.fold_in(rng, 2), (rows, number_of), 0, 4096) + pull
    holders = jax.random.permutation(jax.random.fold_in(rng, 3), rows)[jnp.arange(number_of) % rows]
    tickets = jnp.where(jnp.arange(rows)[:, None] == holders[None, :], 1 << 14, tickets)
    score = tickets * number_of + jnp.arange(number_of)
    return lax.top_k(score.astype(jnp.int32), top)[1].astype(jnp.int32)


def profile(amount, total, reach, slope):
    weights = [(1 << 20) // math.isqrt(grade ** slope) + 1 for grade in range(2, amount + 1)]
    surplus, holding = total - reach - (amount - 1), [1] * (amount - 1)
    while surplus > 0:
        candidates = [i for i in range(amount - 1) if holding[i] < reach]
        pool, budget = sum([weights[i] for i in candidates]), surplus
        for i in candidates:
            more = min(reach - holding[i], max(1, budget * weights[i] // pool), surplus)
            holding[i] = holding[i] + more
            surplus = surplus - more
    return np.array([reach] + holding)


def ragged(key, number_of, total, bound, skew):
    if number_of == 2:
        one = jax.random.randint(key, (), max(1, total - bound), min(bound, total - 1) + 1)
        return jnp.stack([one, total - one])
    tallies = jnp.asarray(profile(number_of, total, bound, skew), jnp.int32)
    pairs = (number_of - 1) // 2
    source_of, sink = tallies[1:1 + 2 * pairs:2], tallies[2:2 + 2 * pairs:2]
    margin = jnp.minimum(source_of - 1, bound - sink)
    passed = jax.random.randint(jax.random.fold_in(key, 1), (pairs,), 0, 1 << 20) % (margin + 1)
    tallies = tallies.at[1:1 + 2 * pairs:2].set(source_of - passed).at[2:2 + 2 * pairs:2].set(sink + passed)
    return tallies[jax.random.permutation(jax.random.fold_in(key, 2), number_of)]


def bell_draw(rng, shape, scale, reach, cuts=(), held_as=jnp.bfloat16):
    loudness = block_levels(rng, shape, cuts, -0.22, 0.18) if cuts else 1.0
    array = jax.random.normal(rng, shape, jnp.float32) * scale * loudness
    return jnp.minimum(jnp.maximum(array, -reach), reach).astype(held_as)


def setup_inputs(seed: int = 0) -> dict:
    key_of = jax.random.split(jax.random.key(seed), 18)
    return {
        "hidden_in": bell_draw(key_of[0], (SEQS, LEN, D), 1.0, 6.0, ((0, 16), (2, 8))),
        "cotangent": bell_draw(key_of[1], (SEQS, LEN, D), 1.0, 6.0, ((0, 16), (2, 8))),
        "sequence_order": jax.random.permutation(key_of[2], SEQS).astype(jnp.int32),
        "seq_lengths": ragged(key_of[3], SEQS, SEQS * LEN * 3 // 4, LEN, 2).astype(jnp.int32),
        "expert_ids": choose_distinct(key_of[4], SEQS * LEN, EXPERTS, TOP, 4096).reshape((SEQS, LEN, TOP)),
        "gate_weights": jnp.clip(jax.random.uniform(key_of[5], (SEQS, LEN, TOP), jnp.float32, 0.2, 1.0), 0.2, 1.0),
        "w_query": bell_draw(key_of[6], (D, QW), D ** -0.5, 0.125, ((1, 8),)),
        "w_key": bell_draw(key_of[7], (D, QW), D ** -0.5, 0.125, ((1, 8),)),
        "w_value": bell_draw(key_of[8], (D, QW), D ** -0.5, 0.125, ((1, 8),)),
        "w_output": bell_draw(key_of[9], (QW, D), (max(D // 256, 2)) ** -0.5, 2.0, ((0, 8),)),
        "gain_attn": jnp.clip(1.0 + 0.1 * jax.random.normal(key_of[10], (D,), jnp.float32), 0.5, 1.5),
        "gain_query": jnp.clip(1.0 + 0.1 * jax.random.normal(key_of[11], (QW,), jnp.float32), 0.5, 1.5),
        "gain_key": jnp.clip(1.0 + 0.1 * jax.random.normal(key_of[12], (QW,), jnp.float32), 0.5, 1.5),
        "gain_mlp": jnp.clip(1.0 + 0.1 * jax.random.normal(key_of[13], (D,), jnp.float32), 0.5, 1.5),
        "w_gate": bell_draw(key_of[14], (EXPERTS, D, FF), D ** -0.5, 0.125, ((2, 8),)),
        "w_up": bell_draw(key_of[15], (EXPERTS, D, FF), D ** -0.5, 0.125, ((2, 8),)),
        "w_down": bell_draw(key_of[16], (EXPERTS, FF, D), FF ** -0.5, 0.1875, ((1, 8),)),
    }


EPS = 1e-06
BASE = 50000.0
HIGH = lax.Precision.HIGHEST

@jax.custom_vjp
def low(v):
    return lax.optimization_barrier(v.astype(jnp.bfloat16)).astype(jnp.float32)

@jax.custom_vjp
def low_back(v):
    return v

def low_keep(v):
    return (low(v), None)

def low_pass(kept, grad):
    return (grad,)

def back_keep(v):
    return (v, None)

def back_low(kept, grad):
    return (low(grad),)
low.defvjp(low_keep, low_pass)
low_back.defvjp(back_keep, back_low)

def matmul(left, right):
    return jnp.matmul(left, right, precision=HIGH)

def normalize(values):
    return values * lax.rsqrt(lax.optimization_barrier(jnp.mean(values * values, axis=-1, keepdims=True)) + EPS)

def rope_tables():
    half_dim = HEAD_DIM // 2
    frequency = BASE ** (-2.0 * jnp.arange(half_dim, dtype=jnp.float32) / HEAD_DIM)
    angles = jnp.arange(LEN, dtype=jnp.float32)[:, None] * frequency[None, :]
    return (jnp.cos(angles), jnp.sin(angles))

def rotate(values, cosine_table, sine_table):
    half_dim = HEAD_DIM // 2
    front_half = values[..., :half_dim]
    back_half = values[..., half_dim:]
    cosine_part = cosine_table[:, None, :]
    sine_part = sine_table[:, None, :]
    return jnp.concatenate([front_half * cosine_part - back_half * sine_part, back_half * cosine_part + front_half * sine_part], axis=-1)

def plan_slots(choice_ids):
    token_count = choice_ids.shape[0]
    flat_ids = choice_ids.reshape(-1).astype(jnp.int32)
    expert_range = jnp.arange(EXPERTS, dtype=jnp.int32)
    one_hot = (flat_ids[:, None] == expert_range[None, :]).astype(jnp.int32)
    earlier = (jnp.cumsum(one_hot, axis=0) - one_hot).astype(jnp.int32)
    position = lax.optimization_barrier(jnp.sum(earlier * one_hot, axis=1)).astype(jnp.int32)
    slot_of = jnp.where(position < CAP, flat_ids * CAP + position, EXPERTS * CAP).astype(jnp.int32)
    owners = (jnp.arange(token_count * TOP, dtype=jnp.int32) // TOP).astype(jnp.int32)
    slot_token = jnp.full((EXPERTS * CAP + 1,), token_count, jnp.int32).at[slot_of].set(owners)
    return (slot_of.reshape(token_count, TOP), slot_token[:EXPERTS * CAP])

def group_forward(work_x, weights, lengths_here, slot_of, slot_token, gates_here):
    w_query, w_key, w_value, w_output, gain_attn, gain_query, gain_key, gain_mlp, w_gate, w_up, w_down = weights
    head_cols = QW // N_TENSOR
    hidden_cols = FF // N_TENSOR
    cosine_table, sine_table = rope_tables()
    attn_in = low(normalize(work_x) * gain_attn)
    query_list = []
    key_list = []
    value_list = []
    for group_rank in range(N_TENSOR):
        branch_in = low_back(attn_in)
        column_range = slice(group_rank * head_cols, (group_rank + 1) * head_cols)
        query_list.append(low_back(matmul(branch_in, w_query[:, column_range])))
        key_list.append(low_back(matmul(branch_in, w_key[:, column_range])))
        value_list.append(low_back(matmul(branch_in, w_value[:, column_range])))
    q_raw = jnp.concatenate(query_list, axis=-1)
    k_raw = jnp.concatenate(key_list, axis=-1)
    v_raw = jnp.concatenate(value_list, axis=-1)
    head_shape = (SEQ_GRP, LEN, HEADS, HEAD_DIM)
    q_rot = low(rotate((normalize(q_raw) * gain_query).reshape(head_shape), cosine_table, sine_table))
    k_rot = low(rotate((normalize(k_raw) * gain_key).reshape(head_shape), cosine_table, sine_table))
    v_low = low(v_raw).reshape(head_shape)
    score_scale = 1.0 / math.sqrt(HEAD_DIM)
    scores = low_back(jnp.einsum('gqhd,gkhd->ghqk', q_rot, k_rot, precision=HIGH) * score_scale)
    key_valid = jnp.arange(LEN, dtype=jnp.int32)[None, :] < lengths_here[:, None]
    scores = jnp.where(key_valid[:, None, None, :], scores, -1e+30)
    attention_probs = jax.nn.softmax(scores, axis=-1)
    heads_out = jnp.einsum('ghqk,gkhd->gqhd', low(attention_probs), v_low, precision=HIGH)
    heads_out = low(low_back(heads_out.reshape(SEQ_GRP, LEN, QW)))
    attn_total = jnp.zeros((SEQ_GRP, LEN, D), jnp.float32)
    for group_rank in range(N_TENSOR):
        column_range = slice(group_rank * head_cols, (group_rank + 1) * head_cols)
        attn_total = attn_total + low(matmul(heads_out[..., column_range], w_output[column_range, :]))
    middle = (work_x + low_back(attn_total)).reshape(GROUP_TOK, D)
    moe_in = low(normalize(middle) * gain_mlp)
    moe_total = jnp.zeros((GROUP_TOK, D), jnp.float32)
    for group_rank in range(N_TENSOR):
        hidden_range = slice(group_rank * hidden_cols, (group_rank + 1) * hidden_cols)
        branch_in = low_back(moe_in)
        padded_in = jnp.concatenate([branch_in, jnp.zeros((1, D), jnp.float32)], axis=0)
        slot_rows = padded_in[slot_token].reshape(EXPERTS, CAP, D)
        gate_pre = low_back(jnp.einsum('ecd,edf->ecf', slot_rows, w_gate[:, :, hidden_range], precision=HIGH))
        up_pre = low_back(jnp.einsum('ecd,edf->ecf', slot_rows, w_up[:, :, hidden_range], precision=HIGH))
        act_low = low(jax.nn.silu(gate_pre) * up_pre)
        expert_out = low_back(jnp.einsum('ecf,efd->ecd', act_low, w_down[:, hidden_range, :], precision=HIGH))
        padded_out = jnp.concatenate([expert_out.reshape(EXPERTS * CAP, D), jnp.zeros((1, D), jnp.float32)], axis=0)
        picked = padded_out[slot_of]
        moe_total = moe_total + low(lax.optimization_barrier(jnp.sum(picked * gates_here[:, :, None], axis=1)))
    return (middle + moe_total).reshape(SEQ_GRP, LEN, D)

def reference(hidden_in, cotangent, sequence_order, seq_lengths, expert_ids, gate_weights, w_query, w_key, w_value, w_output, gain_attn, gain_query, gain_key, gain_mlp, w_gate, w_up, w_down):
    order = sequence_order.astype(jnp.int32)
    work_x = hidden_in[order].astype(jnp.float32).reshape(N_DP, SEQ_GRP, LEN, D)
    work_cot = cotangent[order].astype(jnp.float32).reshape(N_DP, SEQ_GRP, LEN, D)
    work_len = seq_lengths[order].astype(jnp.int32).reshape(N_DP, SEQ_GRP)
    work_ids = expert_ids[order].astype(jnp.int32).reshape(N_DP, GROUP_TOK, TOP)
    work_gates = gate_weights[order].astype(jnp.float32).reshape(N_DP, GROUP_TOK, TOP)
    slot_of, slot_token = jax.vmap(plan_slots)(work_ids)
    params = (w_query.astype(jnp.float32), w_key.astype(jnp.float32), w_value.astype(jnp.float32), w_output.astype(jnp.float32), gain_attn.astype(jnp.float32), gain_query.astype(jnp.float32), gain_key.astype(jnp.float32), gain_mlp.astype(jnp.float32), w_gate.astype(jnp.float32), w_up.astype(jnp.float32), w_down.astype(jnp.float32))

    def forward(inputs, weights):

        def one_group(packed):
            return group_forward(packed[0], weights, packed[1], packed[2], packed[3], packed[4])
        return lax.map(jax.checkpoint(one_group), (inputs, work_len, slot_of, slot_token, work_gates))
    result, pullback = jax.vjp(forward, work_x, params)
    grad_x, grad_params = pullback(work_cot)
    inverse = jnp.zeros((SEQS,), jnp.int32).at[order].set(jnp.arange(SEQS, dtype=jnp.int32))
    output = result.reshape(SEQS, LEN, D)[inverse].astype(jnp.bfloat16)
    grad_input = grad_x.reshape(SEQS, LEN, D)[inverse].astype(jnp.bfloat16)
    return (output, grad_input, grad_params[0], grad_params[1], grad_params[2], grad_params[3], grad_params[4], grad_params[5], grad_params[6], grad_params[7], grad_params[8], grad_params[9], grad_params[10])
```

```python
import functools
import math

import jax
import jax.numpy as jnp
import numpy as np
from jax import lax
from jax.experimental import pallas as pl
from jax.experimental.pallas import tpu as pltpu
from jax.sharding import Mesh
from jax.sharding import PartitionSpec as P

AXES = ("zl", "y", "c", "zh", "x")
SIZES = (2, 4, 2, 2, 4)
DP = ("zl", "y", "c")
TENSOR = ("zh", "x")
GROUPS = ("zl", "y", "zh")

HEAD_DIM = 128
EPS = 1e-06
BASE = 50000.0
BF = jnp.bfloat16
F32 = jnp.float32
SCALE = 1.0 / math.sqrt(HEAD_DIM)
VMEM = 48 * 1024 * 1024


def rope_tables(length):
    half = HEAD_DIM // 2
    frequency = np.power(
        np.float32(BASE), np.float32(-2.0) * np.arange(half, dtype=np.float32) / HEAD_DIM
    ).astype(np.float32)
    angles = np.arange(length, dtype=np.float32)[:, None] * frequency[None, :]
    cosine = np.cos(angles.astype(np.float64)).astype(np.float32)
    sine = np.sin(angles.astype(np.float64)).astype(np.float32)
    return np.concatenate([cosine, cosine], 1), np.concatenate([-sine, sine], 1)


def along(value, axis, shift):
    size = SIZES[AXES.index(axis)]
    return lax.ppermute(value, axis, [(i, (i + shift) % size) for i in range(size)])


def other_core(value):
    return lax.ppermute(value, "c", [(0, 1), (1, 0)])


def other_half_chip(value):
    return lax.ppermute(value, ("zl", "zh"), [(i, 3 - i) for i in range(4)])


def sum_x(value):
    return value + along(value, "x", 1) + along(value, "x", 2) + along(value, "x", 3)


def gather_x(value):
    return jnp.concatenate(
        [value, along(value, "x", -1), along(value, "x", 2), along(value, "x", 1)], 0
    )


def block(value, x, step):
    rows = value.shape[0] // 4
    return lax.dynamic_slice_in_dim(value, ((x + step) % 4) * rows, rows, 0)


def scatter_sum(pieces):
    mine = pieces[0].astype(F32)
    return (
        mine
        + along(pieces[1], "x", 1).astype(F32)
        + along(pieces[2], "x", 2).astype(F32)
        + along(pieces[3], "x", -1).astype(F32)
    )


def turn(value, start):
    rows = value.shape[0] // 4
    return lax.dynamic_slice_in_dim(
        jnp.concatenate([value, value], 0), start * rows, 4 * rows, 0
    )


def deal_in(value, c, zh):
    half = value.shape[0] // 2
    got = []
    for k in (0, 1):
        pairs = [(a * 2 + b, (b ^ k) * 2 + a) for a in range(2) for b in range(2)]
        part = lax.dynamic_slice_in_dim(value, (zh ^ k) * half, half, 0)
        got.append(lax.ppermute(part, ("c", "zh"), pairs))
    low = jnp.where(c == 0, got[0], got[1])
    high = jnp.where(c == 0, got[1], got[0])
    both = jnp.stack([low, high], 0)
    wide = lax.all_gather(both, "x", axis=2, tiled=True)
    return jnp.concatenate([wide[0], wide[1]], 1)


def deal_out(rows, c, zh, x):
    count, width = rows.shape
    parts = rows.reshape(count, 8, width // 8).transpose(1, 0, 2)
    out = jnp.zeros((8, count, width // 8), rows.dtype)
    for kb in (0, 1):
        for kx in range(4):
            pairs = [
                ((h * 2 + a) * 4 + i, (a * 2 + (h ^ kb)) * 4 + (i + kx) % 4)
                for h in range(2)
                for a in range(2)
                for i in range(4)
            ]
            part = lax.dynamic_index_in_dim(
                parts, (c ^ kb) * 4 + (x + kx) % 4, 0, keepdims=False
            )
            got = lax.ppermute(part, ("c", "zh", "x"), pairs)
            out = lax.dynamic_update_index_in_dim(out, got, (zh ^ kb) * 4 + (x - kx) % 4, 0)
    return out.reshape(8 * count, width // 8)


def other_shard(weight, c):
    half = weight.shape[0] // 2
    mine = other_half_chip(lax.dynamic_slice_in_dim(weight, c * half, half, 0))
    rest = other_core(mine)
    first = c == 0
    return jnp.concatenate([jnp.where(first, mine, rest), jnp.where(first, rest, mine)], 0)


def both_shards(weight, c, same, axis):
    other = other_shard(weight, c)
    return jnp.concatenate(
        [jnp.where(same, weight, other), jnp.where(same, other, weight)], axis
    )


def settle(value, same):
    got = lax.ppermute(value, ("c", "zh"), [(0, 2), (3, 1)])
    return jnp.where(same, value, got)


def prep_kernel(raw, rq, rk, gains, cosine, sine, rot_keep, rot_send, hat_keep, hat_send):
    for part, (rot, hat) in enumerate(((rot_keep, hat_keep), (rot_send, hat_send))):
        base = part * 768
        for i, inv in enumerate((rq, rk)):
            for h in range(2):
                lo = i * 256 + h * 128
                normed = raw[:, base + lo : base + lo + 128] * inv[...]
                hat[:, lo : lo + 128] = normed.astype(BF)
                normed = normed * gains[part * 2 + i : part * 2 + i + 1, h * 128 : h * 128 + 128]
                rot[:, lo : lo + 128] = (
                    normed * cosine[...] + pltpu.roll(normed, 64, 1) * sine[...]
                ).astype(BF)
        rot[:, 512:768] = raw[:, base + 512 : base + 768].astype(BF)


def prep(raw, rq, rk, gains, cosine, sine):
    rows = raw.shape[0]
    step = 128
    row_spec = lambda width: pl.BlockSpec((step, width), lambda i: (i, 0))
    return pl.pallas_call(
        prep_kernel,
        grid=(rows // step,),
        in_specs=[
            row_spec(1536),
            row_spec(1),
            row_spec(1),
            pl.BlockSpec((4, 256), lambda i: (0, 0)),
            row_spec(128),
            row_spec(128),
        ],
        out_specs=[row_spec(768), row_spec(768), row_spec(512), row_spec(512)],
        out_shape=[
            jax.ShapeDtypeStruct((rows, 768), BF),
            jax.ShapeDtypeStruct((rows, 768), BF),
            jax.ShapeDtypeStruct((rows, 512), BF),
            jax.ShapeDtypeStruct((rows, 512), BF),
        ],
        compiler_params=pltpu.CompilerParams(vmem_limit_bytes=VMEM),
        cost_estimate=pl.CostEstimate(
            flops=rows * 1536 * 6, bytes_accessed=rows * 1536 * 8, transcendentals=0
        ),
    )(raw, rq, rk, gains, cosine, sine)


def dot(left, right, dims):
    return lax.dot_general(left, right, (dims, ((), ())), preferred_element_type=F32)


def attend_kernel(qkv, bias, out, lse):
    rows = 256
    for h in range(2):
        keys = qkv[:, 256 + h * 128 : 384 + h * 128]
        values = qkv[:, 512 + h * 128 : 640 + h * 128]
        for i in range(4):
            here = slice(i * rows, (i + 1) * rows)
            scores = dot(qkv[here, h * 128 : h * 128 + 128], keys, ((1,), (1,))) * SCALE
            scores = scores + bias[...]
            top = jnp.max(scores, axis=1, keepdims=True)
            weight = jnp.exp(scores - top)
            total = jnp.sum(weight, axis=1, keepdims=True)
            mixed = dot(weight.astype(BF), values, ((1,), (0,))) / total
            out[here, h * 128 : h * 128 + 128] = mixed.astype(BF)
            lse[here, h : h + 1] = top + jnp.log(total)


def attend(qkv, bias):
    return pl.pallas_call(
        attend_kernel,
        out_shape=[
            jax.ShapeDtypeStruct((1024, 256), BF),
            jax.ShapeDtypeStruct((1024, 2), F32),
        ],
        compiler_params=pltpu.CompilerParams(vmem_limit_bytes=VMEM),
        cost_estimate=pl.CostEstimate(
            flops=2 * 4 * 1024 * 1024 * 128,
            bytes_accessed=3 * 1024 * 1024,
            transcendentals=2 * 1024 * 1024,
        ),
    )(qkv, bias)


def attend_back_kernel(
    qkv, d_out, bias, lse, cosine, sine, d_query, d_key, d_value, sums, key_sum, value_sum
):
    rows = 256

    def unturn(grad, here):
        return grad * cosine[here, :] - pltpu.roll(grad, 64, 1) * sine[here, :]

    for h in range(2):
        cols = slice(h * 128, h * 128 + 128)
        keys = qkv[:, 256 + h * 128 : 384 + h * 128]
        values = qkv[:, 512 + h * 128 : 640 + h * 128]
        for i in range(4):
            here = slice(i * rows, (i + 1) * rows)
            query = qkv[here, cols]
            d_here = d_out[here, cols]
            scores = dot(query, keys, ((1,), (1,))) * SCALE + bias[...]
            probs = jnp.exp(scores - lse[here, h : h + 1])
            d_probs = dot(d_here, values, ((1,), (1,)))
            mean = jnp.sum(d_probs * probs, axis=1, keepdims=True)
            d_scores = (probs * (d_probs - mean)).astype(BF)
            value_part = dot(probs.astype(BF), d_here, ((0,), (0,)))
            key_part = dot(d_scores, query, ((0,), (0,)))
            if i == 0:
                value_sum[...] = value_part
                key_sum[...] = key_part
            else:
                value_sum[...] += value_part
                key_sum[...] += key_part
            d_rot = dot(d_scores, keys, ((1,), (0,))) * SCALE
            inner = jnp.sum(d_rot * query.astype(F32), axis=1, keepdims=True)
            if h == 0:
                sums[here, 0:1] = inner
            else:
                sums[here, 0:1] += inner
            d_query[here, cols] = unturn(d_rot, here)
        d_value[:, cols] = value_sum[...].astype(BF)
        for i in range(4):
            here = slice(i * rows, (i + 1) * rows)
            d_rot = key_sum[here, :] * SCALE
            inner = jnp.sum(
                d_rot * qkv[here, 256 + h * 128 : 384 + h * 128].astype(F32), axis=1, keepdims=True
            )
            if h == 0:
                sums[here, 1:2] = inner
            else:
                sums[here, 1:2] += inner
            d_key[here, cols] = unturn(d_rot, here)


def attend_back(qkv, d_out, bias, lse, cosine, sine):
    return pl.pallas_call(
        attend_back_kernel,
        out_shape=[
            jax.ShapeDtypeStruct((1024, 256), F32),
            jax.ShapeDtypeStruct((1024, 256), F32),
            jax.ShapeDtypeStruct((1024, 256), BF),
            jax.ShapeDtypeStruct((1024, 2), F32),
        ],
        scratch_shapes=[pltpu.VMEM((1024, 128), F32), pltpu.VMEM((1024, 128), F32)],
        compiler_params=pltpu.CompilerParams(vmem_limit_bytes=VMEM),
        cost_estimate=pl.CostEstimate(
            flops=2 * 10 * 1024 * 1024 * 128,
            bytes_accessed=8 * 1024 * 1024,
            transcendentals=2 * 1024 * 1024,
        ),
    )(qkv, d_out, bias, lse, cosine, sine)


def norm_back(grad_normed, normed_hat, inv_root, gain):
    scaled = grad_normed * gain
    return inv_root * (scaled - normed_hat * jnp.mean(scaled * normed_hat, axis=-1, keepdims=True))


def choice_weights(ids, gates, experts, capacity):
    named = ids[:, :, None] == jnp.arange(experts, dtype=jnp.int32)
    count = jnp.sum(named.astype(F32), axis=1)
    tokens = ids.shape[0]
    earlier = (
        jnp.arange(tokens, dtype=jnp.int32)[:, None] > jnp.arange(tokens, dtype=jnp.int32)[None, :]
    ).astype(BF)
    place = jnp.dot(earlier, count.astype(BF), preferred_element_type=F32)
    weight = jnp.sum(jnp.where(named, gates[:, :, None], 0.0), axis=1)
    return jnp.where(place < capacity, weight, 0.0)


def local(
    hidden_in,
    cotangent,
    sequence_order,
    seq_lengths,
    expert_ids,
    gate_weights,
    w_query,
    w_key,
    w_value,
    w_output,
    gain_attn,
    gain_query,
    gain_key,
    gain_mlp,
    w_gate,
    w_up,
    w_down,
):
    zl, y, c, zh, x = (lax.axis_index(a) for a in AXES)
    same = c == zh
    length = hidden_in.shape[1]
    half = length // 2
    quarter = half // 4
    experts = w_gate.shape[0]
    width = w_query.shape[0]
    sequence = (zl * SIZES[1] + y) * 2 + zh
    tokens_here = seq_lengths[sequence]
    ids_here = expert_ids[sequence]
    gates_here = gate_weights[sequence]

    x_low = deal_in(hidden_in[0], c, zh)
    cot_low = deal_in(cotangent[0], c, zh)

    w_qkv = both_shards(jnp.concatenate([w_query, w_key, w_value], 1), c, same, 1)
    w_out = both_shards(w_output, c, same, 0)
    w_gate_up = both_shards(
        jnp.concatenate(
            [
                w_gate.transpose(1, 0, 2).reshape(width, -1),
                w_up.transpose(1, 0, 2).reshape(width, -1),
            ],
            1,
        ),
        c,
        same,
        1,
    )
    w_back = both_shards(w_down.reshape(-1, width), c, same, 0)
    gains_own = jnp.stack([gain_query, gain_key], 0)
    gains_other = other_half_chip(gains_own)
    gains_keep = jnp.where(same, gains_own, gains_other)
    gains_qk = jnp.concatenate([gains_keep, jnp.where(same, gains_other, gains_own)], 0)

    cosine_np, sine_np = rope_tables(length)
    cosine_all, sine_all = jnp.asarray(cosine_np), jnp.asarray(sine_np)
    swap_halves = lambda t: lax.dynamic_slice_in_dim(
        jnp.concatenate([t, t], 0), c * half, length, 0
    )
    cosine_all, sine_all = swap_halves(cosine_all), swap_halves(sine_all)
    positions = (jnp.arange(length, dtype=jnp.int32) + c * half) % length
    bias = jnp.where(positions < tokens_here, 0.0, -1e30).astype(F32)[None, :]

    weight_all = choice_weights(ids_here, gates_here, experts, length * 2 // experts)
    weight_here = turn(lax.dynamic_slice_in_dim(weight_all, c * half, half, 0), x)

    x_rows = x_low.astype(F32)
    inv_one = lax.rsqrt(jnp.mean(x_rows * x_rows, axis=-1, keepdims=True) + EPS)
    attn_in = (x_rows * inv_one * gain_attn).astype(BF)
    attn_in_rest = other_core(attn_in)
    raw = jnp.dot(attn_in, w_qkv, preferred_element_type=F32)
    square = raw * raw
    squares = jnp.stack(
        [
            jnp.sum(square[:, 0:256], axis=1) + jnp.sum(square[:, 768:1024], axis=1),
            jnp.sum(square[:, 256:512], axis=1) + jnp.sum(square[:, 1024:1280], axis=1),
        ],
        0,
    )
    inv_qk = lax.rsqrt(sum_x(squares) / width + EPS)
    inv_qk_rest = other_core(inv_qk)
    rot_keep, rot_send, hat_keep, hat_send = prep(
        raw, inv_qk[0][:, None], inv_qk[1][:, None], gains_qk, cosine_all[:half], sine_all[:half]
    )
    qkv = jnp.concatenate([rot_keep, other_core(rot_send)], 0)
    hat = jnp.concatenate([hat_keep, other_core(hat_send)], 0)
    heads, lse = attend(qkv, bias)
    heads_here = jnp.concatenate([heads[:half], other_core(heads[half:])], 1)
    attn_part = jnp.dot(heads_here, w_out, preferred_element_type=F32).astype(BF)
    attn = scatter_sum([block(attn_part, x, r) for r in range(4)])

    x_mine = lax.dynamic_slice_in_dim(x_low, x * quarter, quarter, 0).astype(F32)
    middle = x_mine + attn
    inv_two = lax.rsqrt(jnp.mean(middle * middle, axis=-1, keepdims=True) + EPS)
    mid_hat = middle * inv_two
    moe_in = gather_x((mid_hat * gain_mlp).astype(BF))
    moe_in_rest = other_core(moe_in)
    cot = turn(cot_low, x)
    cot_rest = other_core(cot)
    cot_back = lax.dot_general(cot, w_back, (((1,), (1,)), ((), ())), preferred_element_type=F32)
    pre = jnp.dot(moe_in, w_gate_up, preferred_element_type=F32)
    hidden = experts * 128
    spread = jnp.repeat(weight_here, 128, axis=1)
    act, d_pre = [], []
    for part in range(2):
        gate_pre = pre[:, part * 2 * hidden : (part * 2 + 1) * hidden]
        up_pre = pre[:, (part * 2 + 1) * hidden : (part * 2 + 2) * hidden]
        sigmoid_gate = jax.nn.sigmoid(gate_pre)
        silu_gate = gate_pre * sigmoid_gate
        act.append((spread * (silu_gate * up_pre)).astype(BF))
        d_act = spread * cot_back[:, part * hidden : (part + 1) * hidden]
        d_pre.append(
            (d_act * up_pre * sigmoid_gate * (1.0 + gate_pre * (1.0 - sigmoid_gate))).astype(BF)
        )
        d_pre.append((d_act * silu_gate).astype(BF))
    d_pre_all = jnp.concatenate(d_pre, 1)
    d_moe_part = lax.dot_general(
        d_pre_all, w_gate_up, (((1,), (1,)), ((), ())), preferred_element_type=F32
    ).astype(BF)
    d_moe = scatter_sum([d_moe_part[r * quarter : (r + 1) * quarter] for r in range(4)])
    moe_part = jnp.dot(jnp.concatenate(act, 1), w_back, preferred_element_type=F32).astype(BF)
    moe = scatter_sum([moe_part[r * quarter : (r + 1) * quarter] for r in range(4)])
    out_rows = (middle + moe).astype(BF)
    output = deal_out(out_rows, c, zh, x)

    d_pre_rest = other_core(d_pre_all[:, 2 * hidden :])
    act_rest = other_core(act[1])
    moe_all = jnp.concatenate([moe_in, moe_in_rest], 0)
    cot_all = jnp.concatenate([cot, cot_rest], 0)
    contract_rows = (((0,), (0,)), ((), ()))
    grad_gate_up = lax.dot_general(
        moe_all,
        jnp.concatenate([d_pre_all[:, : 2 * hidden], d_pre_rest], 0),
        contract_rows,
        preferred_element_type=F32,
    ).astype(BF)
    grad_down = lax.dot_general(
        jnp.concatenate([act[0], act_rest], 0), cot_all, contract_rows, preferred_element_type=F32
    ).astype(BF)
    grad_gate_up, grad_down = lax.psum((grad_gate_up, grad_down), GROUPS)

    gain_mlp_part = jnp.sum(d_moe * mid_hat, axis=0)
    d_middle = cot[:quarter].astype(F32) + norm_back(d_moe, mid_hat, inv_two, gain_mlp)
    d_attn = gather_x(d_middle.astype(BF))
    d_attn_rest = other_core(d_attn)
    d_heads = lax.dot_general(
        d_attn, w_out, (((1,), (1,)), ((), ())), preferred_element_type=F32
    ).astype(BF)
    d_heads = turn(d_heads, (4 - x) % 4)
    d_heads_all = jnp.concatenate([d_heads[:, :256], other_core(d_heads[:, 256:])], 0)
    grad_output = lax.dot_general(
        jnp.concatenate([turn(heads[:half], x), turn(heads[half:], x)], 0),
        jnp.concatenate([d_attn, d_attn_rest], 0),
        contract_rows,
        preferred_element_type=F32,
    ).astype(BF)
    d_query, d_key, d_value, sums = attend_back(qkv, d_heads_all, bias, lse, cosine_all, sine_all)
    sums = sums.T
    sums_rest = other_core(sums)
    sums = sums + jnp.concatenate([sums_rest[:, half:], sums_rest[:, :half]], 1)
    sums = sum_x(sums) / width
    inv_all = jnp.concatenate([inv_qk, inv_qk_rest], 1)
    query_hat, key_hat = hat[:, :256].astype(F32), hat[:, 256:].astype(F32)
    gain_query_part = jnp.sum(d_query * query_hat, axis=0)
    gain_key_part = jnp.sum(d_key * key_hat, axis=0)
    d_q_raw = inv_all[0][:, None] * (d_query * gains_keep[0] - query_hat * sums[0][:, None])
    d_k_raw = inv_all[1][:, None] * (d_key * gains_keep[1] - key_hat * sums[1][:, None])
    d_qkv = jnp.concatenate([d_q_raw.astype(BF), d_k_raw.astype(BF), d_value], 1)
    d_qkv_here = jnp.concatenate([d_qkv[:half], other_core(d_qkv[half:])], 1)
    d_in_part = lax.dot_general(
        d_qkv_here, w_qkv, (((1,), (1,)), ((), ())), preferred_element_type=F32
    )
    gain_attn_part = jnp.sum(d_in_part * (x_rows * inv_one), axis=0)
    d_in_low = d_in_part.astype(BF)
    d_attn_in = scatter_sum([block(d_in_low, x, r) for r in range(4)])
    grad_qkv = lax.dot_general(
        jnp.concatenate([attn_in, attn_in_rest], 0),
        d_qkv,
        contract_rows,
        preferred_element_type=F32,
    ).astype(BF)
    grad_qkv = lax.psum(grad_qkv, GROUPS)

    gains_part = sum_x(jnp.stack([gain_attn_part, gain_mlp_part], 0))
    gains_part = gains_part + other_core(gains_part)
    gains_part = jnp.concatenate(
        [gains_part.reshape(-1), gain_query_part, gain_key_part, jnp.zeros((1536,), F32)]
    ).astype(BF)
    grad_output = lax.psum(
        jnp.concatenate([grad_output, gains_part.reshape(3, width), jnp.zeros((13, width), BF)], 0),
        GROUPS,
    )

    inv_mine = lax.dynamic_slice_in_dim(inv_one, x * quarter, quarter, 0)
    d_input = d_middle + norm_back(d_attn_in, x_mine * inv_mine, inv_mine, gain_attn)
    grad_input = deal_out(d_input.astype(BF), c, zh, x)

    grad_qkv = settle(grad_qkv, same).astype(F32)
    grad_gate_up = settle(grad_gate_up, same).astype(F32)
    grad_down = settle(grad_down, same).astype(F32)
    small = grad_output[256:259].astype(F32).reshape(-1)
    grad_output = settle(grad_output[:256], same).astype(F32)
    gain_qk = settle(small[2 * width : 2 * width + 512], same)
    unfold = lambda t: t.reshape(width, experts, 128).transpose(1, 0, 2)
    return (
        output[None],
        grad_input[None],
        grad_qkv[:, :256],
        grad_qkv[:, 256:512],
        grad_qkv[:, 512:],
        grad_output,
        small[:width],
        gain_qk[:256],
        gain_qk[256:],
        small[width : 2 * width],
        unfold(grad_gate_up[:, :hidden]),
        unfold(grad_gate_up[:, hidden:]),
        grad_down.reshape(experts, 128, width),
    )


def solution(mesh):
    fine = Mesh(mesh.devices.reshape(SIZES), AXES)
    columns = P(None, TENSOR)
    placed = (
        P(DP, None, TENSOR),
        P(DP, None, TENSOR),
        P(),
        P(),
        P(),
        P(),
        columns,
        columns,
        columns,
        P(TENSOR, None),
        P(),
        P(TENSOR),
        P(TENSOR),
        P(),
        P(None, None, TENSOR),
        P(None, None, TENSOR),
        P(None, TENSOR, None),
    )
    return jax.shard_map(
        local,
        mesh=fine,
        in_specs=placed,
        out_specs=placed[:2]
        + (columns, columns, columns, P(TENSOR, None), P(), P(TENSOR), P(TENSOR), P())
        + placed[14:],
        check_vma=False,
    )
```

```python
import math

import jax
import jax.numpy as jnp
import numpy as np
from jax import lax
from jax.experimental import pallas as pl
from jax.experimental.pallas import tpu as pltpu
from jax.sharding import Mesh
from jax.sharding import PartitionSpec as P

AXES = ("zl", "y", "c", "zh", "x")
SIZES = (2, 4, 2, 2, 4)
DP = ("zl", "y", "c")
TENSOR = ("zh", "x")
GROUPS = ("zl", "y", "zh")

HEAD_DIM = 128
EPS = 1e-06
BASE = 50000.0
BF = jnp.bfloat16
F32 = jnp.float32
SCALE = 1.0 / math.sqrt(HEAD_DIM)
VMEM = 32 * 1024 * 1024
BIG = 56 * 1024 * 1024


def rope_tables(length):
    half = HEAD_DIM // 2
    frequency = np.power(
        np.float32(BASE), np.float32(-2.0) * np.arange(half, dtype=np.float32) / HEAD_DIM
    ).astype(np.float32)
    angles = np.arange(length, dtype=np.float32)[:, None] * frequency[None, :]
    cosine = np.cos(angles.astype(np.float64)).astype(np.float32)
    sine = np.sin(angles.astype(np.float64)).astype(np.float32)
    return np.concatenate([cosine, cosine], 1), np.concatenate([-sine, sine], 1)


def along(value, axis, shift):
    size = SIZES[AXES.index(axis)]
    return lax.ppermute(value, axis, [(i, (i + shift) % size) for i in range(size)])


def other_core(value):
    return lax.ppermute(value, "c", [(0, 1), (1, 0)])


def other_half_chip(value):
    return lax.ppermute(value, ("zl", "zh"), [(i, 3 - i) for i in range(4)])


def sum_x(value):
    return value + along(value, "x", 1) + along(value, "x", 2) + along(value, "x", 3)


def gather_x(value, awaited=None):
    half = value.shape[0] // 2
    after, before = along(value, "x", -1), along(value, "x", 1)
    far = [after[:half], before[half:]]
    if awaited is not None:
        far = tie(far, awaited)
    return [value, after, along(far[0], "x", -1), along(far[1], "x", 1), before]


def tie_kernel(*refs):
    del refs


def tie(values, awaited):
    anywhere = pl.BlockSpec(memory_space=pl.ANY)
    count = len(values)
    return pl.pallas_call(
        tie_kernel,
        in_specs=[anywhere] * (count + 1),
        out_specs=[anywhere] * count,
        out_shape=[jax.ShapeDtypeStruct(v.shape, v.dtype) for v in values],
        input_output_aliases={i: i for i in range(count)},
    )(*values, awaited)


def later(start, awaited):
    ends = awaited[(0,) * awaited.ndim].astype(F32) + awaited[(-1,) * awaited.ndim].astype(F32)
    return start + (ends != ends).astype(jnp.int32)


def send_x(pieces):
    return [
        pieces[0],
        along(pieces[1], "x", 1),
        along(pieces[2], "x", 2),
        along(pieces[3], "x", -1),
    ]


def deal_in(value, zh, awaited=None):
    half = value.shape[0] // 2
    got = []
    for k in (0, 1):
        pairs = [(a * 2 + b, (b ^ k) * 2 + a) for a in range(2) for b in range(2)]
        start = (zh ^ k) * half
        if awaited is not None:
            start = later(start, awaited)
        part = lax.dynamic_slice_in_dim(value, start, half, 0)
        got.append(lax.ppermute(part, ("c", "zh"), pairs))
    return jnp.stack(got, 0)


def deal_out(parts, same):
    dealt = lax.all_to_all(parts, ("c", "x"), 0, 0, tiled=True)
    got = dealt.transpose(1, 0, 2, 3).reshape(2, 1024, 256)
    moved = lax.ppermute(got, ("c", "zh"), [(1, 2), (2, 1)])
    got = jnp.where(same, got, moved)
    return got[0], got[1]


def other_half(weights, c, awaited):
    half = weights[0].shape[0] // 2
    start = later(c * half, awaited)
    parts = [lax.dynamic_slice_in_dim(w, start, half, 0) for w in weights]
    return other_half_chip(jnp.concatenate(parts, parts[0].ndim - 1))


def other_rows(out, down, c, awaited):
    start = later(c * 128, awaited)
    low = down.reshape(-1, down.shape[2])
    parts = [
        lax.dynamic_slice_in_dim(out, start, 128, 0),
        lax.dynamic_slice_in_dim(low, start * 2, 256, 0),
    ]
    return jnp.concatenate(parts, 0)


def settle(value):
    return lax.ppermute(value, ("c", "zh"), [(0, 2), (3, 1)])


def dot(left, right, dims):
    return lax.dot_general(left, right, (dims, ((), ())), preferred_element_type=F32)


NT = ((1,), (1,))
NN = ((1,), (0,))
TN = ((0,), (0,))


def call(kernel, grid, in_specs, out_specs, out_shape, scratch=(), flops=1, vmem=VMEM):
    return pl.pallas_call(
        kernel,
        grid_spec=pltpu.PrefetchScalarGridSpec(
            num_scalar_prefetch=1,
            grid=grid,
            in_specs=in_specs,
            out_specs=out_specs,
            scratch_shapes=scratch,
        ),
        out_shape=out_shape,
        compiler_params=pltpu.CompilerParams(vmem_limit_bytes=vmem),
        cost_estimate=pl.CostEstimate(flops=flops, bytes_accessed=1, transcendentals=0),
    )


def shape(*dims, dtype=BF):
    return jax.ShapeDtypeStruct(dims, dtype)


def whole(*dims):
    return pl.BlockSpec(dims, lambda i, p: (0,) * len(dims))


ANYWHERE = pl.BlockSpec(memory_space=pl.ANY)


def line_rows(place, r, rows=128):
    return pl.ds(pl.multiple_of(lax.rem(place[0] + r, 4) * rows, rows), rows)


def pick(flag, yes, no):
    return jnp.where(flag == 1, yes, no)


def pair_of(i, p):
    return jnp.where(i == 0, p[1], jnp.where(i == 1, 1 - p[1], i - 2))


def send_pair(i, p):
    other = jnp.where(i == 0, p[1], 1 - p[1])
    return jnp.where(p[2] == 1, other, jnp.maximum(i - 2, 0))


def keep_pair(i, p):
    other = jnp.where(i == 0, p[1], 1 - p[1])
    return jnp.where(p[2] == 1, jnp.maximum(i - 2, 0), other)


def role(i, p, first):
    return jnp.where(i < first, 1 - p[2], p[2])


def column_blocks(place, pieces):
    own, after, far_low, far_high, before = pieces
    for r, (first, second) in enumerate(
        ((own, own), (after, after), (far_low, far_high), (before, before))
    ):
        for k, piece in enumerate((first, second)):
            index = lax.rem(place[1] + k, 2) * 4 + lax.rem(place[0] + r, 4)
            yield pl.multiple_of(index * 256, 256), piece[k if r != 2 else 0]


def norm_kernel(place, own, after, far_low, far_high, before, gain, low, normed, inv):
    squares = jnp.zeros((low.shape[0], 1), F32)
    for column, here in column_blocks(place, (own, after, far_low, far_high, before)):
        low[:, pl.ds(column, 256)] = here
        here = here.astype(F32)
        squares += jnp.sum(here * here, axis=1, keepdims=True)
    root = lax.rsqrt(squares / low.shape[1] + EPS)
    inv[...] = root
    normed[...] = (low[...].astype(F32) * root * gain[...]).astype(BF)


def piece_specs(step, rows_of):
    return [pl.BlockSpec((n, step, 256), rows_of) for n in (2, 2, 1, 1, 2)]


def norm_rows(pieces, place, gain):
    rows, step = pieces[0].shape[1], 128
    full = lambda: pl.BlockSpec((step, 2048), lambda i, p: (i, 0))
    return call(
        norm_kernel,
        (rows // step,),
        piece_specs(step, lambda i, p: (0, i, 0)) + [whole(1, 2048)],
        [full(), full(), pl.BlockSpec((step, 1), lambda i, p: (i, 0))],
        [shape(rows, 2048), shape(rows, 2048), shape(rows, 1, dtype=F32)],
    )(place, *pieces, gain)


def place_kernel(place, own, after, far_low, far_high, before, low):
    for column, here in column_blocks(place, (own, after, far_low, far_high, before)):
        low[:, pl.ds(column, 256)] = here


def place_rows(pieces, place):
    rows = pieces[0].shape[1]
    step = rows // 4
    return call(
        place_kernel,
        (4,),
        piece_specs(step, lambda i, p: (0, lax.rem(i + p[0], 4), 0)),
        pl.BlockSpec((step, 2048), lambda i, p: (i, 0)),
        shape(rows, 2048),
    )(place, *pieces)


def project_kernel(place, rows_in, *refs):
    *own, near, far, send, keep, squares, columns = refs
    i = pl.program_id(0)
    lane = lax.broadcasted_iota(jnp.int32, columns.shape, 1)

    @pl.when(i == 0)
    def _():
        columns[...] = jnp.zeros_like(columns)

    def finish(raw):
        kept = role(i, place, 3)

        @pl.when(kept == 1)
        def _():
            keep[...] = raw

        @pl.when(kept == 0)
        def _():
            send[...] = raw

        total = jnp.sum(raw * raw, axis=1, keepdims=True)
        columns[...] += jnp.where(lane == lax.rem(i, 3), total, 0.0)

    @pl.when(i < 3)
    def _():
        half = near.shape[0]
        here = pl.ds(pl.multiple_of(place[1] * half, half), half)
        there = pl.ds(pl.multiple_of((1 - place[1]) * half, half), half)
        finish(dot(rows_in[:, here], near[...], NN) + dot(rows_in[:, there], far[...], NN))

    for j, weight in enumerate(own):

        @pl.when(i == 3 + j)
        def _(weight=weight):
            finish(dot(rows_in[...], weight[...], NN))

    @pl.when(i == 5)
    def _():
        squares[...] = columns[...].T


def project(rows_in, own, near, far, place):
    rows, width = rows_in.shape
    other = lambda i: jnp.minimum(i, 2)
    mine = lambda i: jnp.maximum(i - 3, 0)
    return call(
        project_kernel,
        (6,),
        [
            whole(rows, width),
            whole(width, 256),
            whole(width, 256),
            whole(width, 256),
            pl.BlockSpec((width // 2, 256), lambda i, p: (0, other(i))),
            pl.BlockSpec((width // 2, 256), lambda i, p: (0, other(i))),
        ],
        [
            pl.BlockSpec((rows, 256), lambda i, p: (0, jnp.where(p[2] == 1, other(i), mine(i)))),
            pl.BlockSpec((rows, 256), lambda i, p: (0, jnp.where(p[2] == 1, mine(i), other(i)))),
            whole(8, rows),
        ],
        [shape(rows, 768, dtype=F32), shape(rows, 768, dtype=F32), shape(8, rows, dtype=F32)],
        scratch=[pltpu.VMEM((rows, 8), F32)],
    )(place, rows_in, *own, near, far)


def columns_of(rows_two):
    rest = jnp.zeros((6, rows_two.shape[1]), F32)
    return jnp.concatenate([rows_two, rest], 0).T


def prep_kernel(place, raw_send, raw_keep, inv_rows, gains, cosine, sine, first, second, out_send, out_keep):
    inv = columns_of(inv_rows[...])
    for part, (raw, out) in enumerate(((raw_keep, out_keep), (raw_send, out_send))):
        for i in range(2):
            for h in range(2):
                lo = i * 256 + h * 128
                normed = raw[:, lo : lo + 128] * inv[:, i : i + 1]
                out[:, 768 + lo : 896 + lo] = normed.astype(BF)
                normed = normed * gains[part * 2 + i : part * 2 + i + 1, h * 128 : h * 128 + 128]
                out[:, lo : lo + 128] = (
                    normed * cosine[...] + pltpu.roll(normed, 64, 1) * sine[...]
                ).astype(BF)
        out[:, 512:768] = raw[:, 512:768].astype(BF)


def prep(raw_send, raw_keep, inv_rows, gains, cosine, sine, awaited, place):
    rows, step = raw_send.shape[0], 128
    spec = lambda width: pl.BlockSpec((step, width), lambda i, p: (i, 0))
    return call(
        prep_kernel,
        (rows // step,),
        [
            spec(768),
            spec(768),
            pl.BlockSpec((2, step), lambda i, p: (0, i)),
            whole(4, 256),
            spec(128),
            spec(128),
            ANYWHERE,
            ANYWHERE,
        ],
        [spec(1280), spec(1280)],
        [shape(rows, 1280), shape(rows, 1280)],
    )(place, raw_send, raw_keep, inv_rows, gains, cosine, sine, *awaited)


def attend_kernel(place, mine, rest, bias, qkv, out_mine, out_rest, lse):
    rows = 256
    qkv[0:512, :] = mine[...]
    qkv[512:1024, :] = rest[...]
    for h in range(2):
        cols = slice(h * 128, h * 128 + 128)
        keys = qkv[:, 256 + h * 128 : 384 + h * 128]
        values = qkv[:, 512 + h * 128 : 640 + h * 128]
        for i in range(4):
            here = slice(i * rows, (i + 1) * rows)
            scores = dot(qkv[here, cols], keys, NT) * SCALE + bias[...]
            top = jnp.max(scores, axis=1, keepdims=True)
            weight = jnp.exp(scores - top)
            total = jnp.sum(weight, axis=1, keepdims=True)
            out = out_mine if i < 2 else out_rest
            out[i % 2 * rows : i % 2 * rows + rows, cols] = (
                dot(weight.astype(BF), values, NN) / total
            ).astype(BF)
            wide = jnp.broadcast_to(top + jnp.log(total), (rows, 8))
            lse[h : h + 1, here] = wide.T[0:1, :]


def attend(mine, rest, bias, place):
    return call(
        attend_kernel,
        (1,),
        [whole(512, 1280), whole(512, 1280), whole(1, 1024)],
        [whole(1024, 1280), whole(512, 256), whole(512, 256), whole(2, 1024)],
        [shape(1024, 1280), shape(512, 256), shape(512, 256), shape(2, 1024, dtype=F32)],
    )(place, mine, rest, bias)


def fill_other(place, near, far, other):
    half = near.shape[0]
    other[pl.ds(pl.multiple_of(place[1] * half, half), half), :] = near[...]
    other[pl.ds(pl.multiple_of((1 - place[1]) * half, half), half), :] = far[...]


def heads_to_rows_kernel(place, keep, send, own, near, far, first, second, a, b, c, d, other):
    fill_other(place, near, far, other)
    for r, out in enumerate((a, b, c, d)):
        here = line_rows(place, r)
        left, right = keep[here, :], send[here, :]
        part = dot(pick(place[2], left, right), own[...], NN)
        part += dot(pick(place[2], right, left), other[...], NN)
        out[...] = part.astype(BF)


def heads_to_rows(heads, rest, own, near, far, awaited, place):
    width = own.shape[1]
    step = width // 2
    tile = lambda n: pl.BlockSpec((n, step), lambda i, p: (0, i))
    return call(
        heads_to_rows_kernel,
        (2,),
        [whole(512, 256), whole(512, 256), tile(256), tile(128), tile(128), ANYWHERE, ANYWHERE],
        [tile(128)] * 4,
        [shape(128, width)] * 4,
        scratch=[pltpu.VMEM((256, step), BF)],
    )(place, heads, rest, own, near, far, *awaited)


def fill(rows, pieces):
    start = 0
    for piece in pieces:
        rows[start : start + piece.shape[0], :] = piece[...]
        start += piece.shape[0]


def rows_to_heads_kernel(
    place, own_rows, after, far_low, far_high, before, own, near, far,
    keep, send, rows, other,
):
    fill(rows, (own_rows, after, far_low, far_high, before))
    fill_other(place, near, far, other)
    mine = dot(rows[...], own[...], NT).astype(BF)
    rest = dot(rows[...], other[...], NT).astype(BF)
    for out, part in ((send, pick(place[2], rest, mine)), (keep, pick(place[2], mine, rest))):
        for r in range(4):
            out[line_rows(place, r), :] = part[r * 128 : r * 128 + 128]


def rows_to_heads(pieces, own, near, far, place):
    width = own.shape[1]
    return call(
        rows_to_heads_kernel,
        (1,),
        [whole(n, width) for n in (128, 128, 64, 64, 128, 256, 128, 128)],
        [whole(512, 256), whole(512, 256), whole(512, width)],
        [shape(512, 256), shape(512, 256), shape(512, width)],
        scratch=[pltpu.VMEM((256, width), BF)],
        vmem=BIG,
    )(place, *pieces, own, near, far)


def middle_kernel(place, a, b, c, d, low, gain, middle, normed, inv):
    total = sum((t[...].astype(F32) for t in (b, c, d)), a[...].astype(F32))
    total = low[...].astype(F32) + total
    middle[...] = total
    root = lax.rsqrt(jnp.mean(total * total, axis=1, keepdims=True) + EPS)
    inv[...] = root
    normed[...] = (total * root * gain[...]).astype(BF)


def middle_rows(terms, low, gain, place):
    width = low.shape[1]
    return call(
        middle_kernel,
        (1,),
        [whole(128, width)] * 4
        + [pl.BlockSpec((128, width), lambda i, p: (p[0], 0)), whole(1, width)],
        [whole(128, width), whole(128, width), whole(128, 1)],
        [shape(128, width, dtype=F32), shape(128, width), shape(128, 1, dtype=F32)],
    )(place, *terms, low, gain)


def middle_back_kernel(
    place, a, b, c, d, middle, inv, gain, cot, ready_a, ready_b, ready_c, d_middle, d_low, gain_part
):
    d_in = sum((t[...].astype(F32) for t in (b, c, d)), a[...].astype(F32))
    hat = middle[...] * inv[...]
    gain_part[...] = jnp.sum(d_in * hat, axis=0, keepdims=True)
    scaled = d_in * gain[...]
    mean = jnp.mean(scaled * hat, axis=1, keepdims=True)
    total = cot[...].astype(F32) + inv[...] * (scaled - hat * mean)
    d_middle[...] = total
    d_low[...] = total.astype(BF)


def middle_back(terms, middle, inv, gain, cot, ready, place):
    width = middle.shape[1]
    return call(
        middle_back_kernel,
        (1,),
        [whole(128, width)] * 5
        + [whole(128, 1), whole(1, width), whole(128, width)]
        + [ANYWHERE] * 3,
        [whole(128, width), whole(128, width), whole(1, width)],
        [shape(128, width, dtype=F32), shape(128, width), shape(1, width, dtype=F32)],
        vmem=BIG,
    )(place, *terms, middle, inv, gain, cot, *ready)


def cot_back_kernel(place, cot, own, near, far, out):
    def one(down):
        out[0] = dot(cot[...], down, NT)

    i = pl.program_id(0)
    pl.when(i == 0)(lambda: one(near[128:384, :]))
    pl.when(i == 1)(lambda: one(far[128:384, :]))
    pl.when(i >= 2)(lambda: one(own[...].reshape(256, own.shape[2])))


def own_pair(i, p):
    return (jnp.maximum(i - 2, 0), 0, 0)


def cot_back(cot, own, near, far, place):
    rows, width = cot.shape
    return call(
        cot_back_kernel,
        (4,),
        [
            whole(rows, width),
            pl.BlockSpec((2, 128, width), own_pair),
            whole(384, width),
            whole(384, width),
        ],
        pl.BlockSpec((1, rows, 256), lambda i, p: (i, 0, 0)),
        shape(4, rows, 256, dtype=F32),
        flops=5_000_000_000,
    )(place, cot, own, near, far)


def expert_kernel(
    place, own_rows, after, far_low, far_high, before, back, weights, own_gate, own_up, near, far,
    send, keep, rows, a, b, c, d, total, both_weights,
):
    i = pl.program_id(0)

    @pl.when(i == 0)
    def _():
        fill(rows, (own_rows, after, far_low, far_high, before))

    def two(gate, gate_start, up, up_start):
        for j in range(2):
            both_weights[:, j * 256 : j * 256 + 128] = gate[j, :, gate_start : gate_start + 128]
            both_weights[:, j * 256 + 128 : j * 256 + 256] = up[j, :, up_start : up_start + 128]
        lane = lax.broadcasted_iota(jnp.int32, weights.shape, 1)
        pre = dot(rows[...], both_weights[...], NN)
        grads, acts = [], []
        for j in range(2):
            named = lane == pair_of(i, place) * 2 + j
            weight = jnp.sum(jnp.where(named, weights[...], 0.0), axis=1, keepdims=True)
            gate = pre[:, j * 256 : j * 256 + 128]
            up = pre[:, j * 256 + 128 : j * 256 + 256]
            sig = 1.0 / (1.0 + jnp.exp(-gate))
            silu = gate * sig
            d_act = weight * back[0, :, j * 128 : j * 128 + 128]
            acts.append((weight * (silu * up)).astype(BF))
            grads.append((d_act * up * sig * (1.0 + gate * (1.0 - sig))).astype(BF))
            grads.append((d_act * silu).astype(BF))
        both = jnp.concatenate(grads, 1)
        hidden = jnp.concatenate([both] + acts, 1)
        kept = role(i, place, 2)

        @pl.when(kept == 1)
        def _():
            keep[0] = hidden

        @pl.when(kept == 0)
        def _():
            send[0] = hidden

        part = dot(both, both_weights[...], NT)

        @pl.when(i == 0)
        def _():
            total[...] = part

        @pl.when(i > 0)
        def _():
            total[...] += part

    pl.when(i == 0)(lambda: two(near, 0, near, 128))
    pl.when(i == 1)(lambda: two(far, 0, far, 128))
    pl.when(i >= 2)(lambda: two(own_gate, 0, own_up, 0))

    @pl.when(i == 3)
    def _():
        for r, out in enumerate((a, b, c, d)):
            out[...] = total[r * 128 : r * 128 + 128, :].astype(BF)


def expert_layer(pieces, back, weights, own_gate, own_up, near, far, place):
    rows, width = 512, pieces[0].shape[1]
    return call(
        expert_kernel,
        (4,),
        [whole(n, width) for n in (128, 128, 64, 64, 128)]
        + [
            pl.BlockSpec((1, rows, 256), lambda i, p: (i, 0, 0)),
            whole(rows, 4),
            pl.BlockSpec((2, width, 128), own_pair),
            pl.BlockSpec((2, width, 128), own_pair),
            whole(2, width, 256),
            whole(2, width, 256),
        ],
        [
            pl.BlockSpec((1, rows, 768), lambda i, p: (send_pair(i, p), 0, 0)),
            pl.BlockSpec((1, rows, 768), lambda i, p: (keep_pair(i, p), 0, 0)),
            whole(rows, width),
        ]
        + [whole(128, width)] * 4,
        [shape(2, rows, 768), shape(2, rows, 768), shape(rows, width)] + [shape(128, width)] * 4,
        scratch=[pltpu.VMEM((rows, width), F32), pltpu.VMEM((width, 512), BF)],
        vmem=44 * 1024 * 1024,
    )(place, *pieces, back, weights, own_gate, own_up, near, far)


def expert_out_kernel(place, send, keep, own, near, far, awaited, a, b, c, d, total):
    i = pl.program_id(0)

    def one(down):
        acts = pick(role(i, place, 2), keep[0], send[0])
        part = dot(acts, down, NN)

        @pl.when(i == 0)
        def _():
            total[...] = part

        @pl.when(i > 0)
        def _():
            total[...] += part

    pl.when(i == 0)(lambda: one(near[128:384, :]))
    pl.when(i == 1)(lambda: one(far[128:384, :]))
    pl.when(i >= 2)(lambda: one(own[...].reshape(256, own.shape[2])))

    @pl.when(i == 3)
    def _():
        for r, out in enumerate((a, b, c, d)):
            out[...] = total[r * 128 : r * 128 + 128, :].astype(BF)


def expert_out(send, keep, own, near, far, awaited, place):
    rows, width = 512, own.shape[2]
    return call(
        expert_out_kernel,
        (4,),
        [
            pl.BlockSpec((1, rows, 256), lambda i, p: (send_pair(i, p), 0, 2)),
            pl.BlockSpec((1, rows, 256), lambda i, p: (keep_pair(i, p), 0, 2)),
            pl.BlockSpec((2, 128, width), own_pair),
            whole(384, width),
            whole(384, width),
            ANYWHERE,
        ],
        [whole(128, width)] * 4,
        [shape(128, width)] * 4,
        scratch=[pltpu.VMEM((rows, width), F32)],
        flops=5_000_000_000,
    )(place, send, keep, own, near, far, awaited)


def attend_back_kernel(
    place, qkv, d_mine, d_rest, heads_mine, heads_rest, bias, lse, cosine, sine, d_query, d_key, d_value, sums, key_sum, value_sum
):
    rows = 256

    def unturn(grad, here):
        return grad * cosine[here, :] - pltpu.roll(grad, 64, 1) * sine[here, :]

    masked = jnp.broadcast_to(bias[...], (8, 1024)).T[:, 0:1]
    for h in range(2):
        cols = slice(h * 128, h * 128 + 128)
        keys = qkv[:, 256 + h * 128 : 384 + h * 128]
        keys_turned = keys.T
        values = qkv[:, 512 + h * 128 : 640 + h * 128]
        for i in range(4):
            here = slice(i * rows, (i + 1) * rows)
            query = qkv[here, cols]
            inside = slice(i % 2 * rows, i % 2 * rows + rows)
            d_here = (d_mine if i < 2 else d_rest)[inside, cols]
            heads = (heads_mine if i < 2 else heads_rest)[inside, cols]
            scores = dot(keys, query, NT) * SCALE + masked
            probs = jnp.exp(scores - lse[h : h + 1, here])
            mean = d_here.astype(F32) * heads.astype(F32)
            mean = jnp.sum(mean.T, axis=0, keepdims=True)
            d_scores = (probs * (dot(values, d_here, NT) - mean)).astype(BF)
            value_part = dot(probs.astype(BF), d_here, NN)
            key_part = dot(d_scores, query, NN)
            if i == 0:
                value_sum[...] = value_part
                key_sum[...] = key_part
            else:
                value_sum[...] += value_part
                key_sum[...] += key_part
            d_turned = dot(keys_turned, d_scores, NN) * SCALE
            inner = jnp.sum(d_turned * query.astype(F32).T, axis=0, keepdims=True)
            if h == 0:
                sums[0:1, here] = inner
            else:
                sums[0:1, here] += inner
            d_query[here, cols] = unturn(d_turned.T, here)
        d_value[:, cols] = value_sum[...].astype(BF)
        for i in range(4):
            here = slice(i * rows, (i + 1) * rows)
            d_rot = key_sum[here, :] * SCALE
            inner = d_rot * qkv[here, 256 + h * 128 : 384 + h * 128].astype(F32)
            inner = jnp.sum(inner.T, axis=0, keepdims=True)
            if h == 0:
                sums[1:2, here] = inner
            else:
                sums[1:2, here] += inner
            d_key[here, cols] = unturn(d_rot, here)


def attend_back(qkv, d_mine, d_rest, heads_mine, heads_rest, bias, lse, cosine, sine, place):
    return call(
        attend_back_kernel,
        (1,),
        [whole(1024, 1280)]
        + [whole(512, 256)] * 4
        + [whole(1, 1024), whole(2, 1024), whole(1024, 128), whole(1024, 128)],
        [whole(1024, 256), whole(1024, 256), whole(1024, 256), whole(2, 1024)],
        [
            shape(1024, 256, dtype=F32),
            shape(1024, 256, dtype=F32),
            shape(1024, 256),
            shape(2, 1024, dtype=F32),
        ],
        scratch=[pltpu.VMEM((1024, 128), F32), pltpu.VMEM((1024, 128), F32)],
        vmem=BIG,
    )(place, qkv, d_mine, d_rest, heads_mine, heads_rest, bias, lse, cosine, sine)


def raw_back_kernel(
    place, d_query, d_key, d_value, query_hat, key_hat, sums, inv_rows, gains, mine, rest, gain_parts
):
    step = pl.program_id(0)

    @pl.when(step == 0)
    def _():
        gain_parts[...] = jnp.zeros_like(gain_parts)

    mean, inv = columns_of(sums[...]), columns_of(inv_rows[...])
    parts = []
    for i, (grad, hat) in enumerate(((d_query, query_hat), (d_key, key_hat))):
        normed = hat[...].astype(F32)
        scaled = grad[...] * gains[i : i + 1, :]
        parts.append((inv[:, i : i + 1] * (scaled - normed * mean[:, i : i + 1])).astype(BF))
        gain_parts[i : i + 1, :] += jnp.sum(grad[...] * normed, axis=0, keepdims=True)
    total = jnp.concatenate(parts + [d_value[...]], 1)

    @pl.when(step < 2)
    def _():
        mine[...] = total

    @pl.when(step >= 2)
    def _():
        rest[...] = total


def raw_back(d_query, d_key, d_value, qkv, sums, inv_rows, gains, place):
    step = 256
    spec = lambda width, column=0: pl.BlockSpec((step, width), lambda i, p: (i, column))
    line = lambda: pl.BlockSpec((2, step), lambda i, p: (0, i))
    return call(
        raw_back_kernel,
        (4,),
        [
            spec(256),
            spec(256),
            spec(256),
            spec(256, 3),
            spec(256, 4),
            line(),
            line(),
            whole(2, 256),
        ],
        [
            pl.BlockSpec((step, 768), lambda i, p: (jnp.minimum(i, 1), 0)),
            pl.BlockSpec((step, 768), lambda i, p: (jnp.maximum(i - 2, 0), 0)),
            whole(2, 256),
        ],
        [shape(512, 768), shape(512, 768), shape(2, 256, dtype=F32)],
    )(place, d_query, d_key, d_value, qkv, qkv, sums, inv_rows, gains)


def back_kernel(place, *refs):
    rows_mine, rows_rest, d_mine, d_rest, raw_mine, raw_rest, raw_got = refs[:7]
    heads_mine, heads_rest, own_q, own_k, own_v, near, far, low, inv, gain_mlp = refs[7:17]
    weights, terms = refs[17], refs[18:22]
    mine, rest, total, d_own, d_other = refs[22:]
    i = pl.program_id(0)

    @pl.when(i == 0)
    def _():
        for r in range(4):
            mine[r * 128 : r * 128 + 128, :] = heads_mine[line_rows(place, r), :]
            rest[r * 128 : r * 128 + 128, :] = heads_rest[line_rows(place, r), :]
        d_own[...] = pick(place[2], raw_mine[...], raw_got[...])
        d_other[...] = pick(place[2], raw_got[...], raw_mine[...])

    qkv = dot(rows_mine[...], raw_mine[...], TN) + dot(rows_rest[...], raw_rest[...], TN)
    back = dot(d_mine[...], mine[...], TN) + dot(d_rest[...], rest[...], TN)
    weights[...] = jnp.concatenate([qkv.astype(BF), back.astype(BF)], 1)
    other = jnp.where(i // 4 == place[1], near[...], far[...])
    own = jnp.concatenate([own_q[...], own_k[...], own_v[...]], 1)
    part = dot(d_own[...], own, NT) + dot(d_other[...], other, NT)
    total[...] = part
    gain = jnp.sum(part * (low[...].astype(F32) * inv[...]), axis=0, keepdims=True)
    zeros = jnp.zeros((14, gain.shape[1]), F32)
    gains = jnp.concatenate([gain, gain_mlp[...], zeros], 0).astype(BF)
    for r, out in enumerate(terms):
        out[0:128, :] = total[line_rows(place, r), :].astype(BF)
        out[128:144, :] = gains


def back(
    rows_mine, rows_rest, d_mine, d_rest, raw_mine, raw_rest, raw_got, heads,
    own, near, far, low, inv, gain_mlp, place,
):
    rows, width, step = 512, low.shape[1], 256
    block = lambda: pl.BlockSpec((rows, step), lambda i, p: (0, i))
    half = lambda: pl.BlockSpec((step, 768), lambda i, p: (lax.rem(i, 4), 0))
    tile = lambda: pl.BlockSpec((step, 256), lambda i, p: (i, 0))
    column = lambda n: pl.BlockSpec((n, step), lambda i, p: (0, i))
    return call(
        back_kernel,
        (width // step,),
        [block(), block(), block(), block()]
        + [whole(rows, 768)] * 3
        + [whole(rows, 256)] * 2
        + [tile(), tile(), tile(), half(), half(), column(rows), whole(rows, 1), column(1)],
        [pl.BlockSpec((step, 1024), lambda i, p: (i, 0))] + [column(144)] * 4,
        [shape(width + 16, 1024)] + [shape(144, width)] * 4,
        scratch=[
            pltpu.VMEM((rows, 256), BF),
            pltpu.VMEM((rows, 256), BF),
            pltpu.VMEM((rows, step), F32),
            pltpu.VMEM((rows, 768), BF),
            pltpu.VMEM((rows, 768), BF),
        ],
    )(
        place, rows_mine, rows_rest, d_mine, d_rest, raw_mine, raw_rest, raw_got, *heads,
        *own, near, far, low, inv, gain_mlp,
    )


def last_rows_kernel(place, *refs):
    d_terms, moe_terms = refs[:4], refs[4:8]
    d_middle, middle, low, inv, gain = refs[8:13]
    parts, gains, rows = refs[13:]
    total = sum((t[...].astype(F32) for t in d_terms[1:]), d_terms[0][...].astype(F32))
    gains[...] = total[128:130]
    d_in = total[:128]
    hat = low[...].astype(F32) * inv[...]
    scaled = d_in * gain[...]
    mean = jnp.mean(scaled * hat, axis=1, keepdims=True)
    rows[1] = (d_middle[...] + inv[...] * (scaled - hat * mean)).astype(BF)
    moe = sum((t[...].astype(F32) for t in moe_terms[1:]), moe_terms[0][...].astype(F32))
    rows[0] = (middle[...] + moe).astype(BF)
    for i in range(8):
        parts[i] = rows[:, :, i * 256 : i * 256 + 256]


def last_rows(d_terms, moe_terms, d_middle, middle, low, inv, gain, place):
    width = low.shape[1]
    mine = lambda n: pl.BlockSpec((128, n), lambda i, p: (p[0], 0))
    return call(
        last_rows_kernel,
        (1,),
        [whole(144, width)] * 4
        + [whole(128, width)] * 6
        + [mine(width), mine(1), whole(1, width)],
        [whole(8, 2, 128, 256), whole(2, width)],
        [shape(8, 2, 128, 256), shape(2, width, dtype=F32)],
        scratch=[pltpu.VMEM((2, 128, width), BF)],
        vmem=BIG,
    )(place, *d_terms, *moe_terms, d_middle, middle, low, inv, gain)


def settle_attention_kernel(
    place, mine, got, small_mine, small_rest, awaited, query, key, value, back, small
):
    total = pick(place[2], mine[...], got[...]).astype(F32)
    query[...] = total[:, :256]
    key[...] = total[:, 256:512]
    value[...] = total[:, 512:768]
    back[...] = total[:, 768:].T
    mine, rest = small_mine[...].astype(F32), small_rest[...].astype(F32)
    row = lax.broadcasted_iota(jnp.int32, mine.shape, 0)
    small[...] = jnp.where(row < 4, mine + rest, pick(place[2], mine, rest))


def settle_attention(mine, got, small_rest, awaited, place):
    def rows(flag):
        return pl.BlockSpec((256, 1024), lambda i, p: (jnp.where(p[2] == flag, i, 0), 0))

    tile = lambda: pl.BlockSpec((256, 256), lambda i, p: (i, 0))
    return call(
        settle_attention_kernel,
        (8,),
        [
            rows(1),
            rows(0),
            pl.BlockSpec((16, 1024), lambda i, p: (128, 0)),
            whole(16, 1024),
            ANYWHERE,
        ],
        [tile(), tile(), tile(), pl.BlockSpec((256, 256), lambda i, p: (0, i)), whole(16, 1024)],
        [shape(2048, 256, dtype=F32)] * 3
        + [shape(256, 2048, dtype=F32), shape(16, 1024, dtype=F32)],
    )(place, mine, got, mine, small_rest, awaited)


def settle_experts_kernel(place, gu_mine, gu_got, down_mine, down_got, gate, up, down):
    total = pick(place[2], gu_mine[0], gu_got[0]).astype(F32)
    for j in range(2):
        gate[j] = total[:, j * 256 : j * 256 + 128]
        up[j] = total[:, j * 256 + 128 : j * 256 + 256]
    total = pick(place[2], down_mine[0], down_got[0]).astype(F32)
    down[...] = total.reshape(down.shape)


def settle_experts(gu_mine, gu_got, down_mine, down_got, place):
    def step(i, p, mine):
        return jnp.where(p[2] == mine, i, 0)

    def tall(mine):
        def index(i, p):
            j = step(i, p, mine)
            return (j // 4, lax.rem(j, 4), 0)

        return pl.BlockSpec((1, 512, 512), index)

    def flat(mine):
        def index(i, p):
            j = step(i, p, mine)
            return (j // 4, 0, lax.rem(j, 4))

        return pl.BlockSpec((1, 256, 512), index)

    thin = lambda: pl.BlockSpec((2, 512, 128), lambda i, p: (i // 4, lax.rem(i, 4), 0))
    return call(
        settle_experts_kernel,
        (8,),
        [tall(1), tall(0), flat(1), flat(0)],
        [thin(), thin(), pl.BlockSpec((2, 128, 512), lambda i, p: (i // 4, 0, lax.rem(i, 4)))],
        [shape(4, 2048, 128, dtype=F32)] * 2 + [shape(4, 128, 2048, dtype=F32)],
        flops=20_000_000_000,
    )(place, gu_mine, gu_got, down_mine, down_got)


def choice_weights(ids, gates, experts, capacity):
    named = ids[:, :, None] == jnp.arange(experts, dtype=jnp.int32)
    count = jnp.sum(named.astype(F32), axis=1)
    tokens = ids.shape[0]
    earlier = (
        jnp.arange(tokens, dtype=jnp.int32)[:, None] > jnp.arange(tokens, dtype=jnp.int32)[None, :]
    ).astype(BF)
    place = jnp.dot(earlier, count.astype(BF), preferred_element_type=F32)
    weight = jnp.sum(jnp.where(named, gates[:, :, None], 0.0), axis=1)
    return jnp.where(place < capacity, weight, 0.0)


def local(
    hidden_in,
    cotangent,
    sequence_order,
    seq_lengths,
    expert_ids,
    gate_weights,
    w_query,
    w_key,
    w_value,
    w_output,
    gain_attn,
    gain_query,
    gain_key,
    gain_mlp,
    w_gate,
    w_up,
    w_down,
):
    zl, y, c, zh, x = (lax.axis_index(a) for a in AXES)
    same = c == zh
    length = hidden_in.shape[1]
    half = length // 2
    experts = w_gate.shape[0]
    width = w_query.shape[0]
    place = jnp.stack([x, c, same.astype(jnp.int32), y, zl, zh]).astype(jnp.int32)
    sequence = (zl * SIZES[1] + y) * 2 + zh
    tokens_here = seq_lengths[sequence]
    ids_here = expert_ids[sequence]
    gates_here = gate_weights[sequence]

    x_dealt = deal_in(hidden_in[0], zh)
    qkv_own = [w_query, w_key, w_value]
    qkv_near = other_half(qkv_own, c, x_dealt)
    x_pieces = gather_x(x_dealt)
    cot_dealt = deal_in(cotangent[0], zh, x_pieces[1])
    gains_own = jnp.stack([gain_query, gain_key], 0)
    gains_other = other_half_chip(gains_own)
    gains_keep = jnp.where(same, gains_own, gains_other)
    gains_qk = jnp.concatenate([gains_keep, jnp.where(same, gains_other, gains_own)], 0)

    cosine_np, sine_np = rope_tables(length)
    swap_halves = lambda t: lax.dynamic_slice_in_dim(
        jnp.concatenate([t, t], 0), c * half, length, 0
    )
    cosine_all, sine_all = swap_halves(jnp.asarray(cosine_np)), swap_halves(jnp.asarray(sine_np))
    positions = (jnp.arange(length, dtype=jnp.int32) + c * half) % length
    bias = jnp.where(positions < tokens_here, 0.0, -1e30).astype(F32)
    weight_all = choice_weights(ids_here, gates_here, experts, length * 2 // experts)
    weight_here = lax.dynamic_slice_in_dim(weight_all, c * half, half, 0)
    weight_here = lax.dynamic_slice_in_dim(
        jnp.concatenate([weight_here, weight_here], 0), x * (half // 4), half, 0
    )

    x_low, attn_in, inv_one = norm_rows(x_pieces, place, gain_attn[None, :])
    rows_own = other_rows(w_output, w_down, c, x_pieces[1])
    qkv_near, cot_first, rows_own = tie([qkv_near, cot_dealt, rows_own], attn_in)
    qkv_far = other_core(qkv_near)
    rows_near = other_half_chip(rows_own)
    raw_send, raw_keep, squares = project(attn_in, qkv_own, qkv_near, qkv_far, place)
    inv_qk = lax.rsqrt(sum_x(squares[:2]) / width + EPS)
    (rows_near,) = tie([rows_near], inv_qk)
    gu_near = other_half([w_gate, w_up], c, rows_near)
    cot_pieces = gather_x(cot_first, inv_qk)
    ready_send, ready_keep = prep(
        raw_send,
        raw_keep,
        inv_qk,
        gains_qk,
        cosine_all[:half],
        sine_all[:half],
        (cot_pieces[1], cot_pieces[4]),
        place,
    )
    ready_rest = other_core(ready_send)
    qkv, heads_mine, heads_rest, lse = attend(ready_keep, ready_rest, bias[None, :], place)
    heads_got = other_core(heads_rest)
    rows_near, inv_tied = tie([rows_near, inv_qk], heads_got)
    rows_far = other_core(rows_near)
    inv_qk_rest = other_core(inv_tied)
    cot = place_rows(cot_pieces, place)
    attn_terms = send_x(
        heads_to_rows(heads_mine, heads_got, w_output, rows_near, rows_far, (cot, heads_got), place)
    )
    attn_in, cot = tie([attn_in, cot], heads_got)
    attn_in_rest = other_core(attn_in)
    cot_rest = other_core(cot)
    cot_down = cot_back(cot, w_down, rows_near, rows_far, place)

    middle, moe_own, inv_two = middle_rows(attn_terms, x_low, gain_mlp[None, :], place)
    moe_pieces = gather_x(moe_own)
    (gu_near,) = tie([gu_near], moe_pieces[1])
    gu_far = other_core(gu_near)
    hidden_send, hidden_keep, moe_in, *d_moe_terms = expert_layer(
        moe_pieces, cot_down, weight_here, w_gate, w_up, gu_near, gu_far, place
    )
    d_moe_terms = send_x(d_moe_terms)
    moe_terms = expert_out(
        hidden_send, hidden_keep, w_down, rows_near, rows_far, hidden_keep, place
    )
    hidden_all = jnp.concatenate([hidden_keep, other_core(hidden_send)], 1)
    moe_all = jnp.concatenate([moe_in, other_core(moe_in)], 0)
    cot_all = jnp.concatenate([cot, cot_rest], 0)
    grad_gate_up = jnp.einsum(
        "td,etf->edf", moe_all, hidden_all[:, :, :512], preferred_element_type=F32
    ).astype(BF)
    grad_down = jnp.einsum(
        "etf,td->efd", hidden_all[:, :, 512:], cot_all, preferred_element_type=F32
    ).astype(BF)

    d_middle, d_own, gain_mlp_part = middle_back(
        d_moe_terms,
        middle,
        inv_two,
        gain_mlp[None, :],
        cot,
        (grad_gate_up, grad_down, moe_terms[0]),
        place,
    )
    grad_gate_up, grad_down = lax.psum((grad_gate_up, grad_down), GROUPS)
    d_pieces = gather_x(d_own)
    d_heads_keep, d_heads_send, d_attn = rows_to_heads(
        d_pieces, w_output, rows_near, rows_far, place
    )
    d_heads_rest = other_core(d_heads_send)
    *moe_terms, d_attn = tie(list(moe_terms) + [d_attn], d_heads_rest)
    moe_after, moe_before = along(moe_terms[1], "x", 1), along(moe_terms[3], "x", -1)
    d_attn_rest = other_core(d_attn)
    d_query, d_key, d_value, sums = attend_back(
        qkv,
        d_heads_keep,
        d_heads_rest,
        heads_mine,
        heads_rest,
        bias[None, :],
        lse,
        cosine_all,
        sine_all,
        place,
    )
    (sums,) = tie([sums], moe_after)
    (sums,) = tie([sums], moe_before)
    sums_rest = other_core(sums)
    sums = sums + jnp.concatenate([sums_rest[:, half:], sums_rest[:, :half]], 1)
    sums = sum_x(sums) / width
    raw_mine, raw_rest, gain_qk_parts = raw_back(
        d_query,
        d_key,
        d_value,
        qkv,
        sums,
        jnp.concatenate([inv_qk, inv_qk_rest], 1),
        gains_keep,
        place,
    )
    raw_got = other_core(raw_rest)
    grad_attn, *d_in_terms = back(
        attn_in,
        attn_in_rest,
        d_attn,
        d_attn_rest,
        raw_mine,
        raw_rest,
        raw_got,
        (heads_mine, heads_rest),
        qkv_own,
        qkv_near,
        qkv_far,
        x_low,
        inv_one,
        gain_mlp_part,
        place,
    )
    d_in_terms = send_x(d_in_terms)
    (moe_far,) = tie([moe_terms[2]], grad_attn)
    moe_terms = [moe_terms[0], moe_after, along(moe_far, "x", 2), moe_before]
    dealt, gains = last_rows(
        d_in_terms, moe_terms, d_middle, middle, x_low, inv_one, gain_attn[None, :], place
    )
    output, grad_input = deal_out(dealt, same)
    small = jnp.concatenate([gains.reshape(-1), gain_qk_parts.reshape(-1)])
    small = jnp.concatenate([small, jnp.zeros((11776,), F32)]).reshape(16, 1024).astype(BF)
    grad_attn = lax.dynamic_update_slice(grad_attn, small, (width, 0))
    (grad_attn,) = tie([grad_attn], grad_down)
    (grad_attn,) = tie([grad_attn], grad_gate_up)
    grad_attn = lax.psum(grad_attn, GROUPS)

    grad_gate, grad_up, grad_down = settle_experts(
        grad_gate_up, settle(grad_gate_up), grad_down, settle(grad_down), place
    )
    (grad_attn,) = tie([grad_attn], output)
    (grad_attn,) = tie([grad_attn], grad_down)
    grad_query, grad_key, grad_value, grad_output, small = settle_attention(
        grad_attn, settle(grad_attn), other_core(grad_attn[width:]), grad_down, place
    )
    small = small.reshape(-1)
    return (
        output[None],
        grad_input[None],
        grad_query,
        grad_key,
        grad_value,
        grad_output,
        small[:width],
        small[2 * width : 2 * width + 256],
        small[2 * width + 256 : 2 * width + 512],
        small[width : 2 * width],
        grad_gate,
        grad_up,
        grad_down,
    )


def solution(mesh):
    fine = Mesh(mesh.devices.reshape(SIZES), AXES)
    columns = P(None, TENSOR)
    placed = (
        P(DP, None, TENSOR),
        P(DP, None, TENSOR),
        P(),
        P(),
        P(),
        P(),
        columns,
        columns,
        columns,
        P(TENSOR, None),
        P(),
        P(TENSOR),
        P(TENSOR),
        P(),
        P(None, None, TENSOR),
        P(None, None, TENSOR),
        P(None, TENSOR, None),
    )
    return jax.shard_map(
        local,
        mesh=fine,
        in_specs=placed,
        out_specs=placed[:2]
        + (columns, columns, columns, P(TENSOR, None), P(), P(TENSOR), P(TENSOR), P())
        + placed[14:],
        check_vma=False,
    )
```

```python
import math

import jax
import jax.numpy as jnp
import numpy as np
from jax import lax
from jax.experimental import pallas as pl
from jax.experimental.pallas import tpu as pltpu
from jax.sharding import Mesh
from jax.sharding import PartitionSpec as P

AXES = ("zl", "y", "c", "zh", "x")
SIZES = (2, 4, 2, 2, 4)
DP = ("zl", "y", "c")
TENSOR = ("zh", "x")
GROUPS = ("zl", "y", "zh")

HEAD_DIM = 128
EPS = 1e-06
BASE = 50000.0
BF = jnp.bfloat16
F32 = jnp.float32
SCALE = 1.0 / math.sqrt(HEAD_DIM)
VMEM = 32 * 1024 * 1024
BIG = 56 * 1024 * 1024


def rope_tables(length):
    half = HEAD_DIM // 2
    frequency = np.power(
        np.float32(BASE), np.float32(-2.0) * np.arange(half, dtype=np.float32) / HEAD_DIM
    ).astype(np.float32)
    angles = np.arange(length, dtype=np.float32)[:, None] * frequency[None, :]
    cosine = np.cos(angles.astype(np.float64)).astype(np.float32)
    sine = np.sin(angles.astype(np.float64)).astype(np.float32)
    return np.concatenate([cosine, cosine], 1), np.concatenate([-sine, sine], 1)


def along(value, axis, shift):
    size = SIZES[AXES.index(axis)]
    return lax.ppermute(value, axis, [(i, (i + shift) % size) for i in range(size)])


def other_core(value):
    return lax.ppermute(value, "c", [(0, 1), (1, 0)])


def other_half_chip(value):
    return lax.ppermute(value, ("zl", "zh"), [(i, 3 - i) for i in range(4)])


def sum_x(value):
    return value + along(value, "x", 1) + along(value, "x", 2) + along(value, "x", 3)


def gather_x(value, awaited=None):
    half = value.shape[0] // 2
    after, before = along(value, "x", -1), along(value, "x", 1)
    far = [after[:half], before[half:]]
    if awaited is not None:
        far = tie(far, awaited)
    return [value, after, along(far[0], "x", -1), along(far[1], "x", 1), before]


def tie_kernel(*refs):
    del refs


def tie(values, awaited):
    anywhere = pl.BlockSpec(memory_space=pl.ANY)
    count = len(values)
    return pl.pallas_call(
        tie_kernel,
        in_specs=[anywhere] * (count + 1),
        out_specs=[anywhere] * count,
        out_shape=[jax.ShapeDtypeStruct(v.shape, v.dtype) for v in values],
        input_output_aliases={i: i for i in range(count)},
    )(*values, awaited)


def later(start, awaited):
    ends = awaited[(0,) * awaited.ndim].astype(F32) + awaited[(-1,) * awaited.ndim].astype(F32)
    return start + (ends != ends).astype(jnp.int32)


def send_x(pieces):
    return [
        pieces[0],
        along(pieces[1], "x", 1),
        along(pieces[2], "x", 2),
        along(pieces[3], "x", -1),
    ]


def deal_in(value, zh, awaited=None):
    half = value.shape[0] // 2
    got = []
    for k in (0, 1):
        pairs = [(a * 2 + b, (b ^ k) * 2 + a) for a in range(2) for b in range(2)]
        start = (zh ^ k) * half
        if awaited is not None:
            start = later(start, awaited)
        part = lax.dynamic_slice_in_dim(value, start, half, 0)
        got.append(lax.ppermute(part, ("c", "zh"), pairs))
    return jnp.stack(got, 0)


def deal_out(parts, same):
    dealt = lax.all_to_all(parts, ("c", "x"), 0, 0, tiled=True)
    got = dealt.transpose(1, 0, 2, 3).reshape(2, 1024, 256)
    moved = lax.ppermute(got, ("c", "zh"), [(1, 2), (2, 1)])
    got = jnp.where(same, got, moved)
    return got[0], got[1]


def other_half(weights, c, awaited):
    half = weights[0].shape[0] // 2
    start = later(c * half, awaited)
    parts = [lax.dynamic_slice_in_dim(w, start, half, 0) for w in weights]
    return other_half_chip(jnp.concatenate(parts, parts[0].ndim - 1))


def other_rows(out, down, c, awaited):
    start = later(c * 128, awaited)
    low = down.reshape(-1, down.shape[2])
    parts = [
        lax.dynamic_slice_in_dim(out, start, 128, 0),
        lax.dynamic_slice_in_dim(low, start * 2, 256, 0),
    ]
    return jnp.concatenate(parts, 0)


def settle(value):
    return lax.ppermute(value, ("c", "zh"), [(0, 2), (3, 1)])


def dot(left, right, dims):
    return lax.dot_general(left, right, (dims, ((), ())), preferred_element_type=F32)


NT = ((1,), (1,))
NN = ((1,), (0,))
TN = ((0,), (0,))


def call(kernel, grid, in_specs, out_specs, out_shape, scratch=(), flops=1, vmem=VMEM):
    return pl.pallas_call(
        kernel,
        grid_spec=pltpu.PrefetchScalarGridSpec(
            num_scalar_prefetch=1,
            grid=grid,
            in_specs=in_specs,
            out_specs=out_specs,
            scratch_shapes=scratch,
        ),
        out_shape=out_shape,
        compiler_params=pltpu.CompilerParams(vmem_limit_bytes=vmem),
        cost_estimate=pl.CostEstimate(flops=flops, bytes_accessed=1, transcendentals=0),
    )


def shape(*dims, dtype=BF):
    return jax.ShapeDtypeStruct(dims, dtype)


def whole(*dims):
    return pl.BlockSpec(dims, lambda i, p: (0,) * len(dims))


ANYWHERE = pl.BlockSpec(memory_space=pl.ANY)


def line_rows(place, r, rows=128):
    return pl.ds(pl.multiple_of(lax.rem(place[0] + r, 4) * rows, rows), rows)


def pick(flag, yes, no):
    return jnp.where(flag == 1, yes, no)


def pair_of(i, p):
    return jnp.where(i == 0, p[1], jnp.where(i == 1, 1 - p[1], i - 2))


def send_pair(i, p):
    other = jnp.where(i == 0, p[1], 1 - p[1])
    return jnp.where(p[2] == 1, other, jnp.maximum(i - 2, 0))


def keep_pair(i, p):
    other = jnp.where(i == 0, p[1], 1 - p[1])
    return jnp.where(p[2] == 1, jnp.maximum(i - 2, 0), other)


def role(i, p, first):
    return jnp.where(i < first, 1 - p[2], p[2])


def column_blocks(place, pieces):
    own, after, far_low, far_high, before = pieces
    for r, (first, second) in enumerate(
        ((own, own), (after, after), (far_low, far_high), (before, before))
    ):
        for k, piece in enumerate((first, second)):
            index = lax.rem(place[1] + k, 2) * 4 + lax.rem(place[0] + r, 4)
            yield pl.multiple_of(index * 256, 256), piece[k if r != 2 else 0]


def norm_kernel(place, own, after, far_low, far_high, before, gain, low, normed, inv):
    squares = jnp.zeros((low.shape[0], 1), F32)
    for column, here in column_blocks(place, (own, after, far_low, far_high, before)):
        low[:, pl.ds(column, 256)] = here
        here = here.astype(F32)
        squares += jnp.sum(here * here, axis=1, keepdims=True)
    root = lax.rsqrt(squares / low.shape[1] + EPS)
    inv[...] = root
    normed[...] = (low[...].astype(F32) * root * gain[...]).astype(BF)


def piece_specs(step, rows_of):
    return [pl.BlockSpec((n, step, 256), rows_of) for n in (2, 2, 1, 1, 2)]


def norm_rows(pieces, place, gain):
    rows, step = pieces[0].shape[1], 128
    full = lambda: pl.BlockSpec((step, 2048), lambda i, p: (i, 0))
    return call(
        norm_kernel,
        (rows // step,),
        piece_specs(step, lambda i, p: (0, i, 0)) + [whole(1, 2048)],
        [full(), full(), pl.BlockSpec((step, 1), lambda i, p: (i, 0))],
        [shape(rows, 2048), shape(rows, 2048), shape(rows, 1, dtype=F32)],
    )(place, *pieces, gain)


def place_kernel(place, own, after, far_low, far_high, before, low):
    for column, here in column_blocks(place, (own, after, far_low, far_high, before)):
        low[:, pl.ds(column, 256)] = here


def place_rows(pieces, place):
    rows = pieces[0].shape[1]
    step = rows // 4
    return call(
        place_kernel,
        (4,),
        piece_specs(step, lambda i, p: (0, lax.rem(i + p[0], 4), 0)),
        pl.BlockSpec((step, 2048), lambda i, p: (i, 0)),
        shape(rows, 2048),
    )(place, *pieces)


def project_kernel(place, rows_in, *refs):
    *own, near, far, awaited, send, keep, squares, columns = refs
    i = pl.program_id(0)
    lane = lax.broadcasted_iota(jnp.int32, columns.shape, 1)

    @pl.when(i == 0)
    def _():
        columns[...] = jnp.zeros_like(columns)

    def finish(raw):
        kept = role(i, place, 3)

        @pl.when(kept == 1)
        def _():
            keep[...] = raw

        @pl.when(kept == 0)
        def _():
            send[...] = raw

        total = jnp.sum(raw * raw, axis=1, keepdims=True)
        columns[...] += jnp.where(lane == lax.rem(i, 3), total, 0.0)

    @pl.when(i < 3)
    def _():
        half = near.shape[0]
        here = pl.ds(pl.multiple_of(place[1] * half, half), half)
        there = pl.ds(pl.multiple_of((1 - place[1]) * half, half), half)
        finish(dot(rows_in[:, here], near[...], NN) + dot(rows_in[:, there], far[...], NN))

    for j, weight in enumerate(own):

        @pl.when(i == 3 + j)
        def _(weight=weight):
            finish(dot(rows_in[...], weight[...], NN))

    @pl.when(i == 5)
    def _():
        squares[...] = columns[...].T


def project(rows_in, own, near, far, awaited, place):
    rows, width = rows_in.shape
    other = lambda i: jnp.minimum(i, 2)
    mine = lambda i: jnp.maximum(i - 3, 0)
    return call(
        project_kernel,
        (6,),
        [
            whole(rows, width),
            whole(width, 256),
            whole(width, 256),
            whole(width, 256),
            pl.BlockSpec((width // 2, 256), lambda i, p: (0, other(i))),
            pl.BlockSpec((width // 2, 256), lambda i, p: (0, other(i))),
            ANYWHERE,
        ],
        [
            pl.BlockSpec((rows, 256), lambda i, p: (0, jnp.where(p[2] == 1, other(i), mine(i)))),
            pl.BlockSpec((rows, 256), lambda i, p: (0, jnp.where(p[2] == 1, mine(i), other(i)))),
            whole(8, rows),
        ],
        [shape(rows, 768, dtype=F32), shape(rows, 768, dtype=F32), shape(8, rows, dtype=F32)],
        scratch=[pltpu.VMEM((rows, 8), F32)],
    )(place, rows_in, *own, near, far, awaited)


def columns_of(rows_two):
    rest = jnp.zeros((6, rows_two.shape[1]), F32)
    return jnp.concatenate([rows_two, rest], 0).T


def prep_kernel(place, raw_send, raw_keep, inv_rows, gains, cosine, sine, first, second, out_send, out_keep):
    inv = columns_of(inv_rows[...])
    for part, (raw, out) in enumerate(((raw_keep, out_keep), (raw_send, out_send))):
        for i in range(2):
            for h in range(2):
                lo = i * 256 + h * 128
                normed = raw[:, lo : lo + 128] * inv[:, i : i + 1]
                out[:, 768 + lo : 896 + lo] = normed.astype(BF)
                normed = normed * gains[part * 2 + i : part * 2 + i + 1, h * 128 : h * 128 + 128]
                out[:, lo : lo + 128] = (
                    normed * cosine[...] + pltpu.roll(normed, 64, 1) * sine[...]
                ).astype(BF)
        out[:, 512:768] = raw[:, 512:768].astype(BF)


def prep(raw_send, raw_keep, inv_rows, gains, cosine, sine, awaited, place):
    rows, step = raw_send.shape[0], 128
    spec = lambda width: pl.BlockSpec((step, width), lambda i, p: (i, 0))
    return call(
        prep_kernel,
        (rows // step,),
        [
            spec(768),
            spec(768),
            pl.BlockSpec((2, step), lambda i, p: (0, i)),
            whole(4, 256),
            spec(128),
            spec(128),
            ANYWHERE,
            ANYWHERE,
        ],
        [spec(1280), spec(1280)],
        [shape(rows, 1280), shape(rows, 1280)],
    )(place, raw_send, raw_keep, inv_rows, gains, cosine, sine, *awaited)


def attend_kernel(place, mine, rest, bias, qkv, out_mine, out_rest, lse):
    rows = 256
    qkv[0:512, :] = mine[...]
    qkv[512:1024, :] = rest[...]
    for h in range(2):
        cols = slice(h * 128, h * 128 + 128)
        keys = qkv[:, 256 + h * 128 : 384 + h * 128]
        values = qkv[:, 512 + h * 128 : 640 + h * 128]
        for i in range(4):
            here = slice(i * rows, (i + 1) * rows)
            scores = dot(qkv[here, cols], keys, NT) * SCALE + bias[...]
            top = jnp.max(scores, axis=1, keepdims=True)
            weight = jnp.exp(scores - top)
            total = jnp.sum(weight, axis=1, keepdims=True)
            out = out_mine if i < 2 else out_rest
            out[i % 2 * rows : i % 2 * rows + rows, cols] = (
                dot(weight.astype(BF), values, NN) / total
            ).astype(BF)
            wide = jnp.broadcast_to(top + jnp.log(total), (rows, 8))
            lse[h : h + 1, here] = wide.T[0:1, :]


def attend(mine, rest, bias, place):
    return call(
        attend_kernel,
        (1,),
        [whole(512, 1280), whole(512, 1280), whole(1, 1024)],
        [whole(1024, 1280), whole(512, 256), whole(512, 256), whole(2, 1024)],
        [shape(1024, 1280), shape(512, 256), shape(512, 256), shape(2, 1024, dtype=F32)],
    )(place, mine, rest, bias)


def fill_other(place, near, far, other):
    half = near.shape[0]
    other[pl.ds(pl.multiple_of(place[1] * half, half), half), :] = near[...]
    other[pl.ds(pl.multiple_of((1 - place[1]) * half, half), half), :] = far[...]


def heads_to_rows_kernel(place, keep, send, own, near, far, first, second, a, b, c, d, other):
    fill_other(place, near, far, other)
    for r, out in enumerate((a, b, c, d)):
        here = line_rows(place, r)
        left, right = keep[here, :], send[here, :]
        part = dot(pick(place[2], left, right), own[...], NN)
        part += dot(pick(place[2], right, left), other[...], NN)
        out[...] = part.astype(BF)


def heads_to_rows(heads, rest, own, near, far, awaited, place):
    width = own.shape[1]
    step = width // 2
    tile = lambda n: pl.BlockSpec((n, step), lambda i, p: (0, i))
    return call(
        heads_to_rows_kernel,
        (2,),
        [whole(512, 256), whole(512, 256), tile(256), tile(128), tile(128), ANYWHERE, ANYWHERE],
        [tile(128)] * 4,
        [shape(128, width)] * 4,
        scratch=[pltpu.VMEM((256, step), BF)],
    )(place, heads, rest, own, near, far, *awaited)


def fill(rows, pieces):
    start = 0
    for piece in pieces:
        rows[start : start + piece.shape[0], :] = piece[...]
        start += piece.shape[0]


def rows_to_heads_kernel(
    place, own_rows, after, far_low, far_high, before, own, near, far,
    keep, send, rows, other,
):
    fill(rows, (own_rows, after, far_low, far_high, before))
    fill_other(place, near, far, other)
    mine = dot(rows[...], own[...], NT).astype(BF)
    rest = dot(rows[...], other[...], NT).astype(BF)
    for out, part in ((send, pick(place[2], rest, mine)), (keep, pick(place[2], mine, rest))):
        for r in range(4):
            out[line_rows(place, r), :] = part[r * 128 : r * 128 + 128]


def rows_to_heads(pieces, own, near, far, place):
    width = own.shape[1]
    return call(
        rows_to_heads_kernel,
        (1,),
        [whole(n, width) for n in (128, 128, 64, 64, 128, 256, 128, 128)],
        [whole(512, 256), whole(512, 256), whole(512, width)],
        [shape(512, 256), shape(512, 256), shape(512, width)],
        scratch=[pltpu.VMEM((256, width), BF)],
        vmem=BIG,
    )(place, *pieces, own, near, far)


def middle_kernel(place, a, b, c, d, low, gain, middle, normed, inv):
    total = sum((t[...].astype(F32) for t in (b, c, d)), a[...].astype(F32))
    total = low[...].astype(F32) + total
    middle[...] = total
    root = lax.rsqrt(jnp.mean(total * total, axis=1, keepdims=True) + EPS)
    inv[...] = root
    normed[...] = (total * root * gain[...]).astype(BF)


def middle_rows(terms, low, gain, place):
    width = low.shape[1]
    return call(
        middle_kernel,
        (1,),
        [whole(128, width)] * 4
        + [pl.BlockSpec((128, width), lambda i, p: (p[0], 0)), whole(1, width)],
        [whole(128, width), whole(128, width), whole(128, 1)],
        [shape(128, width, dtype=F32), shape(128, width), shape(128, 1, dtype=F32)],
    )(place, *terms, low, gain)


def middle_back_kernel(
    place, a, b, c, d, middle, inv, gain, cot, ready_a, ready_b, ready_c, d_middle, d_low, gain_part
):
    d_in = sum((t[...].astype(F32) for t in (b, c, d)), a[...].astype(F32))
    hat = middle[...] * inv[...]
    gain_part[...] = jnp.sum(d_in * hat, axis=0, keepdims=True)
    scaled = d_in * gain[...]
    mean = jnp.mean(scaled * hat, axis=1, keepdims=True)
    total = cot[...].astype(F32) + inv[...] * (scaled - hat * mean)
    d_middle[...] = total
    d_low[...] = total.astype(BF)


def middle_back(terms, middle, inv, gain, cot, ready, place):
    width = middle.shape[1]
    return call(
        middle_back_kernel,
        (1,),
        [whole(128, width)] * 5
        + [whole(128, 1), whole(1, width), whole(128, width)]
        + [ANYWHERE] * 3,
        [whole(128, width), whole(128, width), whole(1, width)],
        [shape(128, width, dtype=F32), shape(128, width), shape(1, width, dtype=F32)],
        vmem=BIG,
    )(place, *terms, middle, inv, gain, cot, *ready)


def cot_back_kernel(place, cot, own, near, far, out):
    def one(down):
        out[0] = dot(cot[...], down, NT)

    i = pl.program_id(0)
    pl.when(i == 0)(lambda: one(near[128:384, :]))
    pl.when(i == 1)(lambda: one(far[128:384, :]))
    pl.when(i >= 2)(lambda: one(own[...].reshape(256, own.shape[2])))


def own_pair(i, p):
    return (jnp.maximum(i - 2, 0), 0, 0)


def cot_back(cot, own, near, far, place):
    rows, width = cot.shape
    return call(
        cot_back_kernel,
        (4,),
        [
            whole(rows, width),
            pl.BlockSpec((2, 128, width), own_pair),
            whole(384, width),
            whole(384, width),
        ],
        pl.BlockSpec((1, rows, 256), lambda i, p: (i, 0, 0)),
        shape(4, rows, 256, dtype=F32),
        flops=5_000_000_000,
    )(place, cot, own, near, far)


def expert_kernel(
    place, own_rows, after, far_low, far_high, before, back, weights, own_gate, own_up, near, far,
    send, keep, rows, a, b, c, d, total, both_weights,
):
    i = pl.program_id(0)

    @pl.when(i == 0)
    def _():
        fill(rows, (own_rows, after, far_low, far_high, before))

    def two(gate, gate_start, up, up_start):
        for j in range(2):
            both_weights[:, j * 256 : j * 256 + 128] = gate[j, :, gate_start : gate_start + 128]
            both_weights[:, j * 256 + 128 : j * 256 + 256] = up[j, :, up_start : up_start + 128]
        lane = lax.broadcasted_iota(jnp.int32, weights.shape, 1)
        pre = dot(rows[...], both_weights[...], NN)
        grads, acts = [], []
        for j in range(2):
            named = lane == pair_of(i, place) * 2 + j
            weight = jnp.sum(jnp.where(named, weights[...], 0.0), axis=1, keepdims=True)
            gate = pre[:, j * 256 : j * 256 + 128]
            up = pre[:, j * 256 + 128 : j * 256 + 256]
            sig = 1.0 / (1.0 + jnp.exp(-gate))
            silu = gate * sig
            d_act = weight * back[0, :, j * 128 : j * 128 + 128]
            acts.append((weight * (silu * up)).astype(BF))
            grads.append((d_act * up * sig * (1.0 + gate * (1.0 - sig))).astype(BF))
            grads.append((d_act * silu).astype(BF))
        both = jnp.concatenate(grads, 1)
        hidden = jnp.concatenate([both] + acts, 1)
        kept = role(i, place, 2)

        @pl.when(kept == 1)
        def _():
            keep[0] = hidden

        @pl.when(kept == 0)
        def _():
            send[0] = hidden

        part = dot(both, both_weights[...], NT)

        @pl.when(i == 0)
        def _():
            total[...] = part

        @pl.when(i > 0)
        def _():
            total[...] += part

    pl.when(i == 0)(lambda: two(near, 0, near, 128))
    pl.when(i == 1)(lambda: two(far, 0, far, 128))
    pl.when(i >= 2)(lambda: two(own_gate, 0, own_up, 0))

    @pl.when(i == 3)
    def _():
        for r, out in enumerate((a, b, c, d)):
            out[...] = total[r * 128 : r * 128 + 128, :].astype(BF)


def expert_layer(pieces, back, weights, own_gate, own_up, near, far, place):
    rows, width = 512, pieces[0].shape[1]
    return call(
        expert_kernel,
        (4,),
        [whole(n, width) for n in (128, 128, 64, 64, 128)]
        + [
            pl.BlockSpec((1, rows, 256), lambda i, p: (i, 0, 0)),
            whole(rows, 4),
            pl.BlockSpec((2, width, 128), own_pair),
            pl.BlockSpec((2, width, 128), own_pair),
            whole(2, width, 256),
            whole(2, width, 256),
        ],
        [
            pl.BlockSpec((1, rows, 768), lambda i, p: (send_pair(i, p), 0, 0)),
            pl.BlockSpec((1, rows, 768), lambda i, p: (keep_pair(i, p), 0, 0)),
            whole(rows, width),
        ]
        + [whole(128, width)] * 4,
        [shape(2, rows, 768), shape(2, rows, 768), shape(rows, width)] + [shape(128, width)] * 4,
        scratch=[pltpu.VMEM((rows, width), F32), pltpu.VMEM((width, 512), BF)],
        vmem=44 * 1024 * 1024,
    )(place, *pieces, back, weights, own_gate, own_up, near, far)


def expert_out_kernel(place, send, keep, own, near, far, awaited, a, b, c, d, total):
    i = pl.program_id(0)

    def one(down):
        acts = pick(role(i, place, 2), keep[0], send[0])
        part = dot(acts, down, NN)

        @pl.when(i == 0)
        def _():
            total[...] = part

        @pl.when(i > 0)
        def _():
            total[...] += part

    pl.when(i == 0)(lambda: one(near[128:384, :]))
    pl.when(i == 1)(lambda: one(far[128:384, :]))
    pl.when(i >= 2)(lambda: one(own[...].reshape(256, own.shape[2])))

    @pl.when(i == 3)
    def _():
        for r, out in enumerate((a, b, c, d)):
            out[...] = total[r * 128 : r * 128 + 128, :].astype(BF)


def expert_out(send, keep, own, near, far, awaited, place):
    rows, width = 512, own.shape[2]
    return call(
        expert_out_kernel,
        (4,),
        [
            pl.BlockSpec((1, rows, 256), lambda i, p: (send_pair(i, p), 0, 2)),
            pl.BlockSpec((1, rows, 256), lambda i, p: (keep_pair(i, p), 0, 2)),
            pl.BlockSpec((2, 128, width), own_pair),
            whole(384, width),
            whole(384, width),
            ANYWHERE,
        ],
        [whole(128, width)] * 4,
        [shape(128, width)] * 4,
        scratch=[pltpu.VMEM((rows, width), F32)],
        flops=5_000_000_000,
    )(place, send, keep, own, near, far, awaited)


def attend_back_kernel(
    place, qkv, d_mine, d_rest, heads_mine, heads_rest, bias, lse, cosine, sine, d_query, d_key, d_value, sums, key_sum, value_sum
):
    rows = 256

    def unturn(grad, here):
        return grad * cosine[here, :] - pltpu.roll(grad, 64, 1) * sine[here, :]

    masked = jnp.broadcast_to(bias[...], (8, 1024)).T[:, 0:1]
    for h in range(2):
        cols = slice(h * 128, h * 128 + 128)
        keys = qkv[:, 256 + h * 128 : 384 + h * 128]
        keys_turned = keys.T
        values = qkv[:, 512 + h * 128 : 640 + h * 128]
        for i in range(4):
            here = slice(i * rows, (i + 1) * rows)
            query = qkv[here, cols]
            inside = slice(i % 2 * rows, i % 2 * rows + rows)
            d_here = (d_mine if i < 2 else d_rest)[inside, cols]
            heads = (heads_mine if i < 2 else heads_rest)[inside, cols]
            scores = dot(keys, query, NT) * SCALE + masked
            probs = jnp.exp(scores - lse[h : h + 1, here])
            mean = d_here.astype(F32) * heads.astype(F32)
            mean = jnp.sum(mean.T, axis=0, keepdims=True)
            d_scores = (probs * (dot(values, d_here, NT) - mean)).astype(BF)
            value_part = dot(probs.astype(BF), d_here, NN)
            key_part = dot(d_scores, query, NN)
            if i == 0:
                value_sum[...] = value_part
                key_sum[...] = key_part
            else:
                value_sum[...] += value_part
                key_sum[...] += key_part
            d_turned = dot(keys_turned, d_scores, NN) * SCALE
            inner = jnp.sum(d_turned * query.astype(F32).T, axis=0, keepdims=True)
            if h == 0:
                sums[0:1, here] = inner
            else:
                sums[0:1, here] += inner
            d_query[here, cols] = unturn(d_turned.T, here)
        d_value[:, cols] = value_sum[...].astype(BF)
        for i in range(4):
            here = slice(i * rows, (i + 1) * rows)
            d_rot = key_sum[here, :] * SCALE
            inner = d_rot * qkv[here, 256 + h * 128 : 384 + h * 128].astype(F32)
            inner = jnp.sum(inner.T, axis=0, keepdims=True)
            if h == 0:
                sums[1:2, here] = inner
            else:
                sums[1:2, here] += inner
            d_key[here, cols] = unturn(d_rot, here)


def attend_back(qkv, d_mine, d_rest, heads_mine, heads_rest, bias, lse, cosine, sine, place):
    return call(
        attend_back_kernel,
        (1,),
        [whole(1024, 1280)]
        + [whole(512, 256)] * 4
        + [whole(1, 1024), whole(2, 1024), whole(1024, 128), whole(1024, 128)],
        [whole(1024, 256), whole(1024, 256), whole(1024, 256), whole(2, 1024)],
        [
            shape(1024, 256, dtype=F32),
            shape(1024, 256, dtype=F32),
            shape(1024, 256),
            shape(2, 1024, dtype=F32),
        ],
        scratch=[pltpu.VMEM((1024, 128), F32), pltpu.VMEM((1024, 128), F32)],
        vmem=BIG,
    )(place, qkv, d_mine, d_rest, heads_mine, heads_rest, bias, lse, cosine, sine)


def raw_back_kernel(
    place, d_query, d_key, d_value, query_hat, key_hat, sums, inv_rows, gains, mine, rest, gain_parts
):
    step = pl.program_id(0)

    @pl.when(step == 0)
    def _():
        gain_parts[...] = jnp.zeros_like(gain_parts)

    mean, inv = columns_of(sums[...]), columns_of(inv_rows[...])
    parts = []
    for i, (grad, hat) in enumerate(((d_query, query_hat), (d_key, key_hat))):
        normed = hat[...].astype(F32)
        scaled = grad[...] * gains[i : i + 1, :]
        parts.append((inv[:, i : i + 1] * (scaled - normed * mean[:, i : i + 1])).astype(BF))
        gain_parts[i : i + 1, :] += jnp.sum(grad[...] * normed, axis=0, keepdims=True)
    total = jnp.concatenate(parts + [d_value[...]], 1)

    @pl.when(step < 2)
    def _():
        mine[...] = total

    @pl.when(step >= 2)
    def _():
        rest[...] = total


def raw_back(d_query, d_key, d_value, qkv, sums, inv_rows, gains, place):
    step = 256
    spec = lambda width, column=0: pl.BlockSpec((step, width), lambda i, p: (i, column))
    line = lambda: pl.BlockSpec((2, step), lambda i, p: (0, i))
    return call(
        raw_back_kernel,
        (4,),
        [
            spec(256),
            spec(256),
            spec(256),
            spec(256, 3),
            spec(256, 4),
            line(),
            line(),
            whole(2, 256),
        ],
        [
            pl.BlockSpec((step, 768), lambda i, p: (jnp.minimum(i, 1), 0)),
            pl.BlockSpec((step, 768), lambda i, p: (jnp.maximum(i - 2, 0), 0)),
            whole(2, 256),
        ],
        [shape(512, 768), shape(512, 768), shape(2, 256, dtype=F32)],
    )(place, d_query, d_key, d_value, qkv, qkv, sums, inv_rows, gains)


def back_kernel(place, *refs):
    rows_mine, rows_rest, d_mine, d_rest, raw_mine, raw_rest, raw_got = refs[:7]
    heads_mine, heads_rest, own_q, own_k, own_v, near, far, low, inv, gain_mlp = refs[7:17]
    weights, terms = refs[17], refs[18:22]
    mine, rest, total, d_own, d_other = refs[22:]
    i = pl.program_id(0)

    @pl.when(i == 0)
    def _():
        for r in range(4):
            mine[r * 128 : r * 128 + 128, :] = heads_mine[line_rows(place, r), :]
            rest[r * 128 : r * 128 + 128, :] = heads_rest[line_rows(place, r), :]
        d_own[...] = pick(place[2], raw_mine[...], raw_got[...])
        d_other[...] = pick(place[2], raw_got[...], raw_mine[...])

    qkv = dot(rows_mine[...], raw_mine[...], TN) + dot(rows_rest[...], raw_rest[...], TN)
    back = dot(d_mine[...], mine[...], TN) + dot(d_rest[...], rest[...], TN)
    weights[...] = jnp.concatenate([qkv.astype(BF), back.astype(BF)], 1)
    other = jnp.where(i // 4 == place[1], near[...], far[...])
    own = jnp.concatenate([own_q[...], own_k[...], own_v[...]], 1)
    part = dot(d_own[...], own, NT) + dot(d_other[...], other, NT)
    total[...] = part
    gain = jnp.sum(part * (low[...].astype(F32) * inv[...]), axis=0, keepdims=True)
    zeros = jnp.zeros((14, gain.shape[1]), F32)
    gains = jnp.concatenate([gain, gain_mlp[...], zeros], 0).astype(BF)
    for r, out in enumerate(terms):
        out[0:128, :] = total[line_rows(place, r), :].astype(BF)
        out[128:144, :] = gains


def back(
    rows_mine, rows_rest, d_mine, d_rest, raw_mine, raw_rest, raw_got, heads,
    own, near, far, low, inv, gain_mlp, place,
):
    rows, width, step = 512, low.shape[1], 256
    block = lambda: pl.BlockSpec((rows, step), lambda i, p: (0, i))
    half = lambda: pl.BlockSpec((step, 768), lambda i, p: (lax.rem(i, 4), 0))
    tile = lambda: pl.BlockSpec((step, 256), lambda i, p: (i, 0))
    column = lambda n: pl.BlockSpec((n, step), lambda i, p: (0, i))
    return call(
        back_kernel,
        (width // step,),
        [block(), block(), block(), block()]
        + [whole(rows, 768)] * 3
        + [whole(rows, 256)] * 2
        + [tile(), tile(), tile(), half(), half(), column(rows), whole(rows, 1), column(1)],
        [pl.BlockSpec((step, 1024), lambda i, p: (i, 0))] + [column(144)] * 4,
        [shape(width + 16, 1024)] + [shape(144, width)] * 4,
        scratch=[
            pltpu.VMEM((rows, 256), BF),
            pltpu.VMEM((rows, 256), BF),
            pltpu.VMEM((rows, step), F32),
            pltpu.VMEM((rows, 768), BF),
            pltpu.VMEM((rows, 768), BF),
        ],
    )(
        place, rows_mine, rows_rest, d_mine, d_rest, raw_mine, raw_rest, raw_got, *heads,
        *own, near, far, low, inv, gain_mlp,
    )


def last_rows_kernel(place, *refs):
    d_terms, moe_terms = refs[:4], refs[4:8]
    d_middle, middle, low, inv, gain = refs[8:13]
    parts, gains, rows = refs[13:]
    total = sum((t[...].astype(F32) for t in d_terms[1:]), d_terms[0][...].astype(F32))
    gains[...] = total[128:130]
    d_in = total[:128]
    hat = low[...].astype(F32) * inv[...]
    scaled = d_in * gain[...]
    mean = jnp.mean(scaled * hat, axis=1, keepdims=True)
    rows[1] = (d_middle[...] + inv[...] * (scaled - hat * mean)).astype(BF)
    moe = sum((t[...].astype(F32) for t in moe_terms[1:]), moe_terms[0][...].astype(F32))
    rows[0] = (middle[...] + moe).astype(BF)
    for i in range(8):
        parts[i] = rows[:, :, i * 256 : i * 256 + 256]


def last_rows(d_terms, moe_terms, d_middle, middle, low, inv, gain, place):
    width = low.shape[1]
    mine = lambda n: pl.BlockSpec((128, n), lambda i, p: (p[0], 0))
    return call(
        last_rows_kernel,
        (1,),
        [whole(144, width)] * 4
        + [whole(128, width)] * 6
        + [mine(width), mine(1), whole(1, width)],
        [whole(8, 2, 128, 256), whole(2, width)],
        [shape(8, 2, 128, 256), shape(2, width, dtype=F32)],
        scratch=[pltpu.VMEM((2, 128, width), BF)],
        vmem=BIG,
    )(place, *d_terms, *moe_terms, d_middle, middle, low, inv, gain)


def settle_attention_kernel(
    place, mine, got, small_mine, small_rest, awaited, query, key, value, back, small
):
    total = pick(place[2], mine[...], got[...]).astype(F32)
    query[...] = total[:, :256]
    key[...] = total[:, 256:512]
    value[...] = total[:, 512:768]
    back[...] = total[:, 768:].T
    mine, rest = small_mine[...].astype(F32), small_rest[...].astype(F32)
    row = lax.broadcasted_iota(jnp.int32, mine.shape, 0)
    small[...] = jnp.where(row < 4, mine + rest, pick(place[2], mine, rest))


def settle_attention(mine, got, small_rest, awaited, place):
    def rows(flag):
        return pl.BlockSpec((256, 1024), lambda i, p: (jnp.where(p[2] == flag, i, 0), 0))

    tile = lambda: pl.BlockSpec((256, 256), lambda i, p: (i, 0))
    return call(
        settle_attention_kernel,
        (8,),
        [
            rows(1),
            rows(0),
            pl.BlockSpec((16, 1024), lambda i, p: (128, 0)),
            whole(16, 1024),
            ANYWHERE,
        ],
        [tile(), tile(), tile(), pl.BlockSpec((256, 256), lambda i, p: (0, i)), whole(16, 1024)],
        [shape(2048, 256, dtype=F32)] * 3
        + [shape(256, 2048, dtype=F32), shape(16, 1024, dtype=F32)],
    )(place, mine, got, mine, small_rest, awaited)


def settle_experts_kernel(place, gu_mine, gu_got, down_mine, down_got, gate, up, down):
    total = pick(place[2], gu_mine[0], gu_got[0]).astype(F32)
    for j in range(2):
        gate[j] = total[:, j * 256 : j * 256 + 128]
        up[j] = total[:, j * 256 + 128 : j * 256 + 256]
    total = pick(place[2], down_mine[0], down_got[0]).astype(F32)
    down[...] = total.reshape(down.shape)


def settle_experts(gu_mine, gu_got, down_mine, down_got, place):
    def step(i, p, mine):
        return jnp.where(p[2] == mine, i, 0)

    def tall(mine):
        def index(i, p):
            j = step(i, p, mine)
            return (j // 4, lax.rem(j, 4), 0)

        return pl.BlockSpec((1, 512, 512), index)

    def flat(mine):
        def index(i, p):
            j = step(i, p, mine)
            return (j // 4, 0, lax.rem(j, 4))

        return pl.BlockSpec((1, 256, 512), index)

    thin = lambda: pl.BlockSpec((2, 512, 128), lambda i, p: (i // 4, lax.rem(i, 4), 0))
    return call(
        settle_experts_kernel,
        (8,),
        [tall(1), tall(0), flat(1), flat(0)],
        [thin(), thin(), pl.BlockSpec((2, 128, 512), lambda i, p: (i // 4, 0, lax.rem(i, 4)))],
        [shape(4, 2048, 128, dtype=F32)] * 2 + [shape(4, 128, 2048, dtype=F32)],
        flops=20_000_000_000,
    )(place, gu_mine, gu_got, down_mine, down_got)


def choice_weights(ids, gates, experts, capacity):
    named = ids[:, :, None] == jnp.arange(experts, dtype=jnp.int32)
    count = jnp.sum(named.astype(F32), axis=1)
    tokens = ids.shape[0]
    earlier = (
        jnp.arange(tokens, dtype=jnp.int32)[:, None] > jnp.arange(tokens, dtype=jnp.int32)[None, :]
    ).astype(BF)
    place = jnp.dot(earlier, count.astype(BF), preferred_element_type=F32)
    weight = jnp.sum(jnp.where(named, gates[:, :, None], 0.0), axis=1)
    return jnp.where(place < capacity, weight, 0.0)


def local(
    hidden_in,
    cotangent,
    sequence_order,
    seq_lengths,
    expert_ids,
    gate_weights,
    w_query,
    w_key,
    w_value,
    w_output,
    gain_attn,
    gain_query,
    gain_key,
    gain_mlp,
    w_gate,
    w_up,
    w_down,
):
    zl, y, c, zh, x = (lax.axis_index(a) for a in AXES)
    same = c == zh
    length = hidden_in.shape[1]
    half = length // 2
    experts = w_gate.shape[0]
    width = w_query.shape[0]
    place = jnp.stack([x, c, same.astype(jnp.int32), y, zl, zh]).astype(jnp.int32)
    sequence = (zl * SIZES[1] + y) * 2 + zh
    tokens_here = seq_lengths[sequence]
    ids_here = expert_ids[sequence]
    gates_here = gate_weights[sequence]

    x_dealt = deal_in(hidden_in[0], zh)
    qkv_own = [w_query, w_key, w_value]
    qkv_near = other_half(qkv_own, c, x_dealt)
    x_pieces = gather_x(x_dealt)
    rows_near = other_half_chip(other_rows(w_output, w_down, c, x_pieces[1]))
    cot_dealt = deal_in(cotangent[0], zh, x_pieces[1])
    gains_own = jnp.stack([gain_query, gain_key], 0)
    gains_other = other_half_chip(gains_own)
    gains_keep = jnp.where(same, gains_own, gains_other)
    gains_qk = jnp.concatenate([gains_keep, jnp.where(same, gains_other, gains_own)], 0)

    cosine_np, sine_np = rope_tables(length)
    swap_halves = lambda t: lax.dynamic_slice_in_dim(
        jnp.concatenate([t, t], 0), c * half, length, 0
    )
    cosine_all, sine_all = swap_halves(jnp.asarray(cosine_np)), swap_halves(jnp.asarray(sine_np))
    positions = (jnp.arange(length, dtype=jnp.int32) + c * half) % length
    bias = jnp.where(positions < tokens_here, 0.0, -1e30).astype(F32)
    weight_all = choice_weights(ids_here, gates_here, experts, length * 2 // experts)
    weight_here = lax.dynamic_slice_in_dim(weight_all, c * half, half, 0)
    weight_here = lax.dynamic_slice_in_dim(
        jnp.concatenate([weight_here, weight_here], 0), x * (half // 4), half, 0
    )

    x_low, attn_in, inv_one = norm_rows(x_pieces, place, gain_attn[None, :])
    qkv_near, cot_first = tie([qkv_near, cot_dealt], attn_in)
    qkv_far = other_core(qkv_near)
    raw_send, raw_keep, squares = project(attn_in, qkv_own, qkv_near, qkv_far, rows_near, place)
    inv_qk = lax.rsqrt(sum_x(squares[:2]) / width + EPS)
    gu_near = other_half([w_gate, w_up], c, inv_qk)
    cot_pieces = gather_x(cot_first, inv_qk)
    ready_send, ready_keep = prep(
        raw_send,
        raw_keep,
        inv_qk,
        gains_qk,
        cosine_all[:half],
        sine_all[:half],
        (cot_pieces[1], cot_pieces[4]),
        place,
    )
    ready_rest = other_core(ready_send)
    qkv, heads_mine, heads_rest, lse = attend(ready_keep, ready_rest, bias[None, :], place)
    heads_got = other_core(heads_rest)
    rows_near, inv_tied = tie([rows_near, inv_qk], heads_got)
    rows_far = other_core(rows_near)
    inv_qk_rest = other_core(inv_tied)
    cot = place_rows(cot_pieces, place)
    attn_terms = send_x(
        heads_to_rows(heads_mine, heads_got, w_output, rows_near, rows_far, (cot, heads_got), place)
    )
    attn_in, cot = tie([attn_in, cot], heads_got)
    attn_in_rest = other_core(attn_in)
    cot_rest = other_core(cot)
    cot_down = cot_back(cot, w_down, rows_near, rows_far, place)

    middle, moe_own, inv_two = middle_rows(attn_terms, x_low, gain_mlp[None, :], place)
    moe_pieces = gather_x(moe_own)
    (gu_near,) = tie([gu_near], moe_pieces[1])
    gu_far = other_core(gu_near)
    hidden_send, hidden_keep, moe_in, *d_moe_terms = expert_layer(
        moe_pieces, cot_down, weight_here, w_gate, w_up, gu_near, gu_far, place
    )
    d_moe_terms = send_x(d_moe_terms)
    moe_terms = expert_out(
        hidden_send, hidden_keep, w_down, rows_near, rows_far, hidden_keep, place
    )
    hidden_all = jnp.concatenate([hidden_keep, other_core(hidden_send)], 1)
    moe_all = jnp.concatenate([moe_in, other_core(moe_in)], 0)
    cot_all = jnp.concatenate([cot, cot_rest], 0)
    grad_gate_up = jnp.einsum(
        "td,etf->edf", moe_all, hidden_all[:, :, :512], preferred_element_type=F32
    ).astype(BF)
    grad_down = jnp.einsum(
        "etf,td->efd", hidden_all[:, :, 512:], cot_all, preferred_element_type=F32
    ).astype(BF)

    d_middle, d_own, gain_mlp_part = middle_back(
        d_moe_terms,
        middle,
        inv_two,
        gain_mlp[None, :],
        cot,
        (grad_gate_up, grad_down, moe_terms[0]),
        place,
    )
    grad_gate_up, grad_down = lax.psum((grad_gate_up, grad_down), GROUPS)
    d_pieces = gather_x(d_own)
    d_heads_keep, d_heads_send, d_attn = rows_to_heads(
        d_pieces, w_output, rows_near, rows_far, place
    )
    d_heads_rest = other_core(d_heads_send)
    *moe_terms, d_attn = tie(list(moe_terms) + [d_attn], d_heads_rest)
    moe_after, moe_before = along(moe_terms[1], "x", 1), along(moe_terms[3], "x", -1)
    d_attn_rest = other_core(d_attn)
    d_query, d_key, d_value, sums = attend_back(
        qkv,
        d_heads_keep,
        d_heads_rest,
        heads_mine,
        heads_rest,
        bias[None, :],
        lse,
        cosine_all,
        sine_all,
        place,
    )
    (sums,) = tie([sums], moe_after)
    (sums,) = tie([sums], moe_before)
    sums_rest = other_core(sums)
    sums = sums + jnp.concatenate([sums_rest[:, half:], sums_rest[:, :half]], 1)
    sums = sum_x(sums) / width
    raw_mine, raw_rest, gain_qk_parts = raw_back(
        d_query,
        d_key,
        d_value,
        qkv,
        sums,
        jnp.concatenate([inv_qk, inv_qk_rest], 1),
        gains_keep,
        place,
    )
    raw_got = other_core(raw_rest)
    grad_attn, *d_in_terms = back(
        attn_in,
        attn_in_rest,
        d_attn,
        d_attn_rest,
        raw_mine,
        raw_rest,
        raw_got,
        (heads_mine, heads_rest),
        qkv_own,
        qkv_near,
        qkv_far,
        x_low,
        inv_one,
        gain_mlp_part,
        place,
    )
    d_in_terms = send_x(d_in_terms)
    (moe_far,) = tie([moe_terms[2]], grad_attn)
    moe_terms = [moe_terms[0], moe_after, along(moe_far, "x", 2), moe_before]
    dealt, gains = last_rows(
        d_in_terms, moe_terms, d_middle, middle, x_low, inv_one, gain_attn[None, :], place
    )
    output, grad_input = deal_out(dealt, same)
    small = jnp.concatenate([gains.reshape(-1), gain_qk_parts.reshape(-1)])
    small = jnp.concatenate([small, jnp.zeros((11776,), F32)]).reshape(16, 1024).astype(BF)
    grad_gate_up, grad_down = tie([grad_gate_up, grad_down], dealt)
    grad_attn = lax.dynamic_update_slice(grad_attn, small, (width, 0))
    (grad_attn,) = tie([grad_attn], grad_down)
    (grad_attn,) = tie([grad_attn], grad_gate_up)
    grad_attn = lax.psum(grad_attn, GROUPS)

    grad_gate, grad_up, grad_down = settle_experts(
        grad_gate_up, settle(grad_gate_up), grad_down, settle(grad_down), place
    )
    (grad_attn,) = tie([grad_attn], output)
    (grad_attn,) = tie([grad_attn], grad_down)
    grad_query, grad_key, grad_value, grad_output, small = settle_attention(
        grad_attn, settle(grad_attn), other_core(grad_attn[width:]), grad_down, place
    )
    small = small.reshape(-1)
    return (
        output[None],
        grad_input[None],
        grad_query,
        grad_key,
        grad_value,
        grad_output,
        small[:width],
        small[2 * width : 2 * width + 256],
        small[2 * width + 256 : 2 * width + 512],
        small[width : 2 * width],
        grad_gate,
        grad_up,
        grad_down,
    )


def solution(mesh):
    fine = Mesh(mesh.devices.reshape(SIZES), AXES)
    columns = P(None, TENSOR)
    placed = (
        P(DP, None, TENSOR),
        P(DP, None, TENSOR),
        P(),
        P(),
        P(),
        P(),
        columns,
        columns,
        columns,
        P(TENSOR, None),
        P(),
        P(TENSOR),
        P(TENSOR),
        P(),
        P(None, None, TENSOR),
        P(None, None, TENSOR),
        P(None, TENSOR, None),
    )
    return jax.shard_map(
        local,
        mesh=fine,
        in_specs=placed,
        out_specs=placed[:2]
        + (columns, columns, columns, P(TENSOR, None), P(), P(TENSOR), P(TENSOR), P())
        + placed[14:],
        check_vma=False,
    )
```

```python
import math

import jax
import jax.numpy as jnp
import numpy as np
from jax import lax
from jax.experimental import pallas as pl
from jax.experimental.pallas import tpu as pltpu
from jax.sharding import Mesh
from jax.sharding import PartitionSpec as P

AXES = ("zl", "y", "c", "zh", "x")
SIZES = (2, 4, 2, 2, 4)
DP = ("zl", "y", "c")
TENSOR = ("zh", "x")
GROUPS = ("zl", "y", "zh")

HEAD_DIM = 128
EPS = 1e-06
BASE = 50000.0
BF = jnp.bfloat16
F32 = jnp.float32
SCALE = 1.0 / math.sqrt(HEAD_DIM)
VMEM = 32 * 1024 * 1024
BIG = 56 * 1024 * 1024


def rope_tables(length):
    half = HEAD_DIM // 2
    frequency = np.power(
        np.float32(BASE), np.float32(-2.0) * np.arange(half, dtype=np.float32) / HEAD_DIM
    ).astype(np.float32)
    angles = np.arange(length, dtype=np.float32)[:, None] * frequency[None, :]
    cosine = np.cos(angles.astype(np.float64)).astype(np.float32)
    sine = np.sin(angles.astype(np.float64)).astype(np.float32)
    return np.concatenate([cosine, cosine], 1), np.concatenate([-sine, sine], 1)


def along(value, axis, shift):
    size = SIZES[AXES.index(axis)]
    return lax.ppermute(value, axis, [(i, (i + shift) % size) for i in range(size)])


def other_core(value):
    return lax.ppermute(value, "c", [(0, 1), (1, 0)])


def other_half_chip(value):
    return lax.ppermute(value, ("zl", "zh"), [(i, 3 - i) for i in range(4)])


def sum_x(value):
    return value + along(value, "x", 1) + along(value, "x", 2) + along(value, "x", 3)


def gather_x(value, awaited=None):
    half = value.shape[0] // 2
    after, before = along(value, "x", -1), along(value, "x", 1)
    far = [after[:half], before[half:]]
    if awaited is not None:
        far = tie(far, awaited)
    return [value, after, along(far[0], "x", -1), along(far[1], "x", 1), before]


def tie_kernel(*refs):
    del refs


def tie(values, awaited):
    anywhere = pl.BlockSpec(memory_space=pl.ANY)
    count = len(values)
    return pl.pallas_call(
        tie_kernel,
        in_specs=[anywhere] * (count + 1),
        out_specs=[anywhere] * count,
        out_shape=[jax.ShapeDtypeStruct(v.shape, v.dtype) for v in values],
        input_output_aliases={i: i for i in range(count)},
    )(*values, awaited)


def later(start, awaited):
    ends = awaited[(0,) * awaited.ndim].astype(F32) + awaited[(-1,) * awaited.ndim].astype(F32)
    return start + (ends != ends).astype(jnp.int32)


def send_x(pieces):
    return [
        pieces[0],
        along(pieces[1], "x", 1),
        along(pieces[2], "x", 2),
        along(pieces[3], "x", -1),
    ]


def deal_in(value, zh, awaited=None):
    half = value.shape[0] // 2
    got = []
    for k in (0, 1):
        pairs = [(a * 2 + b, (b ^ k) * 2 + a) for a in range(2) for b in range(2)]
        start = (zh ^ k) * half
        if awaited is not None:
            start = later(start, awaited)
        part = lax.dynamic_slice_in_dim(value, start, half, 0)
        got.append(lax.ppermute(part, ("c", "zh"), pairs))
    return jnp.stack(got, 0)


def deal_out(parts, same):
    dealt = lax.all_to_all(parts, ("c", "x"), 0, 0, tiled=True)
    got = dealt.transpose(1, 0, 2, 3).reshape(2, 1024, 256)
    moved = lax.ppermute(got, ("c", "zh"), [(1, 2), (2, 1)])
    got = jnp.where(same, got, moved)
    return got[0], got[1], dealt


def other_half(weights, c, awaited):
    half = weights[0].shape[0] // 2
    start = later(c * half, awaited)
    parts = [lax.dynamic_slice_in_dim(w, start, half, 0) for w in weights]
    return other_half_chip(jnp.concatenate(parts, parts[0].ndim - 1))


def send_y(pieces):
    return [pieces[0]] + [along(pieces[r], "y", r) for r in (1, 2, 3)]


def to_shard(value, zl, same):
    low, high = value[:256], value[256:]
    near = jnp.where(zl == 0, low, high)
    far = jnp.where(zl == 0, high, low)
    order = [(i, k, m) for i in range(2) for k in range(2) for m in range(2)]
    index = lambda i, k, m: (i * 2 + k) * 2 + m
    stay = [(index(i, k, m), index(i, m, k)) for i, k, m in order if k != m]
    flip = [(index(i, k, m), index(1 - i, m, k)) for i, k, m in order]
    axes = ("zl", "c", "zh")
    got = lax.ppermute(near, axes, stay)
    return jnp.where(same, near, got), lax.ppermute(far, axes, flip)


def from_groups(piece):
    pair = jnp.stack([piece, lax.ppermute(piece, "zl", [(0, 1), (1, 0)])], 0)
    return [pair] + [along(pair, "y", -r) for r in (1, 2, 3)]


def settle(value):
    return lax.ppermute(value, ("c", "zh"), [(0, 2), (3, 1)])


def dot(left, right, dims):
    return lax.dot_general(left, right, (dims, ((), ())), preferred_element_type=F32)


NT = ((1,), (1,))
NN = ((1,), (0,))
TN = ((0,), (0,))


def call(kernel, grid, in_specs, out_specs, out_shape, scratch=(), flops=1, vmem=VMEM):
    return pl.pallas_call(
        kernel,
        grid_spec=pltpu.PrefetchScalarGridSpec(
            num_scalar_prefetch=1,
            grid=grid,
            in_specs=in_specs,
            out_specs=out_specs,
            scratch_shapes=scratch,
        ),
        out_shape=out_shape,
        compiler_params=pltpu.CompilerParams(vmem_limit_bytes=vmem),
        cost_estimate=pl.CostEstimate(flops=flops, bytes_accessed=1, transcendentals=0),
    )


def shape(*dims, dtype=BF):
    return jax.ShapeDtypeStruct(dims, dtype)


def whole(*dims):
    return pl.BlockSpec(dims, lambda i, p: (0,) * len(dims))


ANYWHERE = pl.BlockSpec(memory_space=pl.ANY)


def line_rows(place, r, rows=128):
    return pl.ds(pl.multiple_of(lax.rem(place[0] + r, 4) * rows, rows), rows)


def pick(flag, yes, no):
    return jnp.where(flag == 1, yes, no)


def pair_of(i, p):
    return jnp.where(i == 0, p[1], jnp.where(i == 1, 1 - p[1], i - 2))


def send_pair(i, p):
    other = jnp.where(i == 0, p[1], 1 - p[1])
    return jnp.where(p[2] == 1, other, jnp.maximum(i - 2, 0))


def keep_pair(i, p):
    other = jnp.where(i == 0, p[1], 1 - p[1])
    return jnp.where(p[2] == 1, jnp.maximum(i - 2, 0), other)


def role(i, p, first):
    return jnp.where(i < first, 1 - p[2], p[2])


def column_blocks(place, pieces):
    own, after, far_low, far_high, before = pieces
    for r, (first, second) in enumerate(
        ((own, own), (after, after), (far_low, far_high), (before, before))
    ):
        for k, piece in enumerate((first, second)):
            index = lax.rem(place[1] + k, 2) * 4 + lax.rem(place[0] + r, 4)
            yield pl.multiple_of(index * 256, 256), piece[k if r != 2 else 0]


def norm_kernel(place, own, after, far_low, far_high, before, gain, low, normed, inv):
    squares = jnp.zeros((low.shape[0], 1), F32)
    for column, here in column_blocks(place, (own, after, far_low, far_high, before)):
        low[:, pl.ds(column, 256)] = here
        here = here.astype(F32)
        squares += jnp.sum(here * here, axis=1, keepdims=True)
    root = lax.rsqrt(squares / low.shape[1] + EPS)
    inv[...] = root
    normed[...] = (low[...].astype(F32) * root * gain[...]).astype(BF)


def piece_specs(step, rows_of):
    return [pl.BlockSpec((n, step, 256), rows_of) for n in (2, 2, 1, 1, 2)]


def norm_rows(pieces, place, gain):
    rows, step = pieces[0].shape[1], 128
    full = lambda: pl.BlockSpec((step, 2048), lambda i, p: (i, 0))
    return call(
        norm_kernel,
        (rows // step,),
        piece_specs(step, lambda i, p: (0, i, 0)) + [whole(1, 2048)],
        [full(), full(), pl.BlockSpec((step, 1), lambda i, p: (i, 0))],
        [shape(rows, 2048), shape(rows, 2048), shape(rows, 1, dtype=F32)],
    )(place, *pieces, gain)


def place_kernel(place, own, after, far_low, far_high, before, low):
    for column, here in column_blocks(place, (own, after, far_low, far_high, before)):
        low[:, pl.ds(column, 256)] = here


def place_rows(pieces, place):
    rows = pieces[0].shape[1]
    step = rows // 4
    return call(
        place_kernel,
        (4,),
        piece_specs(step, lambda i, p: (0, lax.rem(i + p[0], 4), 0)),
        pl.BlockSpec((step, 2048), lambda i, p: (i, 0)),
        shape(rows, 2048),
    )(place, *pieces)


def project_kernel(place, rows_in, *refs):
    *own, near, far, awaited, send, keep, squares, columns = refs
    i = pl.program_id(0)
    lane = lax.broadcasted_iota(jnp.int32, columns.shape, 1)

    @pl.when(i == 0)
    def _():
        columns[...] = jnp.zeros_like(columns)

    def finish(raw):
        kept = role(i, place, 3)

        @pl.when(kept == 1)
        def _():
            keep[...] = raw

        @pl.when(kept == 0)
        def _():
            send[...] = raw

        total = jnp.sum(raw * raw, axis=1, keepdims=True)
        columns[...] += jnp.where(lane == lax.rem(i, 3), total, 0.0)

    @pl.when(i < 3)
    def _():
        half = near.shape[0]
        here = pl.ds(pl.multiple_of(place[1] * half, half), half)
        there = pl.ds(pl.multiple_of((1 - place[1]) * half, half), half)
        finish(dot(rows_in[:, here], near[...], NN) + dot(rows_in[:, there], far[...], NN))

    for j, weight in enumerate(own):

        @pl.when(i == 3 + j)
        def _(weight=weight):
            finish(dot(rows_in[...], weight[...], NN))

    @pl.when(i == 5)
    def _():
        squares[...] = columns[...].T


def project(rows_in, own, near, far, awaited, place):
    rows, width = rows_in.shape
    other = lambda i: jnp.minimum(i, 2)
    mine = lambda i: jnp.maximum(i - 3, 0)
    return call(
        project_kernel,
        (6,),
        [
            whole(rows, width),
            whole(width, 256),
            whole(width, 256),
            whole(width, 256),
            pl.BlockSpec((width // 2, 256), lambda i, p: (0, other(i))),
            pl.BlockSpec((width // 2, 256), lambda i, p: (0, other(i))),
            ANYWHERE,
        ],
        [
            pl.BlockSpec((rows, 256), lambda i, p: (0, jnp.where(p[2] == 1, other(i), mine(i)))),
            pl.BlockSpec((rows, 256), lambda i, p: (0, jnp.where(p[2] == 1, mine(i), other(i)))),
            whole(8, rows),
        ],
        [shape(rows, 768, dtype=F32), shape(rows, 768, dtype=F32), shape(8, rows, dtype=F32)],
        scratch=[pltpu.VMEM((rows, 8), F32)],
    )(place, rows_in, *own, near, far, awaited)


def columns_of(rows_two):
    rest = jnp.zeros((6, rows_two.shape[1]), F32)
    return jnp.concatenate([rows_two, rest], 0).T


def prep_kernel(place, raw_send, raw_keep, inv_rows, gains, cosine, sine, first, second, out_send, out_keep):
    inv = columns_of(inv_rows[...])
    for part, (raw, out) in enumerate(((raw_keep, out_keep), (raw_send, out_send))):
        for i in range(2):
            for h in range(2):
                lo = i * 256 + h * 128
                normed = raw[:, lo : lo + 128] * inv[:, i : i + 1]
                out[:, 768 + lo : 896 + lo] = normed.astype(BF)
                normed = normed * gains[part * 2 + i : part * 2 + i + 1, h * 128 : h * 128 + 128]
                out[:, lo : lo + 128] = (
                    normed * cosine[...] + pltpu.roll(normed, 64, 1) * sine[...]
                ).astype(BF)
        out[:, 512:768] = raw[:, 512:768].astype(BF)


def prep(raw_send, raw_keep, inv_rows, gains, cosine, sine, awaited, place):
    rows, step = raw_send.shape[0], 128
    spec = lambda width: pl.BlockSpec((step, width), lambda i, p: (i, 0))
    return call(
        prep_kernel,
        (rows // step,),
        [
            spec(768),
            spec(768),
            pl.BlockSpec((2, step), lambda i, p: (0, i)),
            whole(4, 256),
            spec(128),
            spec(128),
            ANYWHERE,
            ANYWHERE,
        ],
        [spec(1280), spec(1280)],
        [shape(rows, 1280), shape(rows, 1280)],
    )(place, raw_send, raw_keep, inv_rows, gains, cosine, sine, *awaited)


def attend_kernel(place, mine, rest, bias, qkv, out_mine, out_rest, lse):
    rows = 256
    qkv[0:512, :] = mine[...]
    qkv[512:1024, :] = rest[...]
    for h in range(2):
        cols = slice(h * 128, h * 128 + 128)
        keys = qkv[:, 256 + h * 128 : 384 + h * 128]
        values = qkv[:, 512 + h * 128 : 640 + h * 128]
        for i in range(4):
            here = slice(i * rows, (i + 1) * rows)
            scores = dot(qkv[here, cols], keys, NT) * SCALE + bias[...]
            top = jnp.max(scores, axis=1, keepdims=True)
            weight = jnp.exp(scores - top)
            total = jnp.sum(weight, axis=1, keepdims=True)
            out = out_mine if i < 2 else out_rest
            out[i % 2 * rows : i % 2 * rows + rows, cols] = (
                dot(weight.astype(BF), values, NN) / total
            ).astype(BF)
            wide = jnp.broadcast_to(top + jnp.log(total), (rows, 8))
            lse[h : h + 1, here] = wide.T[0:1, :]


def attend(mine, rest, bias, place):
    return call(
        attend_kernel,
        (1,),
        [whole(512, 1280), whole(512, 1280), whole(1, 1024)],
        [whole(1024, 1280), whole(512, 256), whole(512, 256), whole(2, 1024)],
        [shape(1024, 1280), shape(512, 256), shape(512, 256), shape(2, 1024, dtype=F32)],
    )(place, mine, rest, bias)


def fill_other(place, near, far, other):
    half = near.shape[0]
    other[pl.ds(pl.multiple_of(place[1] * half, half), half), :] = near[...]
    other[pl.ds(pl.multiple_of((1 - place[1]) * half, half), half), :] = far[...]


def heads_to_rows_kernel(place, keep, send, own, near, far, first, second, a, b, c, d, other):
    fill_other(place, near, far, other)
    for r, out in enumerate((a, b, c, d)):
        here = line_rows(place, r)
        left, right = keep[here, :], send[here, :]
        part = dot(pick(place[2], left, right), own[...], NN)
        part += dot(pick(place[2], right, left), other[...], NN)
        out[...] = part.astype(BF)


def heads_to_rows(heads, rest, own, near, far, awaited, place):
    width = own.shape[1]
    step = width // 2
    tile = lambda n: pl.BlockSpec((n, step), lambda i, p: (0, i))
    return call(
        heads_to_rows_kernel,
        (2,),
        [whole(512, 256), whole(512, 256), tile(256), tile(128), tile(128), ANYWHERE, ANYWHERE],
        [tile(128)] * 4,
        [shape(128, width)] * 4,
        scratch=[pltpu.VMEM((256, step), BF)],
    )(place, heads, rest, own, near, far, *awaited)


def fill(rows, pieces):
    start = 0
    for piece in pieces:
        rows[start : start + piece.shape[0], :] = piece[...]
        start += piece.shape[0]


def rows_to_heads_kernel(
    place, own_rows, after, far_low, far_high, before, own, near, far,
    keep, send, rows, other,
):
    fill(rows, (own_rows, after, far_low, far_high, before))
    fill_other(place, near, far, other)
    mine = dot(rows[...], own[...], NT).astype(BF)
    rest = dot(rows[...], other[...], NT).astype(BF)
    for out, part in ((send, pick(place[2], rest, mine)), (keep, pick(place[2], mine, rest))):
        for r in range(4):
            out[line_rows(place, r), :] = part[r * 128 : r * 128 + 128]


def rows_to_heads(pieces, own, near, far, place):
    width = own.shape[1]
    return call(
        rows_to_heads_kernel,
        (1,),
        [whole(n, width) for n in (128, 128, 64, 64, 128, 256, 128, 128)],
        [whole(512, 256), whole(512, 256), whole(512, width)],
        [shape(512, 256), shape(512, 256), shape(512, width)],
        scratch=[pltpu.VMEM((256, width), BF)],
        vmem=BIG,
    )(place, *pieces, own, near, far)


def middle_kernel(place, a, b, c, d, low, gain, middle, normed, inv):
    total = sum((t[...].astype(F32) for t in (b, c, d)), a[...].astype(F32))
    total = low[...].astype(F32) + total
    middle[...] = total
    root = lax.rsqrt(jnp.mean(total * total, axis=1, keepdims=True) + EPS)
    inv[...] = root
    normed[...] = (total * root * gain[...]).astype(BF)


def middle_rows(terms, low, gain, place):
    width = low.shape[1]
    return call(
        middle_kernel,
        (1,),
        [whole(128, width)] * 4
        + [pl.BlockSpec((128, width), lambda i, p: (p[0], 0)), whole(1, width)],
        [whole(128, width), whole(128, width), whole(128, 1)],
        [shape(128, width, dtype=F32), shape(128, width), shape(128, 1, dtype=F32)],
    )(place, *terms, low, gain)


def middle_back_kernel(
    place, a, b, c, d, middle, inv, gain, cot, ready_a, ready_b, ready_c, d_middle, d_low, gain_part
):
    d_in = sum((t[...].astype(F32) for t in (b, c, d)), a[...].astype(F32))
    hat = middle[...] * inv[...]
    gain_part[...] = jnp.sum(d_in * hat, axis=0, keepdims=True)
    scaled = d_in * gain[...]
    mean = jnp.mean(scaled * hat, axis=1, keepdims=True)
    total = cot[...].astype(F32) + inv[...] * (scaled - hat * mean)
    d_middle[...] = total
    d_low[...] = total.astype(BF)


def middle_back(terms, middle, inv, gain, cot, ready, place):
    width = middle.shape[1]
    return call(
        middle_back_kernel,
        (1,),
        [whole(128, width)] * 5
        + [whole(128, 1), whole(1, width), whole(128, width)]
        + [ANYWHERE] * 3,
        [whole(128, width), whole(128, width), whole(1, width)],
        [shape(128, width, dtype=F32), shape(128, width), shape(1, width, dtype=F32)],
        vmem=BIG,
    )(place, *terms, middle, inv, gain, cot, *ready)


def cot_back_kernel(place, cot, own, near, far, out):
    def one(down):
        out[0] = dot(cot[...], down, NT)

    i = pl.program_id(0)
    pl.when(i == 0)(lambda: one(near[...].reshape(256, near.shape[2])))
    pl.when(i == 1)(lambda: one(far[...].reshape(256, far.shape[2])))
    pl.when(i >= 2)(lambda: one(own[...].reshape(256, own.shape[2])))


def own_pair(i, p):
    return (jnp.maximum(i - 2, 0), 0, 0)


def cot_back(cot, own, near, far, place):
    rows, width = cot.shape
    return call(
        cot_back_kernel,
        (4,),
        [
            whole(rows, width),
            pl.BlockSpec((2, 128, width), own_pair),
            whole(2, 128, width),
            whole(2, 128, width),
        ],
        pl.BlockSpec((1, rows, 256), lambda i, p: (i, 0, 0)),
        shape(4, rows, 256, dtype=F32),
        flops=5_000_000_000,
    )(place, cot, own, near, far)


def expert_kernel(
    place, own_rows, after, far_low, far_high, before, back, weights, own_gate, own_up, near, far,
    send, keep, rows, a, b, c, d, total, both_weights,
):
    i = pl.program_id(0)

    @pl.when(i == 0)
    def _():
        fill(rows, (own_rows, after, far_low, far_high, before))

    def two(gate, gate_start, up, up_start):
        for j in range(2):
            both_weights[:, j * 256 : j * 256 + 128] = gate[j, :, gate_start : gate_start + 128]
            both_weights[:, j * 256 + 128 : j * 256 + 256] = up[j, :, up_start : up_start + 128]
        lane = lax.broadcasted_iota(jnp.int32, weights.shape, 1)
        pre = dot(rows[...], both_weights[...], NN)
        grads, acts = [], []
        for j in range(2):
            named = lane == pair_of(i, place) * 2 + j
            weight = jnp.sum(jnp.where(named, weights[...], 0.0), axis=1, keepdims=True)
            gate = pre[:, j * 256 : j * 256 + 128]
            up = pre[:, j * 256 + 128 : j * 256 + 256]
            sig = 1.0 / (1.0 + jnp.exp(-gate))
            silu = gate * sig
            d_act = weight * back[0, :, j * 128 : j * 128 + 128]
            acts.append((weight * (silu * up)).astype(BF))
            grads.append((d_act * up * sig * (1.0 + gate * (1.0 - sig))).astype(BF))
            grads.append((d_act * silu).astype(BF))
        both = jnp.concatenate(grads, 1)
        hidden = jnp.concatenate([both] + acts, 1)
        kept = role(i, place, 2)

        @pl.when(kept == 1)
        def _():
            keep[0] = hidden

        @pl.when(kept == 0)
        def _():
            send[0] = hidden

        part = dot(both, both_weights[...], NT)

        @pl.when(i == 0)
        def _():
            total[...] = part

        @pl.when(i > 0)
        def _():
            total[...] += part

    pl.when(i == 0)(lambda: two(near, 0, near, 128))
    pl.when(i == 1)(lambda: two(far, 0, far, 128))
    pl.when(i >= 2)(lambda: two(own_gate, 0, own_up, 0))

    @pl.when(i == 3)
    def _():
        for r, out in enumerate((a, b, c, d)):
            out[...] = total[r * 128 : r * 128 + 128, :].astype(BF)


def expert_layer(pieces, back, weights, own_gate, own_up, near, far, place):
    rows, width = 512, pieces[0].shape[1]
    return call(
        expert_kernel,
        (4,),
        [whole(n, width) for n in (128, 128, 64, 64, 128)]
        + [
            pl.BlockSpec((1, rows, 256), lambda i, p: (i, 0, 0)),
            whole(rows, 4),
            pl.BlockSpec((2, width, 128), own_pair),
            pl.BlockSpec((2, width, 128), own_pair),
            whole(2, width, 256),
            whole(2, width, 256),
        ],
        [
            pl.BlockSpec((1, rows, 768), lambda i, p: (send_pair(i, p), 0, 0)),
            pl.BlockSpec((1, rows, 768), lambda i, p: (keep_pair(i, p), 0, 0)),
            whole(rows, width),
        ]
        + [whole(128, width)] * 4,
        [shape(2, rows, 768), shape(2, rows, 768), shape(rows, width)] + [shape(128, width)] * 4,
        scratch=[pltpu.VMEM((rows, width), F32), pltpu.VMEM((width, 512), BF)],
        vmem=44 * 1024 * 1024,
    )(place, *pieces, back, weights, own_gate, own_up, near, far)


def expert_out_kernel(place, send, keep, own, near, far, awaited, a, b, c, d, total):
    i = pl.program_id(0)

    def one(down):
        acts = pick(role(i, place, 2), keep[0], send[0])
        part = dot(acts, down, NN)

        @pl.when(i == 0)
        def _():
            total[...] = part

        @pl.when(i > 0)
        def _():
            total[...] += part

    pl.when(i == 0)(lambda: one(near[...].reshape(256, near.shape[2])))
    pl.when(i == 1)(lambda: one(far[...].reshape(256, far.shape[2])))
    pl.when(i >= 2)(lambda: one(own[...].reshape(256, own.shape[2])))

    @pl.when(i == 3)
    def _():
        for r, out in enumerate((a, b, c, d)):
            out[...] = total[r * 128 : r * 128 + 128, :].astype(BF)


def expert_out(send, keep, own, near, far, awaited, place):
    rows, width = 512, own.shape[2]
    return call(
        expert_out_kernel,
        (4,),
        [
            pl.BlockSpec((1, rows, 256), lambda i, p: (send_pair(i, p), 0, 2)),
            pl.BlockSpec((1, rows, 256), lambda i, p: (keep_pair(i, p), 0, 2)),
            pl.BlockSpec((2, 128, width), own_pair),
            whole(2, 128, width),
            whole(2, 128, width),
            ANYWHERE,
        ],
        [whole(128, width)] * 4,
        [shape(128, width)] * 4,
        scratch=[pltpu.VMEM((rows, width), F32)],
        flops=5_000_000_000,
    )(place, send, keep, own, near, far, awaited)


def attend_back_kernel(
    place, qkv, d_mine, d_rest, heads_mine, heads_rest, bias, lse, cosine, sine, d_query, d_key, d_value, sums, key_sum, value_sum
):
    rows = 256

    def unturn(grad, here):
        return grad * cosine[here, :] - pltpu.roll(grad, 64, 1) * sine[here, :]

    masked = jnp.broadcast_to(bias[...], (8, 1024)).T[:, 0:1]
    for h in range(2):
        cols = slice(h * 128, h * 128 + 128)
        keys = qkv[:, 256 + h * 128 : 384 + h * 128]
        keys_turned = keys.T
        values = qkv[:, 512 + h * 128 : 640 + h * 128]
        for i in range(4):
            here = slice(i * rows, (i + 1) * rows)
            query = qkv[here, cols]
            inside = slice(i % 2 * rows, i % 2 * rows + rows)
            d_here = (d_mine if i < 2 else d_rest)[inside, cols]
            heads = (heads_mine if i < 2 else heads_rest)[inside, cols]
            scores = dot(keys, query, NT) * SCALE + masked
            probs = jnp.exp(scores - lse[h : h + 1, here])
            mean = d_here.astype(F32) * heads.astype(F32)
            mean = jnp.sum(mean.T, axis=0, keepdims=True)
            d_scores = (probs * (dot(values, d_here, NT) - mean)).astype(BF)
            value_part = dot(probs.astype(BF), d_here, NN)
            key_part = dot(d_scores, query, NN)
            if i == 0:
                value_sum[...] = value_part
                key_sum[...] = key_part
            else:
                value_sum[...] += value_part
                key_sum[...] += key_part
            d_turned = dot(keys_turned, d_scores, NN) * SCALE
            inner = jnp.sum(d_turned * query.astype(F32).T, axis=0, keepdims=True)
            if h == 0:
                sums[0:1, here] = inner
            else:
                sums[0:1, here] += inner
            d_query[here, cols] = unturn(d_turned.T, here)
        d_value[:, cols] = value_sum[...].astype(BF)
        for i in range(4):
            here = slice(i * rows, (i + 1) * rows)
            d_rot = key_sum[here, :] * SCALE
            inner = d_rot * qkv[here, 256 + h * 128 : 384 + h * 128].astype(F32)
            inner = jnp.sum(inner.T, axis=0, keepdims=True)
            if h == 0:
                sums[1:2, here] = inner
            else:
                sums[1:2, here] += inner
            d_key[here, cols] = unturn(d_rot, here)


def attend_back(qkv, d_mine, d_rest, heads_mine, heads_rest, bias, lse, cosine, sine, place):
    return call(
        attend_back_kernel,
        (1,),
        [whole(1024, 1280)]
        + [whole(512, 256)] * 4
        + [whole(1, 1024), whole(2, 1024), whole(1024, 128), whole(1024, 128)],
        [whole(1024, 256), whole(1024, 256), whole(1024, 256), whole(2, 1024)],
        [
            shape(1024, 256, dtype=F32),
            shape(1024, 256, dtype=F32),
            shape(1024, 256),
            shape(2, 1024, dtype=F32),
        ],
        scratch=[pltpu.VMEM((1024, 128), F32), pltpu.VMEM((1024, 128), F32)],
        vmem=BIG,
    )(place, qkv, d_mine, d_rest, heads_mine, heads_rest, bias, lse, cosine, sine)


def raw_back_kernel(
    place, d_query, d_key, d_value, query_hat, key_hat, sums, inv_rows, gains, mine, rest, gain_parts
):
    step = pl.program_id(0)

    @pl.when(step == 0)
    def _():
        gain_parts[...] = jnp.zeros_like(gain_parts)

    mean, inv = columns_of(sums[...]), columns_of(inv_rows[...])
    parts = []
    for i, (grad, hat) in enumerate(((d_query, query_hat), (d_key, key_hat))):
        normed = hat[...].astype(F32)
        scaled = grad[...] * gains[i : i + 1, :]
        parts.append((inv[:, i : i + 1] * (scaled - normed * mean[:, i : i + 1])).astype(BF))
        gain_parts[i : i + 1, :] += jnp.sum(grad[...] * normed, axis=0, keepdims=True)
    total = jnp.concatenate(parts + [d_value[...]], 1)

    @pl.when(step < 2)
    def _():
        mine[...] = total

    @pl.when(step >= 2)
    def _():
        rest[...] = total


def raw_back(d_query, d_key, d_value, qkv, sums, inv_rows, gains, place):
    step = 256
    spec = lambda width, column=0: pl.BlockSpec((step, width), lambda i, p: (i, column))
    line = lambda: pl.BlockSpec((2, step), lambda i, p: (0, i))
    return call(
        raw_back_kernel,
        (4,),
        [
            spec(256),
            spec(256),
            spec(256),
            spec(256, 3),
            spec(256, 4),
            line(),
            line(),
            whole(2, 256),
        ],
        [
            pl.BlockSpec((step, 768), lambda i, p: (jnp.minimum(i, 1), 0)),
            pl.BlockSpec((step, 768), lambda i, p: (jnp.maximum(i - 2, 0), 0)),
            whole(2, 256),
        ],
        [shape(512, 768), shape(512, 768), shape(2, 256, dtype=F32)],
    )(place, d_query, d_key, d_value, qkv, qkv, sums, inv_rows, gains)


def back_kernel(place, *refs):
    rows_mine, rows_rest, d_mine, d_rest, raw_mine, raw_rest, raw_got = refs[:7]
    heads_mine, heads_rest, own_q, own_k, own_v, near, far, low, inv, gain_mlp, moe = refs[7:18]
    pieces, terms = refs[18:22], refs[22:26]
    mine, rest, total, d_own, d_other = refs[26:]
    i = pl.program_id(0)

    @pl.when(i == 0)
    def _():
        for r in range(4):
            mine[r * 128 : r * 128 + 128, :] = heads_mine[line_rows(place, r), :]
            rest[r * 128 : r * 128 + 128, :] = heads_rest[line_rows(place, r), :]
        d_own[...] = pick(place[2], raw_mine[...], raw_got[...])
        d_other[...] = pick(place[2], raw_got[...], raw_mine[...])

    qkv = dot(rows_mine[...], raw_mine[...], TN) + dot(rows_rest[...], raw_rest[...], TN)
    back = dot(d_mine[...], mine[...], TN) + dot(d_rest[...], rest[...], TN)
    grads = jnp.concatenate([qkv.astype(BF), back.astype(BF)], 1)
    for j, piece in enumerate(pieces):

        @pl.when(i // 2 == j)
        def _(piece=piece):
            piece[pl.ds(pl.multiple_of(lax.rem(i, 2) * 256, 256), 256), :] = grads

    other = jnp.where(i // 4 == place[1], near[...], far[...])
    own = jnp.concatenate([own_q[...], own_k[...], own_v[...]], 1)
    part = dot(d_own[...], own, NT) + dot(d_other[...], other, NT)
    total[...] = part
    gain = jnp.sum(part * (low[...].astype(F32) * inv[...]), axis=0, keepdims=True)
    zeros = jnp.zeros((14, gain.shape[1]), F32)
    gains = jnp.concatenate([gain, gain_mlp[...], zeros], 0).astype(BF)
    for r, out in enumerate(terms):
        out[0:128, :] = total[line_rows(place, r), :].astype(BF)
        out[128:144, :] = gains
    terms[2][144:272, :] = moe[...]


def back(
    rows_mine, rows_rest, d_mine, d_rest, raw_mine, raw_rest, raw_got, heads,
    own, near, far, low, inv, gain_mlp, moe, place,
):
    rows, width, step = 512, low.shape[1], 256
    block = lambda: pl.BlockSpec(
        (rows, step), lambda i, p: (0, lax.rem(p[3] + i // 2, 4) * 2 + lax.rem(i, 2))
    )
    half = lambda: pl.BlockSpec((step, 768), lambda i, p: (lax.rem(i, 4), 0))
    tile = lambda: pl.BlockSpec((step, 256), lambda i, p: (i, 0))
    column = lambda n: pl.BlockSpec((n, step), lambda i, p: (0, i))
    return call(
        back_kernel,
        (width // step,),
        [block(), block(), block(), block()]
        + [whole(rows, 768)] * 3
        + [whole(rows, 256)] * 2
        + [tile(), tile(), tile(), half(), half(), column(rows), whole(rows, 1), column(1), column(128)],
        [whole(512, 1024)] * 4 + [column(n) for n in (144, 144, 272, 144)],
        [shape(512, 1024)] * 4 + [shape(n, width) for n in (144, 144, 272, 144)],
        scratch=[
            pltpu.VMEM((rows, 256), BF),
            pltpu.VMEM((rows, 256), BF),
            pltpu.VMEM((rows, step), F32),
            pltpu.VMEM((rows, 768), BF),
            pltpu.VMEM((rows, 768), BF),
        ],
    )(
        place, rows_mine, rows_rest, d_mine, d_rest, raw_mine, raw_rest, raw_got, *heads,
        *own, near, far, low, inv, gain_mlp, moe,
    )


def last_rows_kernel(place, *refs):
    d_terms, moe_terms = refs[:4], refs[4:7]
    d_middle, middle, low, inv, gain = refs[7:12]
    parts, gains, rows = refs[-3:]
    total = sum((t[0:144].astype(F32) for t in d_terms[1:]), d_terms[0][...].astype(F32))
    gains[...] = total[128:130]
    d_in = total[:128]
    hat = low[...].astype(F32) * inv[...]
    scaled = d_in * gain[...]
    mean = jnp.mean(scaled * hat, axis=1, keepdims=True)
    rows[1] = (d_middle[...] + inv[...] * (scaled - hat * mean)).astype(BF)
    moe = sum((t[...].astype(F32) for t in moe_terms), d_terms[2][144:272].astype(F32))
    rows[0] = (middle[...] + moe).astype(BF)
    for i in range(8):
        parts[i] = rows[:, :, i * 256 : i * 256 + 256]


def last_rows(d_terms, moe_terms, d_middle, middle, low, inv, gain, awaited, place):
    width = low.shape[1]
    mine = lambda n: pl.BlockSpec((128, n), lambda i, p: (p[0], 0))
    return call(
        last_rows_kernel,
        (1,),
        [whole(n, width) for n in (144, 144, 272, 144)]
        + [whole(128, width)] * 5
        + [mine(width), mine(1), whole(1, width)]
        + [ANYWHERE] * len(awaited),
        [whole(8, 2, 128, 256), whole(2, width)],
        [shape(8, 2, 128, 256), shape(2, width, dtype=F32)],
        scratch=[pltpu.VMEM((2, 128, width), BF)],
        vmem=BIG,
    )(place, *d_terms, *moe_terms, d_middle, middle, low, inv, gain, *awaited)


def settle_attention_kernel(place, *refs):
    here, there = refs[:4], refs[4:8]
    query, key, value, back, small = refs[9:]
    i = pl.program_id(0)

    @pl.when(i == 0)
    def _():
        small[...] = jnp.zeros_like(small)

    def one(mine, rest):
        mine, rest = mine[0].astype(F32), rest[0].astype(F32)
        first = pick(place[1], rest[:128], mine[:128])
        second = pick(place[1], mine[:128], rest[:128])
        total = jnp.concatenate([first, second], 0)
        query[...] = total[:, :256]
        key[...] = total[:, 256:512]
        value[...] = total[:, 512:768]
        back[...] = total[:, 768:].T
        mine, rest = mine[128:], rest[128:]
        row = lax.broadcasted_iota(jnp.int32, mine.shape, 0)
        small[...] += jnp.where(row < 4, mine + rest, pick(place[2], mine, rest))

    for r in range(4):

        @pl.when(lax.rem(i // 2 + 4 - place[3], 4) == r)
        def _(r=r):
            one(here[r], there[r])


def settle_attention(here, there, awaited, place):
    piece = lambda: pl.BlockSpec((1, 144, 1024), lambda i, p: (lax.rem(i + p[4], 2), 0, 0))
    rows = lambda: pl.BlockSpec((256, 256), lambda i, p: (i, 0))
    return call(
        settle_attention_kernel,
        (8,),
        [piece() for _ in range(8)] + [ANYWHERE],
        [rows(), rows(), rows(), pl.BlockSpec((256, 256), lambda i, p: (0, i)), whole(16, 1024)],
        [shape(2048, 256, dtype=F32)] * 3
        + [shape(256, 2048, dtype=F32), shape(16, 1024, dtype=F32)],
    )(place, *here, *there, awaited)


def settle_experts_kernel(place, gu_mine, gu_got, down_mine, down_got, gate, up, down):
    total = pick(place[2], gu_mine[0], gu_got[0]).astype(F32)
    for j in range(2):
        gate[j] = total[:, j * 256 : j * 256 + 128]
        up[j] = total[:, j * 256 + 128 : j * 256 + 256]
    total = pick(place[2], down_mine[0], down_got[0]).astype(F32)
    down[...] = total.reshape(down.shape)


def settle_experts(gu_mine, gu_got, down_mine, down_got, place):
    def step(i, p, mine):
        return jnp.where(p[2] == mine, i, 0)

    def tall(mine):
        def index(i, p):
            j = step(i, p, mine)
            return (j // 4, lax.rem(j, 4), 0)

        return pl.BlockSpec((1, 512, 512), index)

    def flat(mine):
        def index(i, p):
            j = step(i, p, mine)
            return (j // 4, 0, lax.rem(j, 4))

        return pl.BlockSpec((1, 256, 512), index)

    thin = lambda: pl.BlockSpec((2, 512, 128), lambda i, p: (i // 4, lax.rem(i, 4), 0))
    return call(
        settle_experts_kernel,
        (8,),
        [tall(1), tall(0), flat(1), flat(0)],
        [thin(), thin(), pl.BlockSpec((2, 128, 512), lambda i, p: (i // 4, 0, lax.rem(i, 4)))],
        [shape(4, 2048, 128, dtype=F32)] * 2 + [shape(4, 128, 2048, dtype=F32)],
        flops=20_000_000_000,
    )(place, gu_mine, gu_got, down_mine, down_got)


def choice_weights(ids, gates, experts, capacity):
    named = ids[:, :, None] == jnp.arange(experts, dtype=jnp.int32)
    count = jnp.sum(named.astype(F32), axis=1)
    tokens = ids.shape[0]
    earlier = (
        jnp.arange(tokens, dtype=jnp.int32)[:, None] > jnp.arange(tokens, dtype=jnp.int32)[None, :]
    ).astype(BF)
    place = jnp.dot(earlier, count.astype(BF), preferred_element_type=F32)
    weight = jnp.sum(jnp.where(named, gates[:, :, None], 0.0), axis=1)
    return jnp.where(place < capacity, weight, 0.0)


def local(
    hidden_in,
    cotangent,
    sequence_order,
    seq_lengths,
    expert_ids,
    gate_weights,
    w_query,
    w_key,
    w_value,
    w_output,
    gain_attn,
    gain_query,
    gain_key,
    gain_mlp,
    w_gate,
    w_up,
    w_down,
):
    zl, y, c, zh, x = (lax.axis_index(a) for a in AXES)
    same = c == zh
    length = hidden_in.shape[1]
    half = length // 2
    experts = w_gate.shape[0]
    width = w_query.shape[0]
    place = jnp.stack([x, c, same.astype(jnp.int32), y, zl, zh]).astype(jnp.int32)
    sequence = (zl * SIZES[1] + y) * 2 + zh
    tokens_here = seq_lengths[sequence]
    ids_here = expert_ids[sequence]
    gates_here = gate_weights[sequence]

    x_dealt = deal_in(hidden_in[0], zh)
    qkv_own = [w_query, w_key, w_value]
    qkv_near = other_half(qkv_own, c, x_dealt)
    x_pieces = gather_x(x_dealt)
    cot_dealt = deal_in(cotangent[0], zh, x_pieces[1])
    gains_own = jnp.stack([gain_query, gain_key], 0)
    gains_other = other_half_chip(gains_own)
    gains_keep = jnp.where(same, gains_own, gains_other)
    gains_qk = jnp.concatenate([gains_keep, jnp.where(same, gains_other, gains_own)], 0)

    cosine_np, sine_np = rope_tables(length)
    swap_halves = lambda t: lax.dynamic_slice_in_dim(
        jnp.concatenate([t, t], 0), c * half, length, 0
    )
    cosine_all, sine_all = swap_halves(jnp.asarray(cosine_np)), swap_halves(jnp.asarray(sine_np))
    positions = (jnp.arange(length, dtype=jnp.int32) + c * half) % length
    bias = jnp.where(positions < tokens_here, 0.0, -1e30).astype(F32)
    weight_all = choice_weights(ids_here, gates_here, experts, length * 2 // experts)
    weight_here = lax.dynamic_slice_in_dim(weight_all, c * half, half, 0)
    weight_here = lax.dynamic_slice_in_dim(
        jnp.concatenate([weight_here, weight_here], 0), x * (half // 4), half, 0
    )

    x_low, attn_in, inv_one = norm_rows(x_pieces, place, gain_attn[None, :])
    qkv_near, cot_first = tie([qkv_near, cot_dealt], attn_in)
    qkv_far = other_core(qkv_near)
    out_near = other_half([w_output], c, attn_in)
    raw_send, raw_keep, squares = project(attn_in, qkv_own, qkv_near, qkv_far, out_near, place)
    inv_qk = lax.rsqrt(sum_x(squares[:2]) / width + EPS)
    (out_near,) = tie([out_near], inv_qk)
    down_near = other_half([w_down], c, out_near)
    gu_near = other_half([w_gate, w_up], c, out_near)
    cot_pieces = gather_x(cot_first, inv_qk)
    ready_send, ready_keep = prep(
        raw_send,
        raw_keep,
        inv_qk,
        gains_qk,
        cosine_all[:half],
        sine_all[:half],
        (cot_pieces[1], cot_pieces[4]),
        place,
    )
    ready_rest = other_core(ready_send)
    qkv, heads_mine, heads_rest, lse = attend(ready_keep, ready_rest, bias[None, :], place)
    heads_got = other_core(heads_rest)
    out_near, inv_tied = tie([out_near, inv_qk], heads_got)
    out_far = other_core(out_near)
    inv_qk_rest = other_core(inv_tied)
    cot = place_rows(cot_pieces, place)
    attn_terms = send_x(
        heads_to_rows(heads_mine, heads_got, w_output, out_near, out_far, (cot, heads_got), place)
    )
    attn_in, cot = tie([attn_in, cot], heads_got)
    attn_in_rest = other_core(attn_in)
    cot_rest = other_core(cot)

    middle, moe_own, inv_two = middle_rows(attn_terms, x_low, gain_mlp[None, :], place)
    moe_pieces = gather_x(moe_own)
    gu_near, down_near = tie([gu_near, down_near], moe_pieces[1])
    gu_near, down_near = tie([gu_near, down_near], moe_pieces[4])
    down_far = other_core(down_near)
    cot_down = cot_back(cot, w_down, down_near, down_far, place)
    gu_far = other_core(gu_near)
    hidden_send, hidden_keep, moe_in, *d_moe_terms = expert_layer(
        moe_pieces, cot_down, weight_here, w_gate, w_up, gu_near, gu_far, place
    )
    d_moe_terms = send_x(d_moe_terms)
    moe_terms = expert_out(
        hidden_send, hidden_keep, w_down, down_near, down_far, hidden_keep, place
    )
    hidden_all = jnp.concatenate([hidden_keep, other_core(hidden_send)], 1)
    moe_all = jnp.concatenate([moe_in, other_core(moe_in)], 0)
    cot_all = jnp.concatenate([cot, cot_rest], 0)
    grad_gate_up = jnp.einsum(
        "td,etf->edf", moe_all, hidden_all[:, :, :512], preferred_element_type=F32
    ).astype(BF)
    grad_down = jnp.einsum(
        "etf,td->efd", hidden_all[:, :, 512:], cot_all, preferred_element_type=F32
    ).astype(BF)

    d_middle, d_own, gain_mlp_part = middle_back(
        d_moe_terms,
        middle,
        inv_two,
        gain_mlp[None, :],
        cot,
        (grad_gate_up, grad_down, moe_terms[0]),
        place,
    )
    grad_gate_up, grad_down = lax.psum((grad_gate_up, grad_down), GROUPS)
    d_pieces = gather_x(d_own)
    d_heads_keep, d_heads_send, d_attn = rows_to_heads(
        d_pieces, w_output, out_near, out_far, place
    )
    d_heads_rest = other_core(d_heads_send)
    *moe_terms, d_attn = tie(list(moe_terms) + [d_attn], d_heads_rest)
    moe_after, moe_before = along(moe_terms[1], "x", 1), along(moe_terms[3], "x", -1)
    d_attn_rest = other_core(d_attn)
    d_query, d_key, d_value, sums = attend_back(
        qkv,
        d_heads_keep,
        d_heads_rest,
        heads_mine,
        heads_rest,
        bias[None, :],
        lse,
        cosine_all,
        sine_all,
        place,
    )
    (sums,) = tie([sums], moe_after)
    (sums,) = tie([sums], moe_before)
    sums_rest = other_core(sums)
    sums = sums + jnp.concatenate([sums_rest[:, half:], sums_rest[:, :half]], 1)
    sums = sum_x(sums) / width
    raw_mine, raw_rest, gain_qk_parts = raw_back(
        d_query,
        d_key,
        d_value,
        qkv,
        sums,
        jnp.concatenate([inv_qk, inv_qk_rest], 1),
        gains_keep,
        place,
    )
    raw_got = other_core(raw_rest)
    pieces = back(
        attn_in,
        attn_in_rest,
        d_attn,
        d_attn_rest,
        raw_mine,
        raw_rest,
        raw_got,
        (heads_mine, heads_rest),
        qkv_own,
        qkv_near,
        qkv_far,
        x_low,
        inv_one,
        gain_mlp_part,
        moe_terms[2],
        place,
    )
    weight_terms = send_y(pieces[:4])
    d_in_terms = send_x(pieces[4:])
    moe_terms = [moe_terms[0], moe_after, moe_before]
    rows_dealt, gains = last_rows(
        d_in_terms,
        moe_terms,
        d_middle,
        middle,
        x_low,
        inv_one,
        gain_attn[None, :],
        weight_terms[1:],
        place,
    )
    output, grad_input, dealt = deal_out(rows_dealt, same)
    grad_gate_up, grad_down = tie([grad_gate_up, grad_down], rows_dealt)
    total = sum((t.astype(F32) for t in weight_terms[1:]), weight_terms[0].astype(F32)).astype(BF)
    near, far = to_shard(total, zl, same)
    total = (near.astype(F32) + far.astype(F32)).astype(BF)
    first = c == 0
    got = other_core(jnp.where(first, total[128:], total[:128]))
    mine = jnp.where(first, total[:128], total[128:]).astype(F32) + got.astype(F32)
    small = jnp.concatenate([gains.reshape(-1), gain_qk_parts.reshape(-1)])
    small = (small + lax.ppermute(small, "zh", [(0, 1), (1, 0)])).reshape(9, 512)
    small = jnp.concatenate([small.reshape(-1), jnp.zeros((11776,), F32)]).reshape(16, 1024)
    (mine,) = tie([jnp.concatenate([mine, small], 0).astype(BF)], dealt)
    here = from_groups(mine)

    grad_gate, grad_up, grad_down = settle_experts(
        grad_gate_up, settle(grad_gate_up), grad_down, settle(grad_down), place
    )
    grad_query, grad_key, grad_value, grad_output, small = settle_attention(
        here, [other_core(t) for t in here], grad_down, place
    )
    small = small.reshape(-1)
    return (
        output[None],
        grad_input[None],
        grad_query,
        grad_key,
        grad_value,
        grad_output,
        small[:width],
        small[2 * width : 2 * width + 256],
        small[2 * width + 256 : 2 * width + 512],
        small[width : 2 * width],
        grad_gate,
        grad_up,
        grad_down,
    )


def solution(mesh):
    fine = Mesh(mesh.devices.reshape(SIZES), AXES)
    columns = P(None, TENSOR)
    placed = (
        P(DP, None, TENSOR),
        P(DP, None, TENSOR),
        P(),
        P(),
        P(),
        P(),
        columns,
        columns,
        columns,
        P(TENSOR, None),
        P(),
        P(TENSOR),
        P(TENSOR),
        P(),
        P(None, None, TENSOR),
        P(None, None, TENSOR),
        P(None, TENSOR, None),
    )
    return jax.shard_map(
        local,
        mesh=fine,
        in_specs=placed,
        out_specs=placed[:2]
        + (columns, columns, columns, P(TENSOR, None), P(), P(TENSOR), P(TENSOR), P())
        + placed[14:],
        check_vma=False,
    )
```

```python
import math

import jax
import jax.numpy as jnp
import numpy as np
from jax import lax
from jax.experimental import pallas as pl
from jax.experimental.pallas import tpu as pltpu
from jax.sharding import Mesh
from jax.sharding import PartitionSpec as P

AXES = ("zl", "y", "c", "zh", "x")
SIZES = (2, 4, 2, 2, 4)
DP = ("zl", "y", "c")
TENSOR = ("zh", "x")
GROUPS = ("zl", "y", "zh")

HEAD_DIM = 128
EPS = 1e-06
BASE = 50000.0
BF = jnp.bfloat16
F32 = jnp.float32
SCALE = 1.0 / math.sqrt(HEAD_DIM)
VMEM = 32 * 1024 * 1024
BIG = 56 * 1024 * 1024


def rope_tables(length):
    half = HEAD_DIM // 2
    frequency = np.power(
        np.float32(BASE), np.float32(-2.0) * np.arange(half, dtype=np.float32) / HEAD_DIM
    ).astype(np.float32)
    angles = np.arange(length, dtype=np.float32)[:, None] * frequency[None, :]
    cosine = np.cos(angles.astype(np.float64)).astype(np.float32)
    sine = np.sin(angles.astype(np.float64)).astype(np.float32)
    return np.concatenate([cosine, cosine], 1), np.concatenate([-sine, sine], 1)


def along(value, axis, shift):
    size = SIZES[AXES.index(axis)]
    return lax.ppermute(value, axis, [(i, (i + shift) % size) for i in range(size)])


def other_core(value):
    return lax.ppermute(value, "c", [(0, 1), (1, 0)])


def other_half_chip(value):
    return lax.ppermute(value, ("zl", "zh"), [(i, 3 - i) for i in range(4)])


def sum_x(value):
    return value + along(value, "x", 1) + along(value, "x", 2) + along(value, "x", 3)


def gather_x(value, awaited=None):
    half = value.shape[0] // 2
    after, before = along(value, "x", -1), along(value, "x", 1)
    far = [after[:half], before[half:]]
    if awaited is not None:
        far = tie(far, awaited)
    return [value, after, along(far[0], "x", -1), along(far[1], "x", 1), before]


def tie_kernel(*refs):
    del refs


def tie(values, awaited):
    anywhere = pl.BlockSpec(memory_space=pl.ANY)
    count = len(values)
    return pl.pallas_call(
        tie_kernel,
        in_specs=[anywhere] * (count + 1),
        out_specs=[anywhere] * count,
        out_shape=[jax.ShapeDtypeStruct(v.shape, v.dtype) for v in values],
        input_output_aliases={i: i for i in range(count)},
    )(*values, awaited)


def later(start, awaited):
    ends = awaited[(0,) * awaited.ndim].astype(F32) + awaited[(-1,) * awaited.ndim].astype(F32)
    return start + (ends != ends).astype(jnp.int32)


def send_x(pieces):
    return [
        pieces[0],
        along(pieces[1], "x", 1),
        along(pieces[2], "x", 2),
        along(pieces[3], "x", -1),
    ]


def deal_in(value, zh, awaited=None):
    half = value.shape[0] // 2
    got = []
    for k in (0, 1):
        pairs = [(a * 2 + b, (b ^ k) * 2 + a) for a in range(2) for b in range(2)]
        start = (zh ^ k) * half
        if awaited is not None:
            start = later(start, awaited)
        part = lax.dynamic_slice_in_dim(value, start, half, 0)
        got.append(lax.ppermute(part, ("c", "zh"), pairs))
    return jnp.stack(got, 0)


def deal_line(parts):
    return lax.all_to_all(parts, ("c", "x"), 0, 0, tiled=True)


def deal_out(dealt, same):
    got = dealt.transpose(1, 0, 2, 3).reshape(2, 1024, 256)
    moved = lax.ppermute(got, ("c", "zh"), [(1, 2), (2, 1)])
    got = jnp.where(same, got, moved)
    return got[0], got[1]


def other_half(weights, c, awaited):
    half = weights[0].shape[0] // 2
    start = later(c * half, awaited)
    parts = [lax.dynamic_slice_in_dim(w, start, half, 0) for w in weights]
    return other_half_chip(jnp.concatenate(parts, parts[0].ndim - 1))


def send_y(pieces):
    return [pieces[0]] + [along(pieces[r], "y", r) for r in (1, 2, 3)]


def to_shard(value, zl, same):
    low, high = value[:256], value[256:]
    near = jnp.where(zl == 0, low, high)
    far = jnp.where(zl == 0, high, low)
    order = [(i, k, m) for i in range(2) for k in range(2) for m in range(2)]
    index = lambda i, k, m: (i * 2 + k) * 2 + m
    stay = [(index(i, k, m), index(i, m, k)) for i, k, m in order if k != m]
    flip = [(index(i, k, m), index(1 - i, m, k)) for i, k, m in order]
    axes = ("zl", "c", "zh")
    got = lax.ppermute(near, axes, stay)
    return jnp.where(same, near, got), lax.ppermute(far, axes, flip)


def from_groups(piece):
    pair = jnp.stack([piece, lax.ppermute(piece, "zl", [(0, 1), (1, 0)])], 0)
    return [pair] + [along(pair, "y", -r) for r in (1, 2, 3)]


def settle(value):
    return lax.ppermute(value, ("c", "zh"), [(0, 2), (3, 1)])


def dot(left, right, dims):
    return lax.dot_general(left, right, (dims, ((), ())), preferred_element_type=F32)


NT = ((1,), (1,))
NN = ((1,), (0,))
TN = ((0,), (0,))


def call(kernel, grid, in_specs, out_specs, out_shape, scratch=(), flops=1, vmem=VMEM):
    return pl.pallas_call(
        kernel,
        grid_spec=pltpu.PrefetchScalarGridSpec(
            num_scalar_prefetch=1,
            grid=grid,
            in_specs=in_specs,
            out_specs=out_specs,
            scratch_shapes=scratch,
        ),
        out_shape=out_shape,
        compiler_params=pltpu.CompilerParams(vmem_limit_bytes=vmem),
        cost_estimate=pl.CostEstimate(flops=flops, bytes_accessed=1, transcendentals=0),
    )


def shape(*dims, dtype=BF):
    return jax.ShapeDtypeStruct(dims, dtype)


def whole(*dims):
    return pl.BlockSpec(dims, lambda i, p: (0,) * len(dims))


ANYWHERE = pl.BlockSpec(memory_space=pl.ANY)


def line_rows(place, r, rows=128):
    return pl.ds(pl.multiple_of(lax.rem(place[0] + r, 4) * rows, rows), rows)


def pick(flag, yes, no):
    return jnp.where(flag == 1, yes, no)


def pair_of(i, p):
    return jnp.where(i == 0, p[1], jnp.where(i == 1, 1 - p[1], i - 2))


def send_pair(i, p):
    other = jnp.where(i == 0, p[1], 1 - p[1])
    return jnp.where(p[2] == 1, other, jnp.maximum(i - 2, 0))


def keep_pair(i, p):
    other = jnp.where(i == 0, p[1], 1 - p[1])
    return jnp.where(p[2] == 1, jnp.maximum(i - 2, 0), other)


def role(i, p, first):
    return jnp.where(i < first, 1 - p[2], p[2])


def column_blocks(place, pieces):
    own, after, far_low, far_high, before = pieces
    for r, (first, second) in enumerate(
        ((own, own), (after, after), (far_low, far_high), (before, before))
    ):
        for k, piece in enumerate((first, second)):
            index = lax.rem(place[1] + k, 2) * 4 + lax.rem(place[0] + r, 4)
            yield pl.multiple_of(index * 256, 256), piece[k if r != 2 else 0]


def norm_kernel(place, own, after, far_low, far_high, before, gain, low, normed, inv):
    squares = jnp.zeros((low.shape[0], 1), F32)
    for column, here in column_blocks(place, (own, after, far_low, far_high, before)):
        low[:, pl.ds(column, 256)] = here
        here = here.astype(F32)
        squares += jnp.sum(here * here, axis=1, keepdims=True)
    root = lax.rsqrt(squares / low.shape[1] + EPS)
    inv[...] = root
    normed[...] = (low[...].astype(F32) * root * gain[...]).astype(BF)


def piece_specs(step, rows_of):
    return [pl.BlockSpec((n, step, 256), rows_of) for n in (2, 2, 1, 1, 2)]


def norm_rows(pieces, place, gain):
    rows, step = pieces[0].shape[1], 128
    full = lambda: pl.BlockSpec((step, 2048), lambda i, p: (i, 0))
    return call(
        norm_kernel,
        (rows // step,),
        piece_specs(step, lambda i, p: (0, i, 0)) + [whole(1, 2048)],
        [full(), full(), pl.BlockSpec((step, 1), lambda i, p: (i, 0))],
        [shape(rows, 2048), shape(rows, 2048), shape(rows, 1, dtype=F32)],
    )(place, *pieces, gain)


def place_kernel(place, own, after, far_low, far_high, before, low):
    for column, here in column_blocks(place, (own, after, far_low, far_high, before)):
        low[:, pl.ds(column, 256)] = here


def place_rows(pieces, place):
    rows = pieces[0].shape[1]
    step = rows // 4
    return call(
        place_kernel,
        (4,),
        piece_specs(step, lambda i, p: (0, lax.rem(i + p[0], 4), 0)),
        pl.BlockSpec((step, 2048), lambda i, p: (i, 0)),
        shape(rows, 2048),
    )(place, *pieces)


def project_kernel(place, rows_in, *refs):
    *own, near, far, awaited, send, keep, squares, columns = refs
    i = pl.program_id(0)
    lane = lax.broadcasted_iota(jnp.int32, columns.shape, 1)

    @pl.when(i == 0)
    def _():
        columns[...] = jnp.zeros_like(columns)

    def finish(raw):
        kept = role(i, place, 3)

        @pl.when(kept == 1)
        def _():
            keep[...] = raw

        @pl.when(kept == 0)
        def _():
            send[...] = raw

        total = jnp.sum(raw * raw, axis=1, keepdims=True)
        columns[...] += jnp.where(lane == lax.rem(i, 3), total, 0.0)

    @pl.when(i < 3)
    def _():
        half = near.shape[0]
        here = pl.ds(pl.multiple_of(place[1] * half, half), half)
        there = pl.ds(pl.multiple_of((1 - place[1]) * half, half), half)
        finish(dot(rows_in[:, here], near[...], NN) + dot(rows_in[:, there], far[...], NN))

    for j, weight in enumerate(own):

        @pl.when(i == 3 + j)
        def _(weight=weight):
            finish(dot(rows_in[...], weight[...], NN))

    @pl.when(i == 5)
    def _():
        squares[...] = columns[...].T


def project(rows_in, own, near, far, awaited, place):
    rows, width = rows_in.shape
    other = lambda i: jnp.minimum(i, 2)
    mine = lambda i: jnp.maximum(i - 3, 0)
    return call(
        project_kernel,
        (6,),
        [
            whole(rows, width),
            whole(width, 256),
            whole(width, 256),
            whole(width, 256),
            pl.BlockSpec((width // 2, 256), lambda i, p: (0, other(i))),
            pl.BlockSpec((width // 2, 256), lambda i, p: (0, other(i))),
            ANYWHERE,
        ],
        [
            pl.BlockSpec((rows, 256), lambda i, p: (0, jnp.where(p[2] == 1, other(i), mine(i)))),
            pl.BlockSpec((rows, 256), lambda i, p: (0, jnp.where(p[2] == 1, mine(i), other(i)))),
            whole(8, rows),
        ],
        [shape(rows, 768, dtype=F32), shape(rows, 768, dtype=F32), shape(8, rows, dtype=F32)],
        scratch=[pltpu.VMEM((rows, 8), F32)],
    )(place, rows_in, *own, near, far, awaited)


def columns_of(rows_two):
    rest = jnp.zeros((6, rows_two.shape[1]), F32)
    return jnp.concatenate([rows_two, rest], 0).T


def prep_kernel(place, raw_send, raw_keep, inv_rows, gains, cosine, sine, first, second, out_send, out_keep):
    inv = columns_of(inv_rows[...])
    for part, (raw, out) in enumerate(((raw_keep, out_keep), (raw_send, out_send))):
        for i in range(2):
            for h in range(2):
                lo = i * 256 + h * 128
                normed = raw[:, lo : lo + 128] * inv[:, i : i + 1]
                out[:, 768 + lo : 896 + lo] = normed.astype(BF)
                normed = normed * gains[part * 2 + i : part * 2 + i + 1, h * 128 : h * 128 + 128]
                out[:, lo : lo + 128] = (
                    normed * cosine[...] + pltpu.roll(normed, 64, 1) * sine[...]
                ).astype(BF)
        out[:, 512:768] = raw[:, 512:768].astype(BF)


def prep(raw_send, raw_keep, inv_rows, gains, cosine, sine, awaited, place):
    rows, step = raw_send.shape[0], 128
    spec = lambda width: pl.BlockSpec((step, width), lambda i, p: (i, 0))
    return call(
        prep_kernel,
        (rows // step,),
        [
            spec(768),
            spec(768),
            pl.BlockSpec((2, step), lambda i, p: (0, i)),
            whole(4, 256),
            spec(128),
            spec(128),
            ANYWHERE,
            ANYWHERE,
        ],
        [spec(1280), spec(1280)],
        [shape(rows, 1280), shape(rows, 1280)],
    )(place, raw_send, raw_keep, inv_rows, gains, cosine, sine, *awaited)


def attend_kernel(place, mine, rest, bias, qkv, out_mine, out_rest, lse):
    rows = 256
    qkv[0:512, :] = mine[...]
    qkv[512:1024, :] = rest[...]
    for h in range(2):
        cols = slice(h * 128, h * 128 + 128)
        keys = qkv[:, 256 + h * 128 : 384 + h * 128]
        values = qkv[:, 512 + h * 128 : 640 + h * 128]
        for i in range(4):
            here = slice(i * rows, (i + 1) * rows)
            scores = dot(qkv[here, cols], keys, NT) * SCALE + bias[...]
            top = jnp.max(scores, axis=1, keepdims=True)
            weight = jnp.exp(scores - top)
            total = jnp.sum(weight, axis=1, keepdims=True)
            out = out_mine if i < 2 else out_rest
            out[i % 2 * rows : i % 2 * rows + rows, cols] = (
                dot(weight.astype(BF), values, NN) / total
            ).astype(BF)
            wide = jnp.broadcast_to(top + jnp.log(total), (rows, 8))
            lse[h : h + 1, here] = wide.T[0:1, :]


def attend(mine, rest, bias, place):
    return call(
        attend_kernel,
        (1,),
        [whole(512, 1280), whole(512, 1280), whole(1, 1024)],
        [whole(1024, 1280), whole(512, 256), whole(512, 256), whole(2, 1024)],
        [shape(1024, 1280), shape(512, 256), shape(512, 256), shape(2, 1024, dtype=F32)],
    )(place, mine, rest, bias)


def fill_other(place, near, far, other):
    half = near.shape[0]
    other[pl.ds(pl.multiple_of(place[1] * half, half), half), :] = near[...]
    other[pl.ds(pl.multiple_of((1 - place[1]) * half, half), half), :] = far[...]


def heads_to_rows_kernel(place, keep, send, own, near, far, first, second, a, b, c, d, other):
    fill_other(place, near, far, other)
    for r, out in enumerate((a, b, c, d)):
        here = line_rows(place, r)
        left, right = keep[here, :], send[here, :]
        part = dot(pick(place[2], left, right), own[...], NN)
        part += dot(pick(place[2], right, left), other[...], NN)
        out[...] = part.astype(BF)


def heads_to_rows(heads, rest, own, near, far, awaited, place):
    width = own.shape[1]
    step = width // 2
    tile = lambda n: pl.BlockSpec((n, step), lambda i, p: (0, i))
    return call(
        heads_to_rows_kernel,
        (2,),
        [whole(512, 256), whole(512, 256), tile(256), tile(128), tile(128), ANYWHERE, ANYWHERE],
        [tile(128)] * 4,
        [shape(128, width)] * 4,
        scratch=[pltpu.VMEM((256, step), BF)],
    )(place, heads, rest, own, near, far, *awaited)


def fill(rows, pieces):
    start = 0
    for piece in pieces:
        rows[start : start + piece.shape[0], :] = piece[...]
        start += piece.shape[0]


def rows_to_heads_kernel(
    place, own_rows, after, far_low, far_high, before, own, near, far,
    keep, send, rows, other,
):
    fill(rows, (own_rows, after, far_low, far_high, before))
    fill_other(place, near, far, other)
    mine = dot(rows[...], own[...], NT).astype(BF)
    rest = dot(rows[...], other[...], NT).astype(BF)
    for out, part in ((send, pick(place[2], rest, mine)), (keep, pick(place[2], mine, rest))):
        for r in range(4):
            out[line_rows(place, r), :] = part[r * 128 : r * 128 + 128]


def rows_to_heads(pieces, own, near, far, place):
    width = own.shape[1]
    return call(
        rows_to_heads_kernel,
        (1,),
        [whole(n, width) for n in (128, 128, 64, 64, 128, 256, 128, 128)],
        [whole(512, 256), whole(512, 256), whole(512, width)],
        [shape(512, 256), shape(512, 256), shape(512, width)],
        scratch=[pltpu.VMEM((256, width), BF)],
        vmem=BIG,
    )(place, *pieces, own, near, far)


def middle_kernel(place, a, b, c, d, low, gain, middle, normed, inv):
    total = sum((t[...].astype(F32) for t in (b, c, d)), a[...].astype(F32))
    total = low[...].astype(F32) + total
    middle[...] = total
    root = lax.rsqrt(jnp.mean(total * total, axis=1, keepdims=True) + EPS)
    inv[...] = root
    normed[...] = (total * root * gain[...]).astype(BF)


def middle_rows(terms, low, gain, place):
    width = low.shape[1]
    return call(
        middle_kernel,
        (1,),
        [whole(128, width)] * 4
        + [pl.BlockSpec((128, width), lambda i, p: (p[0], 0)), whole(1, width)],
        [whole(128, width), whole(128, width), whole(128, 1)],
        [shape(128, width, dtype=F32), shape(128, width), shape(128, 1, dtype=F32)],
    )(place, *terms, low, gain)


def middle_back_kernel(
    place, a, b, c, d, middle, inv, gain, cot, ready_a, ready_b, ready_c, d_middle, d_low, gain_part
):
    d_in = sum((t[...].astype(F32) for t in (b, c, d)), a[...].astype(F32))
    hat = middle[...] * inv[...]
    gain_part[...] = jnp.sum(d_in * hat, axis=0, keepdims=True)
    scaled = d_in * gain[...]
    mean = jnp.mean(scaled * hat, axis=1, keepdims=True)
    total = cot[...].astype(F32) + inv[...] * (scaled - hat * mean)
    d_middle[...] = total
    d_low[...] = total.astype(BF)


def middle_back(terms, middle, inv, gain, cot, ready, place):
    width = middle.shape[1]
    return call(
        middle_back_kernel,
        (1,),
        [whole(128, width)] * 5
        + [whole(128, 1), whole(1, width), whole(128, width)]
        + [ANYWHERE] * 3,
        [whole(128, width), whole(128, width), whole(1, width)],
        [shape(128, width, dtype=F32), shape(128, width), shape(1, width, dtype=F32)],
        vmem=BIG,
    )(place, *terms, middle, inv, gain, cot, *ready)


def cot_back_kernel(place, cot, own, near, far, out):
    def one(down):
        out[0] = dot(cot[...], down, NT)

    i = pl.program_id(0)
    pl.when(i == 0)(lambda: one(near[...].reshape(256, near.shape[2])))
    pl.when(i == 1)(lambda: one(far[...].reshape(256, far.shape[2])))
    pl.when(i >= 2)(lambda: one(own[...].reshape(256, own.shape[2])))


def own_pair(i, p):
    return (jnp.maximum(i - 2, 0), 0, 0)


def cot_back(cot, own, near, far, place):
    rows, width = cot.shape
    return call(
        cot_back_kernel,
        (4,),
        [
            whole(rows, width),
            pl.BlockSpec((2, 128, width), own_pair),
            whole(2, 128, width),
            whole(2, 128, width),
        ],
        pl.BlockSpec((1, rows, 256), lambda i, p: (i, 0, 0)),
        shape(4, rows, 256, dtype=F32),
        flops=5_000_000_000,
    )(place, cot, own, near, far)


def expert_kernel(
    place, own_rows, after, far_low, far_high, before, back, weights, own_gate, own_up, near, far,
    send, keep, rows, a, b, c, d, total, both_weights,
):
    i = pl.program_id(0)

    @pl.when(i == 0)
    def _():
        fill(rows, (own_rows, after, far_low, far_high, before))

    def two(gate, gate_start, up, up_start):
        for j in range(2):
            both_weights[:, j * 256 : j * 256 + 128] = gate[j, :, gate_start : gate_start + 128]
            both_weights[:, j * 256 + 128 : j * 256 + 256] = up[j, :, up_start : up_start + 128]
        lane = lax.broadcasted_iota(jnp.int32, weights.shape, 1)
        pre = dot(rows[...], both_weights[...], NN)
        grads, acts = [], []
        for j in range(2):
            named = lane == pair_of(i, place) * 2 + j
            weight = jnp.sum(jnp.where(named, weights[...], 0.0), axis=1, keepdims=True)
            gate = pre[:, j * 256 : j * 256 + 128]
            up = pre[:, j * 256 + 128 : j * 256 + 256]
            sig = 1.0 / (1.0 + jnp.exp(-gate))
            silu = gate * sig
            d_act = weight * back[0, :, j * 128 : j * 128 + 128]
            acts.append((weight * (silu * up)).astype(BF))
            grads.append((d_act * up * sig * (1.0 + gate * (1.0 - sig))).astype(BF))
            grads.append((d_act * silu).astype(BF))
        both = jnp.concatenate(grads, 1)
        hidden = jnp.concatenate([both] + acts, 1)
        kept = role(i, place, 2)

        @pl.when(kept == 1)
        def _():
            keep[0] = hidden

        @pl.when(kept == 0)
        def _():
            send[0] = hidden

        part = dot(both, both_weights[...], NT)

        @pl.when(i == 0)
        def _():
            total[...] = part

        @pl.when(i > 0)
        def _():
            total[...] += part

    pl.when(i == 0)(lambda: two(near, 0, near, 128))
    pl.when(i == 1)(lambda: two(far, 0, far, 128))
    pl.when(i >= 2)(lambda: two(own_gate, 0, own_up, 0))

    @pl.when(i == 3)
    def _():
        for r, out in enumerate((a, b, c, d)):
            out[...] = total[r * 128 : r * 128 + 128, :].astype(BF)


def expert_layer(pieces, back, weights, own_gate, own_up, near, far, place):
    rows, width = 512, pieces[0].shape[1]
    return call(
        expert_kernel,
        (4,),
        [whole(n, width) for n in (128, 128, 64, 64, 128)]
        + [
            pl.BlockSpec((1, rows, 256), lambda i, p: (i, 0, 0)),
            whole(rows, 4),
            pl.BlockSpec((2, width, 128), own_pair),
            pl.BlockSpec((2, width, 128), own_pair),
            whole(2, width, 256),
            whole(2, width, 256),
        ],
        [
            pl.BlockSpec((1, rows, 768), lambda i, p: (send_pair(i, p), 0, 0)),
            pl.BlockSpec((1, rows, 768), lambda i, p: (keep_pair(i, p), 0, 0)),
            whole(rows, width),
        ]
        + [whole(128, width)] * 4,
        [shape(2, rows, 768), shape(2, rows, 768), shape(rows, width)] + [shape(128, width)] * 4,
        scratch=[pltpu.VMEM((rows, width), F32), pltpu.VMEM((width, 512), BF)],
        vmem=44 * 1024 * 1024,
    )(place, *pieces, back, weights, own_gate, own_up, near, far)


def expert_out_kernel(place, send, keep, own, near, far, awaited, a, b, c, d, total):
    i = pl.program_id(0)

    def one(down):
        acts = pick(role(i, place, 2), keep[0], send[0])
        part = dot(acts, down, NN)

        @pl.when(i == 0)
        def _():
            total[...] = part

        @pl.when(i > 0)
        def _():
            total[...] += part

    pl.when(i == 0)(lambda: one(near[...].reshape(256, near.shape[2])))
    pl.when(i == 1)(lambda: one(far[...].reshape(256, far.shape[2])))
    pl.when(i >= 2)(lambda: one(own[...].reshape(256, own.shape[2])))

    @pl.when(i == 3)
    def _():
        for r, out in enumerate((a, b, c, d)):
            out[...] = total[r * 128 : r * 128 + 128, :].astype(BF)


def expert_out(send, keep, own, near, far, awaited, place):
    rows, width = 512, own.shape[2]
    return call(
        expert_out_kernel,
        (4,),
        [
            pl.BlockSpec((1, rows, 256), lambda i, p: (send_pair(i, p), 0, 2)),
            pl.BlockSpec((1, rows, 256), lambda i, p: (keep_pair(i, p), 0, 2)),
            pl.BlockSpec((2, 128, width), own_pair),
            whole(2, 128, width),
            whole(2, 128, width),
            ANYWHERE,
        ],
        [whole(128, width)] * 4,
        [shape(128, width)] * 4,
        scratch=[pltpu.VMEM((rows, width), F32)],
        flops=5_000_000_000,
    )(place, send, keep, own, near, far, awaited)


def attend_back_kernel(
    place, qkv, d_mine, d_rest, heads_mine, heads_rest, bias, lse, cosine, sine, d_query, d_key, d_value, sums, key_sum, value_sum
):
    rows = 256

    def unturn(grad, here):
        return grad * cosine[here, :] - pltpu.roll(grad, 64, 1) * sine[here, :]

    masked = jnp.broadcast_to(bias[...], (8, 1024)).T[:, 0:1]
    for h in range(2):
        cols = slice(h * 128, h * 128 + 128)
        keys = qkv[:, 256 + h * 128 : 384 + h * 128]
        keys_turned = keys.T
        values = qkv[:, 512 + h * 128 : 640 + h * 128]
        for i in range(4):
            here = slice(i * rows, (i + 1) * rows)
            query = qkv[here, cols]
            inside = slice(i % 2 * rows, i % 2 * rows + rows)
            d_here = (d_mine if i < 2 else d_rest)[inside, cols]
            heads = (heads_mine if i < 2 else heads_rest)[inside, cols]
            scores = dot(keys, query, NT) * SCALE + masked
            probs = jnp.exp(scores - lse[h : h + 1, here])
            mean = d_here.astype(F32) * heads.astype(F32)
            mean = jnp.sum(mean.T, axis=0, keepdims=True)
            d_scores = (probs * (dot(values, d_here, NT) - mean)).astype(BF)
            value_part = dot(probs.astype(BF), d_here, NN)
            key_part = dot(d_scores, query, NN)
            if i == 0:
                value_sum[...] = value_part
                key_sum[...] = key_part
            else:
                value_sum[...] += value_part
                key_sum[...] += key_part
            d_turned = dot(keys_turned, d_scores, NN) * SCALE
            inner = jnp.sum(d_turned * query.astype(F32).T, axis=0, keepdims=True)
            if h == 0:
                sums[0:1, here] = inner
            else:
                sums[0:1, here] += inner
            d_query[here, cols] = unturn(d_turned.T, here)
        d_value[:, cols] = value_sum[...].astype(BF)
        for i in range(4):
            here = slice(i * rows, (i + 1) * rows)
            d_rot = key_sum[here, :] * SCALE
            inner = d_rot * qkv[here, 256 + h * 128 : 384 + h * 128].astype(F32)
            inner = jnp.sum(inner.T, axis=0, keepdims=True)
            if h == 0:
                sums[1:2, here] = inner
            else:
                sums[1:2, here] += inner
            d_key[here, cols] = unturn(d_rot, here)


def attend_back(qkv, d_mine, d_rest, heads_mine, heads_rest, bias, lse, cosine, sine, place):
    return call(
        attend_back_kernel,
        (1,),
        [whole(1024, 1280)]
        + [whole(512, 256)] * 4
        + [whole(1, 1024), whole(2, 1024), whole(1024, 128), whole(1024, 128)],
        [whole(1024, 256), whole(1024, 256), whole(1024, 256), whole(2, 1024)],
        [
            shape(1024, 256, dtype=F32),
            shape(1024, 256, dtype=F32),
            shape(1024, 256),
            shape(2, 1024, dtype=F32),
        ],
        scratch=[pltpu.VMEM((1024, 128), F32), pltpu.VMEM((1024, 128), F32)],
        vmem=BIG,
    )(place, qkv, d_mine, d_rest, heads_mine, heads_rest, bias, lse, cosine, sine)


def raw_back_kernel(
    place, d_query, d_key, d_value, query_hat, key_hat, sums, inv_rows, gains, mine, rest, gain_parts
):
    step = pl.program_id(0)

    @pl.when(step == 0)
    def _():
        gain_parts[...] = jnp.zeros_like(gain_parts)

    mean, inv = columns_of(sums[...]), columns_of(inv_rows[...])
    parts = []
    for i, (grad, hat) in enumerate(((d_query, query_hat), (d_key, key_hat))):
        normed = hat[...].astype(F32)
        scaled = grad[...] * gains[i : i + 1, :]
        parts.append((inv[:, i : i + 1] * (scaled - normed * mean[:, i : i + 1])).astype(BF))
        gain_parts[i : i + 1, :] += jnp.sum(grad[...] * normed, axis=0, keepdims=True)
    total = jnp.concatenate(parts + [d_value[...]], 1)

    @pl.when(step < 2)
    def _():
        mine[...] = total

    @pl.when(step >= 2)
    def _():
        rest[...] = total


def raw_back(d_query, d_key, d_value, qkv, sums, inv_rows, gains, place):
    step = 256
    spec = lambda width, column=0: pl.BlockSpec((step, width), lambda i, p: (i, column))
    line = lambda: pl.BlockSpec((2, step), lambda i, p: (0, i))
    return call(
        raw_back_kernel,
        (4,),
        [
            spec(256),
            spec(256),
            spec(256),
            spec(256, 3),
            spec(256, 4),
            line(),
            line(),
            whole(2, 256),
        ],
        [
            pl.BlockSpec((step, 768), lambda i, p: (jnp.minimum(i, 1), 0)),
            pl.BlockSpec((step, 768), lambda i, p: (jnp.maximum(i - 2, 0), 0)),
            whole(2, 256),
        ],
        [shape(512, 768), shape(512, 768), shape(2, 256, dtype=F32)],
    )(place, d_query, d_key, d_value, qkv, qkv, sums, inv_rows, gains)


def back_kernel(place, *refs):
    rows_mine, rows_rest, d_mine, d_rest, raw_mine, raw_rest, raw_got = refs[:7]
    heads_mine, heads_rest, own_q, own_k, own_v, near, far, low, inv, gain_mlp, moe = refs[7:18]
    pieces, terms = refs[18:22], refs[22:26]
    mine, rest, total, d_own, d_other = refs[26:]
    i = pl.program_id(0)

    @pl.when(i == 0)
    def _():
        for r in range(4):
            mine[r * 128 : r * 128 + 128, :] = heads_mine[line_rows(place, r), :]
            rest[r * 128 : r * 128 + 128, :] = heads_rest[line_rows(place, r), :]
        d_own[...] = pick(place[2], raw_mine[...], raw_got[...])
        d_other[...] = pick(place[2], raw_got[...], raw_mine[...])

    qkv = dot(rows_mine[...], raw_mine[...], TN) + dot(rows_rest[...], raw_rest[...], TN)
    back = dot(d_mine[...], mine[...], TN) + dot(d_rest[...], rest[...], TN)
    grads = jnp.concatenate([qkv.astype(BF), back.astype(BF)], 1)
    for j, piece in enumerate(pieces):

        @pl.when(i // 2 == j)
        def _(piece=piece):
            piece[pl.ds(pl.multiple_of(lax.rem(i, 2) * 256, 256), 256), :] = grads

    other = jnp.where(i // 4 == place[1], near[...], far[...])
    own = jnp.concatenate([own_q[...], own_k[...], own_v[...]], 1)
    part = dot(d_own[...], own, NT) + dot(d_other[...], other, NT)
    total[...] = part
    gain = jnp.sum(part * (low[...].astype(F32) * inv[...]), axis=0, keepdims=True)
    zeros = jnp.zeros((14, gain.shape[1]), F32)
    gains = jnp.concatenate([gain, gain_mlp[...], zeros], 0).astype(BF)
    for r, out in enumerate(terms):
        out[0:128, :] = total[line_rows(place, r), :].astype(BF)
        out[128:144, :] = gains
    terms[2][144:272, :] = moe[...]


def back(
    rows_mine, rows_rest, d_mine, d_rest, raw_mine, raw_rest, raw_got, heads,
    own, near, far, low, inv, gain_mlp, moe, place,
):
    rows, width, step = 512, low.shape[1], 256
    block = lambda: pl.BlockSpec(
        (rows, step), lambda i, p: (0, lax.rem(p[3] + i // 2, 4) * 2 + lax.rem(i, 2))
    )
    half = lambda: pl.BlockSpec((step, 768), lambda i, p: (lax.rem(i, 4), 0))
    tile = lambda: pl.BlockSpec((step, 256), lambda i, p: (i, 0))
    column = lambda n: pl.BlockSpec((n, step), lambda i, p: (0, i))
    return call(
        back_kernel,
        (width // step,),
        [block(), block(), block(), block()]
        + [whole(rows, 768)] * 3
        + [whole(rows, 256)] * 2
        + [tile(), tile(), tile(), half(), half(), column(rows), whole(rows, 1), column(1), column(128)],
        [whole(512, 1024)] * 4 + [column(n) for n in (144, 144, 272, 144)],
        [shape(512, 1024)] * 4 + [shape(n, width) for n in (144, 144, 272, 144)],
        scratch=[
            pltpu.VMEM((rows, 256), BF),
            pltpu.VMEM((rows, 256), BF),
            pltpu.VMEM((rows, step), F32),
            pltpu.VMEM((rows, 768), BF),
            pltpu.VMEM((rows, 768), BF),
        ],
    )(
        place, rows_mine, rows_rest, d_mine, d_rest, raw_mine, raw_rest, raw_got, *heads,
        *own, near, far, low, inv, gain_mlp, moe,
    )


def last_rows_kernel(place, *refs):
    d_terms, moe_terms = refs[:4], refs[4:7]
    d_middle, middle, low, inv, gain = refs[7:12]
    parts, gains, rows = refs[-3:]
    total = sum((t[0:144].astype(F32) for t in d_terms[1:]), d_terms[0][...].astype(F32))
    gains[...] = total[128:130]
    d_in = total[:128]
    hat = low[...].astype(F32) * inv[...]
    scaled = d_in * gain[...]
    mean = jnp.mean(scaled * hat, axis=1, keepdims=True)
    rows[1] = (d_middle[...] + inv[...] * (scaled - hat * mean)).astype(BF)
    moe = sum((t[...].astype(F32) for t in moe_terms), d_terms[2][144:272].astype(F32))
    rows[0] = (middle[...] + moe).astype(BF)
    for i in range(8):
        parts[i] = rows[:, :, i * 256 : i * 256 + 256]


def last_rows(d_terms, moe_terms, d_middle, middle, low, inv, gain, awaited, place):
    width = low.shape[1]
    mine = lambda n: pl.BlockSpec((128, n), lambda i, p: (p[0], 0))
    return call(
        last_rows_kernel,
        (1,),
        [whole(n, width) for n in (144, 144, 272, 144)]
        + [whole(128, width)] * 5
        + [mine(width), mine(1), whole(1, width)]
        + [ANYWHERE] * len(awaited),
        [whole(8, 2, 128, 256), whole(2, width)],
        [shape(8, 2, 128, 256), shape(2, width, dtype=F32)],
        scratch=[pltpu.VMEM((2, 128, width), BF)],
        vmem=BIG,
    )(place, *d_terms, *moe_terms, d_middle, middle, low, inv, gain, *awaited)


def settle_attention_kernel(place, *refs):
    here, there = refs[:4], refs[4:8]
    query, key, value, back, small = refs[9:]
    i = pl.program_id(0)

    @pl.when(i == 0)
    def _():
        small[...] = jnp.zeros_like(small)

    def one(mine, rest):
        mine, rest = mine[0].astype(F32), rest[0].astype(F32)
        first = pick(place[1], rest[:128], mine[:128])
        second = pick(place[1], mine[:128], rest[:128])
        total = jnp.concatenate([first, second], 0)
        query[...] = total[:, :256]
        key[...] = total[:, 256:512]
        value[...] = total[:, 512:768]
        back[...] = total[:, 768:].T
        mine, rest = mine[128:], rest[128:]
        row = lax.broadcasted_iota(jnp.int32, mine.shape, 0)
        small[...] += jnp.where(row < 4, mine + rest, pick(place[2], mine, rest))

    for r in range(4):

        @pl.when(lax.rem(i // 2 + 4 - place[3], 4) == r)
        def _(r=r):
            one(here[r], there[r])


def settle_attention(here, there, awaited, place):
    piece = lambda: pl.BlockSpec((1, 144, 1024), lambda i, p: (lax.rem(i + p[4], 2), 0, 0))
    rows = lambda: pl.BlockSpec((256, 256), lambda i, p: (i, 0))
    return call(
        settle_attention_kernel,
        (8,),
        [piece() for _ in range(8)] + [ANYWHERE],
        [rows(), rows(), rows(), pl.BlockSpec((256, 256), lambda i, p: (0, i)), whole(16, 1024)],
        [shape(2048, 256, dtype=F32)] * 3
        + [shape(256, 2048, dtype=F32), shape(16, 1024, dtype=F32)],
    )(place, *here, *there, awaited)


def settle_experts_kernel(place, gu_mine, gu_got, down_mine, down_got, gate, up, down):
    total = pick(place[2], gu_mine[0], gu_got[0]).astype(F32)
    for j in range(2):
        gate[j] = total[:, j * 256 : j * 256 + 128]
        up[j] = total[:, j * 256 + 128 : j * 256 + 256]
    total = pick(place[2], down_mine[0], down_got[0]).astype(F32)
    down[...] = total.reshape(down.shape)


def settle_experts(gu_mine, gu_got, down_mine, down_got, place):
    def step(i, p, mine):
        return jnp.where(p[2] == mine, i, 0)

    def tall(mine):
        def index(i, p):
            j = step(i, p, mine)
            return (j // 4, lax.rem(j, 4), 0)

        return pl.BlockSpec((1, 512, 512), index)

    def flat(mine):
        def index(i, p):
            j = step(i, p, mine)
            return (j // 4, 0, lax.rem(j, 4))

        return pl.BlockSpec((1, 256, 512), index)

    thin = lambda: pl.BlockSpec((2, 512, 128), lambda i, p: (i // 4, lax.rem(i, 4), 0))
    return call(
        settle_experts_kernel,
        (8,),
        [tall(1), tall(0), flat(1), flat(0)],
        [thin(), thin(), pl.BlockSpec((2, 128, 512), lambda i, p: (i // 4, 0, lax.rem(i, 4)))],
        [shape(4, 2048, 128, dtype=F32)] * 2 + [shape(4, 128, 2048, dtype=F32)],
        flops=20_000_000_000,
    )(place, gu_mine, gu_got, down_mine, down_got)


def choice_weights(ids, gates, experts, capacity):
    named = ids[:, :, None] == jnp.arange(experts, dtype=jnp.int32)
    count = jnp.sum(named.astype(F32), axis=1)
    tokens = ids.shape[0]
    earlier = (
        jnp.arange(tokens, dtype=jnp.int32)[:, None] > jnp.arange(tokens, dtype=jnp.int32)[None, :]
    ).astype(BF)
    place = jnp.dot(earlier, count.astype(BF), preferred_element_type=F32)
    weight = jnp.sum(jnp.where(named, gates[:, :, None], 0.0), axis=1)
    return jnp.where(place < capacity, weight, 0.0)


def local(
    hidden_in,
    cotangent,
    sequence_order,
    seq_lengths,
    expert_ids,
    gate_weights,
    w_query,
    w_key,
    w_value,
    w_output,
    gain_attn,
    gain_query,
    gain_key,
    gain_mlp,
    w_gate,
    w_up,
    w_down,
):
    zl, y, c, zh, x = (lax.axis_index(a) for a in AXES)
    same = c == zh
    length = hidden_in.shape[1]
    half = length // 2
    experts = w_gate.shape[0]
    width = w_query.shape[0]
    place = jnp.stack([x, c, same.astype(jnp.int32), y, zl, zh]).astype(jnp.int32)
    sequence = (zl * SIZES[1] + y) * 2 + zh
    tokens_here = seq_lengths[sequence]
    ids_here = expert_ids[sequence]
    gates_here = gate_weights[sequence]

    x_dealt = deal_in(hidden_in[0], zh)
    qkv_own = [w_query, w_key, w_value]
    qkv_near = other_half(qkv_own, c, x_dealt)
    x_pieces = gather_x(x_dealt)
    cot_dealt = deal_in(cotangent[0], zh, x_pieces[1])
    gains_own = jnp.stack([gain_query, gain_key], 0)
    gains_other = other_half_chip(gains_own)

    cosine_np, sine_np = rope_tables(length)
    swap_halves = lambda t: lax.dynamic_slice_in_dim(
        jnp.concatenate([t, t], 0), c * half, length, 0
    )
    cosine_all, sine_all = swap_halves(jnp.asarray(cosine_np)), swap_halves(jnp.asarray(sine_np))
    positions = (jnp.arange(length, dtype=jnp.int32) + c * half) % length
    bias = jnp.where(positions < tokens_here, 0.0, -1e30).astype(F32)
    weight_all = choice_weights(ids_here, gates_here, experts, length * 2 // experts)
    weight_here = lax.dynamic_slice_in_dim(weight_all, c * half, half, 0)
    weight_here = lax.dynamic_slice_in_dim(
        jnp.concatenate([weight_here, weight_here], 0), x * (half // 4), half, 0
    )

    x_low, attn_in, inv_one = norm_rows(x_pieces, place, gain_attn[None, :])
    qkv_near, cot_first = tie([qkv_near, cot_dealt], attn_in)
    qkv_far = other_core(qkv_near)
    out_near = other_half([w_output], c, attn_in)
    raw_send, raw_keep, squares = project(attn_in, qkv_own, qkv_near, qkv_far, out_near, place)
    (gains_other,) = tie([gains_other], squares)
    gains_keep = jnp.where(same, gains_own, gains_other)
    gains_qk = jnp.concatenate([gains_keep, jnp.where(same, gains_other, gains_own)], 0)
    inv_qk = lax.rsqrt(sum_x(squares[:2]) / width + EPS)
    (out_near,) = tie([out_near], inv_qk)
    down_near = other_half([w_down], c, out_near)
    gu_near = other_half([w_gate, w_up], c, out_near)
    cot_pieces = gather_x(cot_first, inv_qk)
    ready_send, ready_keep = prep(
        raw_send,
        raw_keep,
        inv_qk,
        gains_qk,
        cosine_all[:half],
        sine_all[:half],
        (cot_pieces[1], cot_pieces[4]),
        place,
    )
    ready_rest = other_core(ready_send)
    qkv, heads_mine, heads_rest, lse = attend(ready_keep, ready_rest, bias[None, :], place)
    heads_got = other_core(heads_rest)
    out_near, inv_tied = tie([out_near, inv_qk], heads_got)
    out_far = other_core(out_near)
    inv_qk_rest = other_core(inv_tied)
    cot = place_rows(cot_pieces, place)
    attn_terms = send_x(
        heads_to_rows(heads_mine, heads_got, w_output, out_near, out_far, (cot, heads_got), place)
    )
    attn_in, cot = tie([attn_in, cot], heads_got)
    attn_in_rest = other_core(attn_in)
    cot_rest = other_core(cot)

    middle, moe_own, inv_two = middle_rows(attn_terms, x_low, gain_mlp[None, :], place)
    moe_pieces = gather_x(moe_own)
    gu_near, down_near = tie([gu_near, down_near], moe_pieces[1])
    gu_near, down_near = tie([gu_near, down_near], moe_pieces[4])
    down_far = other_core(down_near)
    cot_down = cot_back(cot, w_down, down_near, down_far, place)
    gu_far = other_core(gu_near)
    hidden_send, hidden_keep, moe_in, *d_moe_terms = expert_layer(
        moe_pieces, cot_down, weight_here, w_gate, w_up, gu_near, gu_far, place
    )
    d_moe_terms = send_x(d_moe_terms)
    moe_terms = expert_out(
        hidden_send, hidden_keep, w_down, down_near, down_far, hidden_keep, place
    )
    hidden_all = jnp.concatenate([hidden_keep, other_core(hidden_send)], 1)
    moe_all = jnp.concatenate([moe_in, other_core(moe_in)], 0)
    cot_all = jnp.concatenate([cot, cot_rest], 0)
    grad_gate_up = jnp.einsum(
        "td,etf->edf", moe_all, hidden_all[:, :, :512], preferred_element_type=F32
    ).astype(BF)
    grad_down = jnp.einsum(
        "etf,td->efd", hidden_all[:, :, 512:], cot_all, preferred_element_type=F32
    ).astype(BF)

    d_middle, d_own, gain_mlp_part = middle_back(
        d_moe_terms,
        middle,
        inv_two,
        gain_mlp[None, :],
        cot,
        (grad_gate_up, grad_down, moe_terms[0]),
        place,
    )
    grad_gate_up, grad_down = lax.psum((grad_gate_up, grad_down), GROUPS)
    d_pieces = gather_x(d_own)
    d_heads_keep, d_heads_send, d_attn = rows_to_heads(
        d_pieces, w_output, out_near, out_far, place
    )
    d_heads_rest = other_core(d_heads_send)
    *moe_terms, d_attn = tie(list(moe_terms) + [d_attn], d_heads_rest)
    moe_after, moe_before = along(moe_terms[1], "x", 1), along(moe_terms[3], "x", -1)
    d_attn_rest = other_core(d_attn)
    d_query, d_key, d_value, sums = attend_back(
        qkv,
        d_heads_keep,
        d_heads_rest,
        heads_mine,
        heads_rest,
        bias[None, :],
        lse,
        cosine_all,
        sine_all,
        place,
    )
    (sums,) = tie([sums], moe_after)
    (sums,) = tie([sums], moe_before)
    sums_rest = other_core(sums)
    sums = sums + jnp.concatenate([sums_rest[:, half:], sums_rest[:, :half]], 1)
    sums = sum_x(sums) / width
    raw_mine, raw_rest, gain_qk_parts = raw_back(
        d_query,
        d_key,
        d_value,
        qkv,
        sums,
        jnp.concatenate([inv_qk, inv_qk_rest], 1),
        gains_keep,
        place,
    )
    raw_got = other_core(raw_rest)
    pieces = back(
        attn_in,
        attn_in_rest,
        d_attn,
        d_attn_rest,
        raw_mine,
        raw_rest,
        raw_got,
        (heads_mine, heads_rest),
        qkv_own,
        qkv_near,
        qkv_far,
        x_low,
        inv_one,
        gain_mlp_part,
        moe_terms[2],
        place,
    )
    weight_terms = send_y(pieces[:4])
    d_in_terms = send_x(pieces[4:])
    moe_terms = [moe_terms[0], moe_after, moe_before]
    rows_dealt, gains = last_rows(
        d_in_terms,
        moe_terms,
        d_middle,
        middle,
        x_low,
        inv_one,
        gain_attn[None, :],
        weight_terms[1:],
        place,
    )
    dealt = deal_line(rows_dealt)
    grad_gate_up, grad_down = tie([grad_gate_up, grad_down], rows_dealt)
    total = sum((t.astype(F32) for t in weight_terms[1:]), weight_terms[0].astype(F32)).astype(BF)
    near, far = to_shard(total, zl, same)
    total = (near.astype(F32) + far.astype(F32)).astype(BF)
    first = c == 0
    got = other_core(jnp.where(first, total[128:], total[:128]))
    mine = jnp.where(first, total[:128], total[128:]).astype(F32) + got.astype(F32)
    small = jnp.concatenate([gains.reshape(-1), gain_qk_parts.reshape(-1)])
    small = (small + lax.ppermute(small, "zh", [(0, 1), (1, 0)])).reshape(9, 512)
    small = jnp.concatenate([small.reshape(-1), jnp.zeros((11776,), F32)]).reshape(16, 1024)
    (mine,) = tie([jnp.concatenate([mine, small], 0).astype(BF)], dealt)
    here = from_groups(mine)
    (dealt,) = tie([dealt], here[0])
    output, grad_input = deal_out(dealt, same)

    grad_gate, grad_up, grad_down = settle_experts(
        grad_gate_up, settle(grad_gate_up), grad_down, settle(grad_down), place
    )
    here = tie(list(here), grad_down)
    grad_query, grad_key, grad_value, grad_output, small = settle_attention(
        here, [other_core(t) for t in here], grad_down, place
    )
    small = small.reshape(-1)
    return (
        output[None],
        grad_input[None],
        grad_query,
        grad_key,
        grad_value,
        grad_output,
        small[:width],
        small[2 * width : 2 * width + 256],
        small[2 * width + 256 : 2 * width + 512],
        small[width : 2 * width],
        grad_gate,
        grad_up,
        grad_down,
    )


def solution(mesh):
    fine = Mesh(mesh.devices.reshape(SIZES), AXES)
    columns = P(None, TENSOR)
    placed = (
        P(DP, None, TENSOR),
        P(DP, None, TENSOR),
        P(),
        P(),
        P(),
        P(),
        columns,
        columns,
        columns,
        P(TENSOR, None),
        P(),
        P(TENSOR),
        P(TENSOR),
        P(),
        P(None, None, TENSOR),
        P(None, None, TENSOR),
        P(None, TENSOR, None),
    )
    return jax.shard_map(
        local,
        mesh=fine,
        in_specs=placed,
        out_specs=placed[:2]
        + (columns, columns, columns, P(TENSOR, None), P(), P(TENSOR), P(TENSOR), P())
        + placed[14:],
        check_vma=False,
    )
```

```python
import math

import jax
import jax.numpy as jnp
import numpy as np
from jax import lax
from jax.experimental import pallas as pl
from jax.experimental.pallas import tpu as pltpu
from jax.sharding import Mesh
from jax.sharding import PartitionSpec as P

AXES = ("zl", "y", "c", "zh", "x")
SIZES = (2, 4, 2, 2, 4)
DP = ("zl", "y", "c")
TENSOR = ("zh", "x")
GROUPS = ("zl", "y", "zh")

HEAD_DIM = 128
EPS = 1e-06
BASE = 50000.0
BF = jnp.bfloat16
F32 = jnp.float32
SCALE = 1.0 / math.sqrt(HEAD_DIM)
VMEM = 32 * 1024 * 1024
BIG = 56 * 1024 * 1024


def rope_tables(length):
    half = HEAD_DIM // 2
    frequency = np.power(
        np.float32(BASE), np.float32(-2.0) * np.arange(half, dtype=np.float32) / HEAD_DIM
    ).astype(np.float32)
    angles = np.arange(length, dtype=np.float32)[:, None] * frequency[None, :]
    cosine = np.cos(angles.astype(np.float64)).astype(np.float32)
    sine = np.sin(angles.astype(np.float64)).astype(np.float32)
    return np.concatenate([cosine, cosine, -sine, sine], 1)


def along(value, axis, shift):
    size = SIZES[AXES.index(axis)]
    return lax.ppermute(value, axis, [(i, (i + shift) % size) for i in range(size)])


def other_core(value):
    return lax.ppermute(value, "c", [(0, 1), (1, 0)])


def other_half_chip(value):
    return lax.ppermute(value, ("zl", "zh"), [(i, 3 - i) for i in range(4)])


def sum_x(value):
    return value + along(value, "x", 1) + along(value, "x", 2) + along(value, "x", 3)


def gather_x(value, awaited=None):
    half = value.shape[0] // 2
    after, before = along(value, "x", -1), along(value, "x", 1)
    far = [after[:half], before[half:]]
    if awaited is not None:
        far = tie(far, awaited)
    return [value, after, along(far[0], "x", -1), along(far[1], "x", 1), before]


def tie_kernel(*refs):
    del refs


def tie(values, awaited):
    anywhere = pl.BlockSpec(memory_space=pl.ANY)
    count = len(values)
    return pl.pallas_call(
        tie_kernel,
        in_specs=[anywhere] * (count + 1),
        out_specs=[anywhere] * count,
        out_shape=[jax.ShapeDtypeStruct(v.shape, v.dtype) for v in values],
        input_output_aliases={i: i for i in range(count)},
    )(*values, awaited)


def later(start, awaited):
    ends = awaited[(0,) * awaited.ndim].astype(F32) + awaited[(-1,) * awaited.ndim].astype(F32)
    return start + (ends != ends).astype(jnp.int32)


def send_x(pieces):
    return [
        pieces[0],
        along(pieces[1], "x", 1),
        along(pieces[2], "x", 2),
        along(pieces[3], "x", -1),
    ]


def deal_in(value, zh, awaited=None):
    half = value.shape[0] // 2
    got = []
    for k in (0, 1):
        pairs = [(a * 2 + b, (b ^ k) * 2 + a) for a in range(2) for b in range(2)]
        start = (zh ^ k) * half
        if awaited is not None:
            start = later(start, awaited)
        part = lax.dynamic_slice_in_dim(value, start, half, 0)
        got.append(lax.ppermute(part, ("c", "zh"), pairs))
    return jnp.stack(got, 0)


def deal_line(parts):
    return lax.all_to_all(parts, ("c", "x"), 0, 0, tiled=True)


def deal_out(dealt, same):
    got = dealt.transpose(1, 0, 2, 3).reshape(2, 1024, 256)
    moved = lax.ppermute(got, ("c", "zh"), [(1, 2), (2, 1)])
    got = jnp.where(same, got, moved)
    return got[0], got[1]


def other_half(weights, c, awaited):
    half = weights[0].shape[0] // 2
    start = later(c * half, awaited)
    parts = [lax.dynamic_slice_in_dim(w, start, half, 0) for w in weights]
    return other_half_chip(jnp.concatenate(parts, parts[0].ndim - 1))


def send_y(pieces):
    own, after, far, before = pieces
    half = far.shape[0] // 2
    up, down = along(far[:half], "y", 1), along(far[half:], "y", -1)
    add = lambda a, b: (a.astype(F32) + b.astype(F32)).astype(a.dtype)
    after = jnp.concatenate([add(after[:half], up), after[half:]], 0)
    before = jnp.concatenate([before[:half], add(before[half:], down)], 0)
    return [own, along(after, "y", 1), along(before, "y", -1)]


def to_shard(value, zl, same):
    low, high = value[:256], value[256:]
    near = jnp.where(zl == 0, low, high)
    far = jnp.where(zl == 0, high, low)
    order = [(i, k, m) for i in range(2) for k in range(2) for m in range(2)]
    index = lambda i, k, m: (i * 2 + k) * 2 + m
    stay = [(index(i, k, m), index(i, m, k)) for i, k, m in order if k != m]
    flip = [(index(i, k, m), index(1 - i, m, k)) for i, k, m in order]
    axes = ("zl", "c", "zh")
    got = lax.ppermute(near, axes, stay)
    return jnp.where(same, near, got), lax.ppermute(far, axes, flip)


def from_groups(piece):
    pair = jnp.stack([piece, lax.ppermute(piece, "zl", [(0, 1), (1, 0)])], 0)
    return [pair] + [along(pair, "y", -r) for r in (1, 2, 3)]


def settle(value):
    return lax.ppermute(value, ("c", "zh"), [(0, 2), (3, 1)])


def dot(left, right, dims):
    return lax.dot_general(left, right, (dims, ((), ())), preferred_element_type=F32)


NT = ((1,), (1,))
NN = ((1,), (0,))
TN = ((0,), (0,))


def call(kernel, grid, in_specs, out_specs, out_shape, scratch=(), flops=1, vmem=VMEM):
    return pl.pallas_call(
        kernel,
        grid_spec=pltpu.PrefetchScalarGridSpec(
            num_scalar_prefetch=1,
            grid=grid,
            in_specs=in_specs,
            out_specs=out_specs,
            scratch_shapes=scratch,
        ),
        out_shape=out_shape,
        compiler_params=pltpu.CompilerParams(vmem_limit_bytes=vmem),
        cost_estimate=pl.CostEstimate(flops=flops, bytes_accessed=1, transcendentals=0),
    )


def shape(*dims, dtype=BF):
    return jax.ShapeDtypeStruct(dims, dtype)


def whole(*dims):
    return pl.BlockSpec(dims, lambda i, p: (0,) * len(dims))


ANYWHERE = pl.BlockSpec(memory_space=pl.ANY)


def line_rows(place, r, rows=128):
    return pl.ds(pl.multiple_of(lax.rem(place[0] + r, 4) * rows, rows), rows)


def pick(flag, yes, no):
    return jnp.where(flag == 1, yes, no)


def pair_of(i, p):
    return jnp.where(i == 0, p[1], jnp.where(i == 1, 1 - p[1], i - 2))


def send_pair(i, p):
    other = jnp.where(i == 0, p[1], 1 - p[1])
    return jnp.where(p[2] == 1, other, jnp.maximum(i - 2, 0))


def keep_pair(i, p):
    other = jnp.where(i == 0, p[1], 1 - p[1])
    return jnp.where(p[2] == 1, jnp.maximum(i - 2, 0), other)


def role(i, p, first):
    return jnp.where(i < first, 1 - p[2], p[2])


def column_blocks(place, pieces):
    own, after, far_low, far_high, before = pieces
    for r, (first, second) in enumerate(
        ((own, own), (after, after), (far_low, far_high), (before, before))
    ):
        for k, piece in enumerate((first, second)):
            index = lax.rem(place[1] + k, 2) * 4 + lax.rem(place[0] + r, 4)
            yield pl.multiple_of(index * 256, 256), piece[k if r != 2 else 0]


def norm_kernel(place, own, after, far_low, far_high, before, gain, low, normed, inv):
    squares = jnp.zeros((low.shape[0], 1), F32)
    for column, here in column_blocks(place, (own, after, far_low, far_high, before)):
        low[:, pl.ds(column, 256)] = here
        here = here.astype(F32)
        squares += jnp.sum(here * here, axis=1, keepdims=True)
    root = lax.rsqrt(squares / low.shape[1] + EPS)
    inv[...] = root
    normed[...] = (low[...].astype(F32) * root * gain[...]).astype(BF)


def piece_specs(step, rows_of):
    return [pl.BlockSpec((n, step, 256), rows_of) for n in (2, 2, 1, 1, 2)]


def norm_rows(pieces, place, gain):
    rows, step = pieces[0].shape[1], 128
    full = lambda: pl.BlockSpec((step, 2048), lambda i, p: (i, 0))
    return call(
        norm_kernel,
        (rows // step,),
        piece_specs(step, lambda i, p: (0, i, 0)) + [whole(1, 2048)],
        [full(), full(), pl.BlockSpec((step, 1), lambda i, p: (i, 0))],
        [shape(rows, 2048), shape(rows, 2048), shape(rows, 1, dtype=F32)],
    )(place, *pieces, gain)


def place_kernel(place, own, after, far_low, far_high, before, low):
    for column, here in column_blocks(place, (own, after, far_low, far_high, before)):
        low[:, pl.ds(column, 256)] = here


def place_rows(pieces, place):
    rows = pieces[0].shape[1]
    step = rows // 4
    return call(
        place_kernel,
        (4,),
        piece_specs(step, lambda i, p: (0, lax.rem(i + p[0], 4), 0)),
        pl.BlockSpec((step, 2048), lambda i, p: (i, 0)),
        shape(rows, 2048),
    )(place, *pieces)


def project_kernel(place, rows_in, *refs):
    *own, near, far, awaited, send, keep, squares, columns = refs
    i = pl.program_id(0)
    lane = lax.broadcasted_iota(jnp.int32, columns.shape, 1)

    @pl.when(i == 0)
    def _():
        columns[...] = jnp.zeros_like(columns)

    def finish(raw):
        kept = role(i, place, 3)

        @pl.when(kept == 1)
        def _():
            keep[...] = raw

        @pl.when(kept == 0)
        def _():
            send[...] = raw

        total = jnp.sum(raw * raw, axis=1, keepdims=True)
        columns[...] += jnp.where(lane == lax.rem(i, 3), total, 0.0)

    @pl.when(i < 3)
    def _():
        half = near.shape[0]
        here = pl.ds(pl.multiple_of(place[1] * half, half), half)
        there = pl.ds(pl.multiple_of((1 - place[1]) * half, half), half)
        finish(dot(rows_in[:, here], near[...], NN) + dot(rows_in[:, there], far[...], NN))

    for j, weight in enumerate(own):

        @pl.when(i == 3 + j)
        def _(weight=weight):
            finish(dot(rows_in[...], weight[...], NN))

    @pl.when(i == 5)
    def _():
        squares[...] = columns[...].T


def project(rows_in, own, near, far, awaited, place):
    rows, width = rows_in.shape
    other = lambda i: jnp.minimum(i, 2)
    mine = lambda i: jnp.maximum(i - 3, 0)
    return call(
        project_kernel,
        (6,),
        [
            whole(rows, width),
            whole(width, 256),
            whole(width, 256),
            whole(width, 256),
            pl.BlockSpec((width // 2, 256), lambda i, p: (0, other(i))),
            pl.BlockSpec((width // 2, 256), lambda i, p: (0, other(i))),
            ANYWHERE,
        ],
        [
            pl.BlockSpec((rows, 256), lambda i, p: (0, jnp.where(p[2] == 1, other(i), mine(i)))),
            pl.BlockSpec((rows, 256), lambda i, p: (0, jnp.where(p[2] == 1, mine(i), other(i)))),
            whole(8, rows),
        ],
        [shape(rows, 768, dtype=F32), shape(rows, 768, dtype=F32), shape(8, rows, dtype=F32)],
        scratch=[pltpu.VMEM((rows, 8), F32)],
    )(place, rows_in, *own, near, far, awaited)


def columns_of(rows_two):
    rest = jnp.zeros((6, rows_two.shape[1]), F32)
    return jnp.concatenate([rows_two, rest], 0).T


def prep_kernel(place, raw_send, raw_keep, inv_rows, gains, table, first, second, out_send, out_keep):
    cosine, sine = table[:, :128], table[:, 128:]
    inv = columns_of(inv_rows[...])
    for part, (raw, out) in enumerate(((raw_keep, out_keep), (raw_send, out_send))):
        for i in range(2):
            for h in range(2):
                lo = i * 256 + h * 128
                normed = raw[:, lo : lo + 128] * inv[:, i : i + 1]
                out[:, 768 + lo : 896 + lo] = normed.astype(BF)
                normed = normed * gains[part * 2 + i : part * 2 + i + 1, h * 128 : h * 128 + 128]
                out[:, lo : lo + 128] = (
                    normed * cosine + pltpu.roll(normed, 64, 1) * sine
                ).astype(BF)
        out[:, 512:768] = raw[:, 512:768].astype(BF)


def prep(raw_send, raw_keep, inv_rows, gains, table, awaited, place):
    rows, step = raw_send.shape[0], 128
    spec = lambda width: pl.BlockSpec((step, width), lambda i, p: (i, 0))
    return call(
        prep_kernel,
        (rows // step,),
        [
            spec(768),
            spec(768),
            pl.BlockSpec((2, step), lambda i, p: (0, i)),
            whole(4, 256),
            pl.BlockSpec((step, 256), lambda i, p: (p[1] * 4 + i, 0)),
            ANYWHERE,
            ANYWHERE,
        ],
        [spec(1280), spec(1280)],
        [shape(rows, 1280), shape(rows, 1280)],
    )(place, raw_send, raw_keep, inv_rows, gains, table, *awaited)


def attend_kernel(place, mine, rest, bias, qkv, out_mine, out_rest, lse):
    rows = 256
    qkv[0:512, :] = mine[...]
    qkv[512:1024, :] = rest[...]
    for h in range(2):
        cols = slice(h * 128, h * 128 + 128)
        keys = qkv[:, 256 + h * 128 : 384 + h * 128]
        values = qkv[:, 512 + h * 128 : 640 + h * 128]
        for i in range(4):
            here = slice(i * rows, (i + 1) * rows)
            scores = dot(qkv[here, cols], keys, NT) * SCALE + bias[...]
            top = jnp.max(scores, axis=1, keepdims=True)
            weight = jnp.exp(scores - top)
            total = jnp.sum(weight, axis=1, keepdims=True)
            out = out_mine if i < 2 else out_rest
            out[i % 2 * rows : i % 2 * rows + rows, cols] = (
                dot(weight.astype(BF), values, NN) / total
            ).astype(BF)
            wide = jnp.broadcast_to(top + jnp.log(total), (rows, 8))
            lse[h : h + 1, here] = wide.T[0:1, :]


def attend(mine, rest, bias, place):
    return call(
        attend_kernel,
        (1,),
        [whole(512, 1280), whole(512, 1280), whole(1, 1024)],
        [whole(1024, 1280), whole(512, 256), whole(512, 256), whole(2, 1024)],
        [shape(1024, 1280), shape(512, 256), shape(512, 256), shape(2, 1024, dtype=F32)],
    )(place, mine, rest, bias)


def fill_other(place, near, far, other):
    half = near.shape[0]
    other[pl.ds(pl.multiple_of(place[1] * half, half), half), :] = near[...]
    other[pl.ds(pl.multiple_of((1 - place[1]) * half, half), half), :] = far[...]


def heads_to_rows_kernel(place, keep, send, own, near, far, first, second, a, b, c, d, other):
    fill_other(place, near, far, other)
    for r, out in enumerate((a, b, c, d)):
        here = line_rows(place, r)
        left, right = keep[here, :], send[here, :]
        part = dot(pick(place[2], left, right), own[...], NN)
        part += dot(pick(place[2], right, left), other[...], NN)
        out[...] = part.astype(BF)


def heads_to_rows(heads, rest, own, near, far, awaited, place):
    width = own.shape[1]
    step = width // 2
    tile = lambda n: pl.BlockSpec((n, step), lambda i, p: (0, i))
    return call(
        heads_to_rows_kernel,
        (2,),
        [whole(512, 256), whole(512, 256), tile(256), tile(128), tile(128), ANYWHERE, ANYWHERE],
        [tile(128)] * 4,
        [shape(128, width)] * 4,
        scratch=[pltpu.VMEM((256, step), BF)],
    )(place, heads, rest, own, near, far, *awaited)


def fill(rows, pieces):
    start = 0
    for piece in pieces:
        rows[start : start + piece.shape[0], :] = piece[...]
        start += piece.shape[0]


def rows_to_heads_kernel(
    place, own_rows, after, far_low, far_high, before, own, near, far,
    keep, send, rows, other,
):
    fill(rows, (own_rows, after, far_low, far_high, before))
    fill_other(place, near, far, other)
    mine = dot(rows[...], own[...], NT).astype(BF)
    rest = dot(rows[...], other[...], NT).astype(BF)
    for out, part in ((send, pick(place[2], rest, mine)), (keep, pick(place[2], mine, rest))):
        for r in range(4):
            out[line_rows(place, r), :] = part[r * 128 : r * 128 + 128]


def rows_to_heads(pieces, own, near, far, place):
    width = own.shape[1]
    return call(
        rows_to_heads_kernel,
        (1,),
        [whole(n, width) for n in (128, 128, 64, 64, 128, 256, 128, 128)],
        [whole(512, 256), whole(512, 256), whole(512, width)],
        [shape(512, 256), shape(512, 256), shape(512, width)],
        scratch=[pltpu.VMEM((256, width), BF)],
        vmem=BIG,
    )(place, *pieces, own, near, far)


def middle_kernel(place, a, b, c, d, low, gain, middle, normed, inv):
    total = sum((t[...].astype(F32) for t in (b, c, d)), a[...].astype(F32))
    total = low[...].astype(F32) + total
    middle[...] = total
    root = lax.rsqrt(jnp.mean(total * total, axis=1, keepdims=True) + EPS)
    inv[...] = root
    normed[...] = (total * root * gain[...]).astype(BF)


def middle_rows(terms, low, gain, place):
    width = low.shape[1]
    return call(
        middle_kernel,
        (1,),
        [whole(128, width)] * 4
        + [pl.BlockSpec((128, width), lambda i, p: (p[0], 0)), whole(1, width)],
        [whole(128, width), whole(128, width), whole(128, 1)],
        [shape(128, width, dtype=F32), shape(128, width), shape(128, 1, dtype=F32)],
    )(place, *terms, low, gain)


def middle_back_kernel(
    place, a, b, c, d, middle, inv, gain, cot, ready_a, ready_b, ready_c, d_middle, d_low, gain_part
):
    d_in = sum((t[...].astype(F32) for t in (b, c, d)), a[...].astype(F32))
    hat = middle[...] * inv[...]
    gain_part[...] = jnp.sum(d_in * hat, axis=0, keepdims=True)
    scaled = d_in * gain[...]
    mean = jnp.mean(scaled * hat, axis=1, keepdims=True)
    total = cot[...].astype(F32) + inv[...] * (scaled - hat * mean)
    d_middle[...] = total
    d_low[...] = total.astype(BF)


def middle_back(terms, middle, inv, gain, cot, ready, place):
    width = middle.shape[1]
    return call(
        middle_back_kernel,
        (1,),
        [whole(128, width)] * 5
        + [whole(128, 1), whole(1, width), whole(128, width)]
        + [ANYWHERE] * 3,
        [whole(128, width), whole(128, width), whole(1, width)],
        [shape(128, width, dtype=F32), shape(128, width), shape(1, width, dtype=F32)],
        vmem=BIG,
    )(place, *terms, middle, inv, gain, cot, *ready)


def cot_back_kernel(place, cot, own, near, far, out):
    def one(down):
        out[0] = dot(cot[...], down, NT)

    i = pl.program_id(0)
    pl.when(i == 0)(lambda: one(near[...].reshape(256, near.shape[2])))
    pl.when(i == 1)(lambda: one(far[...].reshape(256, far.shape[2])))
    pl.when(i >= 2)(lambda: one(own[...].reshape(256, own.shape[2])))


def own_pair(i, p):
    return (jnp.maximum(i - 2, 0), 0, 0)


def cot_back(cot, own, near, far, place):
    rows, width = cot.shape
    return call(
        cot_back_kernel,
        (4,),
        [
            whole(rows, width),
            pl.BlockSpec((2, 128, width), own_pair),
            whole(2, 128, width),
            whole(2, 128, width),
        ],
        pl.BlockSpec((1, rows, 256), lambda i, p: (i, 0, 0)),
        shape(4, rows, 256, dtype=F32),
        flops=5_000_000_000,
    )(place, cot, own, near, far)


def expert_kernel(
    place, own_rows, after, far_low, far_high, before, back, weights, own_gate, own_up, near, far,
    send, keep, rows, a, b, c, d, total, both_weights,
):
    i = pl.program_id(0)

    @pl.when(i == 0)
    def _():
        fill(rows, (own_rows, after, far_low, far_high, before))

    def two(gate, gate_start, up, up_start):
        for j in range(2):
            both_weights[:, j * 256 : j * 256 + 128] = gate[j, :, gate_start : gate_start + 128]
            both_weights[:, j * 256 + 128 : j * 256 + 256] = up[j, :, up_start : up_start + 128]
        lane = lax.broadcasted_iota(jnp.int32, weights.shape, 1)
        pre = dot(rows[...], both_weights[...], NN)
        grads, acts = [], []
        for j in range(2):
            named = lane == pair_of(i, place) * 2 + j
            weight = jnp.sum(jnp.where(named, weights[...], 0.0), axis=1, keepdims=True)
            gate = pre[:, j * 256 : j * 256 + 128]
            up = pre[:, j * 256 + 128 : j * 256 + 256]
            sig = 1.0 / (1.0 + jnp.exp(-gate))
            silu = gate * sig
            d_act = weight * back[0, :, j * 128 : j * 128 + 128]
            acts.append((weight * (silu * up)).astype(BF))
            grads.append((d_act * up * sig * (1.0 + gate * (1.0 - sig))).astype(BF))
            grads.append((d_act * silu).astype(BF))
        both = jnp.concatenate(grads, 1)
        hidden = jnp.concatenate([both] + acts, 1)
        kept = role(i, place, 2)

        @pl.when(kept == 1)
        def _():
            keep[0] = hidden

        @pl.when(kept == 0)
        def _():
            send[0] = hidden

        part = dot(both, both_weights[...], NT)

        @pl.when(i == 0)
        def _():
            total[...] = part

        @pl.when(i > 0)
        def _():
            total[...] += part

    pl.when(i == 0)(lambda: two(near, 0, near, 128))
    pl.when(i == 1)(lambda: two(far, 0, far, 128))
    pl.when(i >= 2)(lambda: two(own_gate, 0, own_up, 0))

    @pl.when(i == 3)
    def _():
        for r, out in enumerate((a, b, c, d)):
            out[...] = total[r * 128 : r * 128 + 128, :].astype(BF)


def expert_layer(pieces, back, weights, own_gate, own_up, near, far, place):
    rows, width = 512, pieces[0].shape[1]
    return call(
        expert_kernel,
        (4,),
        [whole(n, width) for n in (128, 128, 64, 64, 128)]
        + [
            pl.BlockSpec((1, rows, 256), lambda i, p: (i, 0, 0)),
            whole(rows, 4),
            pl.BlockSpec((2, width, 128), own_pair),
            pl.BlockSpec((2, width, 128), own_pair),
            whole(2, width, 256),
            whole(2, width, 256),
        ],
        [
            pl.BlockSpec((1, rows, 768), lambda i, p: (send_pair(i, p), 0, 0)),
            pl.BlockSpec((1, rows, 768), lambda i, p: (keep_pair(i, p), 0, 0)),
            whole(rows, width),
        ]
        + [whole(128, width)] * 4,
        [shape(2, rows, 768), shape(2, rows, 768), shape(rows, width)] + [shape(128, width)] * 4,
        scratch=[pltpu.VMEM((rows, width), F32), pltpu.VMEM((width, 512), BF)],
        vmem=44 * 1024 * 1024,
    )(place, *pieces, back, weights, own_gate, own_up, near, far)


def expert_out_kernel(place, send, keep, own, near, far, awaited, a, b, c, d, total):
    i = pl.program_id(0)

    def one(down):
        acts = pick(role(i, place, 2), keep[0], send[0])
        part = dot(acts, down, NN)

        @pl.when(i == 0)
        def _():
            total[...] = part

        @pl.when(i > 0)
        def _():
            total[...] += part

    pl.when(i == 0)(lambda: one(near[...].reshape(256, near.shape[2])))
    pl.when(i == 1)(lambda: one(far[...].reshape(256, far.shape[2])))
    pl.when(i >= 2)(lambda: one(own[...].reshape(256, own.shape[2])))

    @pl.when(i == 3)
    def _():
        for r, out in enumerate((a, b, c, d)):
            out[...] = total[r * 128 : r * 128 + 128, :].astype(BF)


def expert_out(send, keep, own, near, far, awaited, place):
    rows, width = 512, own.shape[2]
    return call(
        expert_out_kernel,
        (4,),
        [
            pl.BlockSpec((1, rows, 256), lambda i, p: (send_pair(i, p), 0, 2)),
            pl.BlockSpec((1, rows, 256), lambda i, p: (keep_pair(i, p), 0, 2)),
            pl.BlockSpec((2, 128, width), own_pair),
            whole(2, 128, width),
            whole(2, 128, width),
            ANYWHERE,
        ],
        [whole(128, width)] * 4,
        [shape(128, width)] * 4,
        scratch=[pltpu.VMEM((rows, width), F32)],
        flops=5_000_000_000,
    )(place, send, keep, own, near, far, awaited)


def attend_back_kernel(
    place, qkv, d_mine, d_rest, heads_mine, heads_rest, bias, lse, table_mine, table_rest,
    d_query, d_key, d_value, sums, key_sum, value_sum,
):
    rows = 256

    def unturn(grad, i):
        table = (table_mine if i < 2 else table_rest)[i % 2 * rows : i % 2 * rows + rows, :]
        return grad * table[:, :128] - pltpu.roll(grad, 64, 1) * table[:, 128:]

    masked = jnp.broadcast_to(bias[...], (8, 1024)).T[:, 0:1]
    for h in range(2):
        cols = slice(h * 128, h * 128 + 128)
        keys = qkv[:, 256 + h * 128 : 384 + h * 128]
        keys_turned = keys.T
        values = qkv[:, 512 + h * 128 : 640 + h * 128]
        for i in range(4):
            here = slice(i * rows, (i + 1) * rows)
            query = qkv[here, cols]
            inside = slice(i % 2 * rows, i % 2 * rows + rows)
            d_here = (d_mine if i < 2 else d_rest)[inside, cols]
            heads = (heads_mine if i < 2 else heads_rest)[inside, cols]
            scores = dot(keys, query, NT) * SCALE + masked
            probs = jnp.exp(scores - lse[h : h + 1, here])
            mean = d_here.astype(F32) * heads.astype(F32)
            mean = jnp.sum(mean.T, axis=0, keepdims=True)
            d_scores = (probs * (dot(values, d_here, NT) - mean)).astype(BF)
            value_part = dot(probs.astype(BF), d_here, NN)
            key_part = dot(d_scores, query, NN)
            if i == 0:
                value_sum[...] = value_part
                key_sum[...] = key_part
            else:
                value_sum[...] += value_part
                key_sum[...] += key_part
            d_turned = dot(keys_turned, d_scores, NN) * SCALE
            inner = jnp.sum(d_turned * query.astype(F32).T, axis=0, keepdims=True)
            if h == 0:
                sums[0:1, here] = inner
            else:
                sums[0:1, here] += inner
            d_query[here, cols] = unturn(d_turned.T, i)
        d_value[:, cols] = value_sum[...].astype(BF)
        for i in range(4):
            here = slice(i * rows, (i + 1) * rows)
            d_rot = key_sum[here, :] * SCALE
            inner = d_rot * qkv[here, 256 + h * 128 : 384 + h * 128].astype(F32)
            inner = jnp.sum(inner.T, axis=0, keepdims=True)
            if h == 0:
                sums[1:2, here] = inner
            else:
                sums[1:2, here] += inner
            d_key[here, cols] = unturn(d_rot, i)


def attend_back(qkv, d_mine, d_rest, heads_mine, heads_rest, bias, lse, table, place):
    return call(
        attend_back_kernel,
        (1,),
        [whole(1024, 1280)]
        + [whole(512, 256)] * 4
        + [whole(1, 1024), whole(2, 1024)]
        + [
            pl.BlockSpec((512, 256), lambda i, p: (p[1], 0)),
            pl.BlockSpec((512, 256), lambda i, p: (1 - p[1], 0)),
        ],
        [whole(1024, 256), whole(1024, 256), whole(1024, 256), whole(2, 1024)],
        [
            shape(1024, 256, dtype=F32),
            shape(1024, 256, dtype=F32),
            shape(1024, 256),
            shape(2, 1024, dtype=F32),
        ],
        scratch=[pltpu.VMEM((1024, 128), F32), pltpu.VMEM((1024, 128), F32)],
        vmem=BIG,
    )(place, qkv, d_mine, d_rest, heads_mine, heads_rest, bias, lse, table, table)


def raw_back_kernel(
    place, d_query, d_key, d_value, query_hat, key_hat, sums, inv_rows, gains, mine, rest, gain_parts
):
    step = pl.program_id(0)

    @pl.when(step == 0)
    def _():
        gain_parts[...] = jnp.zeros_like(gain_parts)

    mean, inv = columns_of(sums[...]), columns_of(inv_rows[...])
    parts = []
    for i, (grad, hat) in enumerate(((d_query, query_hat), (d_key, key_hat))):
        normed = hat[...].astype(F32)
        scaled = grad[...] * gains[i : i + 1, :]
        parts.append((inv[:, i : i + 1] * (scaled - normed * mean[:, i : i + 1])).astype(BF))
        gain_parts[i : i + 1, :] += jnp.sum(grad[...] * normed, axis=0, keepdims=True)
    total = jnp.concatenate(parts + [d_value[...]], 1)

    @pl.when(step < 2)
    def _():
        mine[...] = total

    @pl.when(step >= 2)
    def _():
        rest[...] = total


def raw_back(d_query, d_key, d_value, qkv, sums, inv_rows, gains, place):
    step = 256
    spec = lambda width, column=0: pl.BlockSpec((step, width), lambda i, p: (i, column))
    line = lambda: pl.BlockSpec((2, step), lambda i, p: (0, i))
    return call(
        raw_back_kernel,
        (4,),
        [
            spec(256),
            spec(256),
            spec(256),
            spec(256, 3),
            spec(256, 4),
            line(),
            line(),
            whole(2, 256),
        ],
        [
            pl.BlockSpec((step, 768), lambda i, p: (jnp.minimum(i, 1), 0)),
            pl.BlockSpec((step, 768), lambda i, p: (jnp.maximum(i - 2, 0), 0)),
            whole(2, 256),
        ],
        [shape(512, 768), shape(512, 768), shape(2, 256, dtype=F32)],
    )(place, d_query, d_key, d_value, qkv, qkv, sums, inv_rows, gains)


def back_kernel(place, *refs):
    rows_mine, rows_rest, d_mine, d_rest, raw_mine, raw_rest, raw_got = refs[:7]
    heads_mine, heads_rest, own_q, own_k, own_v, near, far, low, inv, gain_mlp, moe = refs[7:18]
    pieces, terms = refs[18:22], refs[22:26]
    mine, rest, total, d_own, d_other = refs[26:]
    i = pl.program_id(0)

    @pl.when(i == 0)
    def _():
        for r in range(4):
            mine[r * 128 : r * 128 + 128, :] = heads_mine[line_rows(place, r), :]
            rest[r * 128 : r * 128 + 128, :] = heads_rest[line_rows(place, r), :]
        d_own[...] = pick(place[2], raw_mine[...], raw_got[...])
        d_other[...] = pick(place[2], raw_got[...], raw_mine[...])

    qkv = dot(rows_mine[...], raw_mine[...], TN) + dot(rows_rest[...], raw_rest[...], TN)
    back = dot(d_mine[...], mine[...], TN) + dot(d_rest[...], rest[...], TN)
    grads = jnp.concatenate([qkv.astype(BF), back.astype(BF)], 1)
    for j, piece in enumerate(pieces):

        @pl.when(i // 2 == j)
        def _(piece=piece):
            piece[pl.ds(pl.multiple_of(lax.rem(i, 2) * 256, 256), 256), :] = grads

    other = jnp.where(i // 4 == place[1], near[...], far[...])
    own = jnp.concatenate([own_q[...], own_k[...], own_v[...]], 1)
    part = dot(d_own[...], own, NT) + dot(d_other[...], other, NT)
    total[...] = part
    gain = jnp.sum(part * (low[...].astype(F32) * inv[...]), axis=0, keepdims=True)
    zeros = jnp.zeros((14, gain.shape[1]), F32)
    gains = jnp.concatenate([gain, gain_mlp[...], zeros], 0).astype(BF)
    for r, out in enumerate(terms):
        out[0:128, :] = total[line_rows(place, r), :].astype(BF)
        out[128:144, :] = gains
    terms[2][144:272, :] = moe[...]


def back(
    rows_mine, rows_rest, d_mine, d_rest, raw_mine, raw_rest, raw_got, heads,
    own, near, far, low, inv, gain_mlp, moe, place,
):
    rows, width, step = 512, low.shape[1], 256
    block = lambda: pl.BlockSpec(
        (rows, step), lambda i, p: (0, lax.rem(p[3] + i // 2, 4) * 2 + lax.rem(i, 2))
    )
    half = lambda: pl.BlockSpec((step, 768), lambda i, p: (lax.rem(i, 4), 0))
    tile = lambda: pl.BlockSpec((step, 256), lambda i, p: (i, 0))
    column = lambda n: pl.BlockSpec((n, step), lambda i, p: (0, i))
    return call(
        back_kernel,
        (width // step,),
        [block(), block(), block(), block()]
        + [whole(rows, 768)] * 3
        + [whole(rows, 256)] * 2
        + [tile(), tile(), tile(), half(), half(), column(rows), whole(rows, 1), column(1), column(128)],
        [whole(512, 1024)] * 4 + [column(n) for n in (144, 144, 272, 144)],
        [shape(512, 1024)] * 4 + [shape(n, width) for n in (144, 144, 272, 144)],
        scratch=[
            pltpu.VMEM((rows, 256), BF),
            pltpu.VMEM((rows, 256), BF),
            pltpu.VMEM((rows, step), F32),
            pltpu.VMEM((rows, 768), BF),
            pltpu.VMEM((rows, 768), BF),
        ],
    )(
        place, rows_mine, rows_rest, d_mine, d_rest, raw_mine, raw_rest, raw_got, *heads,
        *own, near, far, low, inv, gain_mlp, moe,
    )


def last_rows_kernel(place, *refs):
    d_terms, moe_terms = refs[:4], refs[4:7]
    d_middle, middle, low, inv, gain = refs[7:12]
    parts, gains, rows = refs[-3:]
    total = sum((t[0:144].astype(F32) for t in d_terms[1:]), d_terms[0][...].astype(F32))
    gains[...] = total[128:130]
    d_in = total[:128]
    hat = low[...].astype(F32) * inv[...]
    scaled = d_in * gain[...]
    mean = jnp.mean(scaled * hat, axis=1, keepdims=True)
    rows[1] = (d_middle[...] + inv[...] * (scaled - hat * mean)).astype(BF)
    moe = sum((t[...].astype(F32) for t in moe_terms), d_terms[2][144:272].astype(F32))
    rows[0] = (middle[...] + moe).astype(BF)
    for i in range(8):
        parts[i] = rows[:, :, i * 256 : i * 256 + 256]


def last_rows(d_terms, moe_terms, d_middle, middle, low, inv, gain, awaited, place):
    width = low.shape[1]
    mine = lambda n: pl.BlockSpec((128, n), lambda i, p: (p[0], 0))
    return call(
        last_rows_kernel,
        (1,),
        [whole(n, width) for n in (144, 144, 272, 144)]
        + [whole(128, width)] * 5
        + [mine(width), mine(1), whole(1, width)]
        + [ANYWHERE] * len(awaited),
        [whole(8, 2, 128, 256), whole(2, width)],
        [shape(8, 2, 128, 256), shape(2, width, dtype=F32)],
        scratch=[pltpu.VMEM((2, 128, width), BF)],
        vmem=BIG,
    )(place, *d_terms, *moe_terms, d_middle, middle, low, inv, gain, *awaited)


def settle_attention_kernel(place, *refs):
    here, there = refs[:4], refs[4:8]
    query, key, value, back, small = refs[9:]
    i = pl.program_id(0)

    @pl.when(i == 0)
    def _():
        small[...] = jnp.zeros_like(small)

    def one(mine, rest):
        mine, rest = mine[0].astype(F32), rest[0].astype(F32)
        first = pick(place[1], rest[:128], mine[:128])
        second = pick(place[1], mine[:128], rest[:128])
        total = jnp.concatenate([first, second], 0)
        query[...] = total[:, :256]
        key[...] = total[:, 256:512]
        value[...] = total[:, 512:768]
        back[...] = total[:, 768:].T
        mine, rest = mine[128:], rest[128:]
        row = lax.broadcasted_iota(jnp.int32, mine.shape, 0)
        small[...] += jnp.where(row < 4, mine + rest, pick(place[2], mine, rest))

    for r in range(4):

        @pl.when(lax.rem(i // 2 + 4 - place[3], 4) == r)
        def _(r=r):
            one(here[r], there[r])


def settle_attention(here, there, awaited, place):
    piece = lambda: pl.BlockSpec((1, 144, 1024), lambda i, p: (lax.rem(i + p[4], 2), 0, 0))
    rows = lambda: pl.BlockSpec((256, 256), lambda i, p: (i, 0))
    return call(
        settle_attention_kernel,
        (8,),
        [piece() for _ in range(8)] + [ANYWHERE],
        [rows(), rows(), rows(), pl.BlockSpec((256, 256), lambda i, p: (0, i)), whole(16, 1024)],
        [shape(2048, 256, dtype=F32)] * 3
        + [shape(256, 2048, dtype=F32), shape(16, 1024, dtype=F32)],
    )(place, *here, *there, awaited)


def settle_experts_kernel(place, gu_mine, gu_got, down_mine, down_got, gate, up, down):
    total = pick(place[2], gu_mine[0], gu_got[0]).astype(F32)
    for j in range(2):
        gate[j] = total[:, j * 256 : j * 256 + 128]
        up[j] = total[:, j * 256 + 128 : j * 256 + 256]
    total = pick(place[2], down_mine[0], down_got[0]).astype(F32)
    down[...] = total.reshape(down.shape)


def settle_experts(gu_mine, gu_got, down_mine, down_got, place):
    def step(i, p, mine):
        return jnp.where(p[2] == mine, i, 0)

    def tall(mine):
        def index(i, p):
            j = step(i, p, mine)
            return (j // 4, lax.rem(j, 4), 0)

        return pl.BlockSpec((1, 512, 512), index)

    def flat(mine):
        def index(i, p):
            j = step(i, p, mine)
            return (j // 4, 0, lax.rem(j, 4))

        return pl.BlockSpec((1, 256, 512), index)

    thin = lambda: pl.BlockSpec((2, 512, 128), lambda i, p: (i // 4, lax.rem(i, 4), 0))
    return call(
        settle_experts_kernel,
        (8,),
        [tall(1), tall(0), flat(1), flat(0)],
        [thin(), thin(), pl.BlockSpec((2, 128, 512), lambda i, p: (i // 4, 0, lax.rem(i, 4)))],
        [shape(4, 2048, 128, dtype=F32)] * 2 + [shape(4, 128, 2048, dtype=F32)],
        flops=20_000_000_000,
    )(place, gu_mine, gu_got, down_mine, down_got)


def choice_weights(ids, gates, experts, capacity):
    named = ids[:, :, None] == jnp.arange(experts, dtype=jnp.int32)
    count = jnp.sum(named.astype(F32), axis=1)
    tokens = ids.shape[0]
    earlier = (
        jnp.arange(tokens, dtype=jnp.int32)[:, None] > jnp.arange(tokens, dtype=jnp.int32)[None, :]
    ).astype(BF)
    place = jnp.dot(earlier, count.astype(BF), preferred_element_type=F32)
    weight = jnp.sum(jnp.where(named, gates[:, :, None], 0.0), axis=1)
    return jnp.where(place < capacity, weight, 0.0)


def local(
    hidden_in,
    cotangent,
    sequence_order,
    seq_lengths,
    expert_ids,
    gate_weights,
    w_query,
    w_key,
    w_value,
    w_output,
    gain_attn,
    gain_query,
    gain_key,
    gain_mlp,
    w_gate,
    w_up,
    w_down,
):
    zl, y, c, zh, x = (lax.axis_index(a) for a in AXES)
    same = c == zh
    length = hidden_in.shape[1]
    half = length // 2
    experts = w_gate.shape[0]
    width = w_query.shape[0]
    place = jnp.stack([x, c, same.astype(jnp.int32), y, zl, zh]).astype(jnp.int32)
    sequence = (zl * SIZES[1] + y) * 2 + zh
    tokens_here = seq_lengths[sequence]
    ids_here = expert_ids[sequence]
    gates_here = gate_weights[sequence]

    x_dealt = deal_in(hidden_in[0], zh)
    qkv_own = [w_query, w_key, w_value]
    qkv_near = other_half(qkv_own, c, x_dealt)
    x_pieces = gather_x(x_dealt)
    cot_dealt = deal_in(cotangent[0], zh, x_pieces[1])
    gains_own = jnp.stack([gain_query, gain_key], 0)
    gains_other = other_half_chip(gains_own)

    table = jnp.asarray(rope_tables(length))
    positions = (jnp.arange(length, dtype=jnp.int32) + c * half) % length
    bias = jnp.where(positions < tokens_here, 0.0, -1e30).astype(F32)
    weight_all = choice_weights(ids_here, gates_here, experts, length * 2 // experts)
    weight_here = lax.dynamic_slice_in_dim(weight_all, c * half, half, 0)
    weight_here = lax.dynamic_slice_in_dim(
        jnp.concatenate([weight_here, weight_here], 0), x * (half // 4), half, 0
    )

    x_low, attn_in, inv_one = norm_rows(x_pieces, place, gain_attn[None, :])
    qkv_near, cot_first = tie([qkv_near, cot_dealt], attn_in)
    qkv_far = other_core(qkv_near)
    out_near = other_half([w_output], c, attn_in)
    raw_send, raw_keep, squares = project(attn_in, qkv_own, qkv_near, qkv_far, out_near, place)
    (gains_other,) = tie([gains_other], squares)
    gains_keep = jnp.where(same, gains_own, gains_other)
    gains_qk = jnp.concatenate([gains_keep, jnp.where(same, gains_other, gains_own)], 0)
    inv_qk = lax.rsqrt(sum_x(squares[:2]) / width + EPS)
    (out_near,) = tie([out_near], inv_qk)
    down_near = other_half([w_down], c, out_near)
    gu_near = other_half([w_gate, w_up], c, out_near)
    cot_pieces = gather_x(cot_first, inv_qk)
    ready_send, ready_keep = prep(
        raw_send,
        raw_keep,
        inv_qk,
        gains_qk,
        table,
        (cot_pieces[1], cot_pieces[4]),
        place,
    )
    ready_rest = other_core(ready_send)
    qkv, heads_mine, heads_rest, lse = attend(ready_keep, ready_rest, bias[None, :], place)
    heads_got = other_core(heads_rest)
    out_near, inv_tied = tie([out_near, inv_qk], heads_got)
    out_far = other_core(out_near)
    inv_qk_rest = other_core(inv_tied)
    cot = place_rows(cot_pieces, place)
    attn_terms = send_x(
        heads_to_rows(heads_mine, heads_got, w_output, out_near, out_far, (cot, heads_got), place)
    )
    attn_in, cot = tie([attn_in, cot], heads_got)
    attn_in_rest = other_core(attn_in)
    cot_rest = other_core(cot)

    middle, moe_own, inv_two = middle_rows(attn_terms, x_low, gain_mlp[None, :], place)
    moe_pieces = gather_x(moe_own)
    gu_near, down_near = tie([gu_near, down_near], moe_pieces[1])
    gu_near, down_near = tie([gu_near, down_near], moe_pieces[4])
    down_far = other_core(down_near)
    cot_down = cot_back(cot, w_down, down_near, down_far, place)
    gu_far = other_core(gu_near)
    hidden_send, hidden_keep, moe_in, *d_moe_terms = expert_layer(
        moe_pieces, cot_down, weight_here, w_gate, w_up, gu_near, gu_far, place
    )
    d_moe_terms = send_x(d_moe_terms)
    moe_terms = expert_out(
        hidden_send, hidden_keep, w_down, down_near, down_far, hidden_keep, place
    )
    hidden_all = jnp.concatenate([hidden_keep, other_core(hidden_send)], 1)
    moe_all = jnp.concatenate([moe_in, other_core(moe_in)], 0)
    cot_all = jnp.concatenate([cot, cot_rest], 0)
    grad_gate_up = jnp.einsum(
        "td,etf->edf", moe_all, hidden_all[:, :, :512], preferred_element_type=F32
    ).astype(BF)
    grad_down = jnp.einsum(
        "etf,td->efd", hidden_all[:, :, 512:], cot_all, preferred_element_type=F32
    ).astype(BF)

    d_middle, d_own, gain_mlp_part = middle_back(
        d_moe_terms,
        middle,
        inv_two,
        gain_mlp[None, :],
        cot,
        (grad_gate_up, grad_down, moe_terms[0]),
        place,
    )
    grad_gate_up, grad_down = lax.psum((grad_gate_up, grad_down), GROUPS)
    d_pieces = gather_x(d_own)
    d_heads_keep, d_heads_send, d_attn = rows_to_heads(
        d_pieces, w_output, out_near, out_far, place
    )
    d_heads_rest = other_core(d_heads_send)
    *moe_terms, d_attn = tie(list(moe_terms) + [d_attn], d_heads_rest)
    moe_after, moe_before = along(moe_terms[1], "x", 1), along(moe_terms[3], "x", -1)
    d_attn_rest = other_core(d_attn)
    d_query, d_key, d_value, sums = attend_back(
        qkv,
        d_heads_keep,
        d_heads_rest,
        heads_mine,
        heads_rest,
        bias[None, :],
        lse,
        table,
        place,
    )
    (sums,) = tie([sums], moe_after)
    (sums,) = tie([sums], moe_before)
    sums_rest = other_core(sums)
    sums = sums + jnp.concatenate([sums_rest[:, half:], sums_rest[:, :half]], 1)
    sums = sum_x(sums) / width
    raw_mine, raw_rest, gain_qk_parts = raw_back(
        d_query,
        d_key,
        d_value,
        qkv,
        sums,
        jnp.concatenate([inv_qk, inv_qk_rest], 1),
        gains_keep,
        place,
    )
    raw_got = other_core(raw_rest)
    pieces = back(
        attn_in,
        attn_in_rest,
        d_attn,
        d_attn_rest,
        raw_mine,
        raw_rest,
        raw_got,
        (heads_mine, heads_rest),
        qkv_own,
        qkv_near,
        qkv_far,
        x_low,
        inv_one,
        gain_mlp_part,
        moe_terms[2],
        place,
    )
    weight_terms = send_y(pieces[:4])
    d_in_terms = send_x(pieces[4:])
    moe_terms = [moe_terms[0], moe_after, moe_before]
    rows_dealt, gains = last_rows(
        d_in_terms,
        moe_terms,
        d_middle,
        middle,
        x_low,
        inv_one,
        gain_attn[None, :],
        weight_terms[1:],
        place,
    )
    dealt = deal_line(rows_dealt)
    grad_gate_up, grad_down = tie([grad_gate_up, grad_down], rows_dealt)
    total = sum((t.astype(F32) for t in weight_terms[1:]), weight_terms[0].astype(F32)).astype(BF)
    near, far = to_shard(total, zl, same)
    total = (near.astype(F32) + far.astype(F32)).astype(BF)
    first = c == 0
    got = other_core(jnp.where(first, total[128:], total[:128]))
    mine = jnp.where(first, total[:128], total[128:]).astype(F32) + got.astype(F32)
    small = jnp.concatenate([gains.reshape(-1), gain_qk_parts.reshape(-1)])
    small = (small + lax.ppermute(small, "zh", [(0, 1), (1, 0)])).reshape(9, 512)
    small = jnp.concatenate([small.reshape(-1), jnp.zeros((11776,), F32)]).reshape(16, 1024)
    (mine,) = tie([jnp.concatenate([mine, small], 0).astype(BF)], dealt)
    here = from_groups(mine)
    (dealt,) = tie([dealt], here[0])
    output, grad_input = deal_out(dealt, same)

    grad_gate, grad_up, grad_down = settle_experts(
        grad_gate_up, settle(grad_gate_up), grad_down, settle(grad_down), place
    )
    here = tie(list(here), grad_down)
    grad_query, grad_key, grad_value, grad_output, small = settle_attention(
        here, [other_core(t) for t in here], grad_down, place
    )
    small = small.reshape(-1)
    return (
        output[None],
        grad_input[None],
        grad_query,
        grad_key,
        grad_value,
        grad_output,
        small[:width],
        small[2 * width : 2 * width + 256],
        small[2 * width + 256 : 2 * width + 512],
        small[width : 2 * width],
        grad_gate,
        grad_up,
        grad_down,
    )


def solution(mesh):
    fine = Mesh(mesh.devices.reshape(SIZES), AXES)
    columns = P(None, TENSOR)
    placed = (
        P(DP, None, TENSOR),
        P(DP, None, TENSOR),
        P(),
        P(),
        P(),
        P(),
        columns,
        columns,
        columns,
        P(TENSOR, None),
        P(),
        P(TENSOR),
        P(TENSOR),
        P(),
        P(None, None, TENSOR),
        P(None, None, TENSOR),
        P(None, TENSOR, None),
    )
    return jax.shard_map(
        local,
        mesh=fine,
        in_specs=placed,
        out_specs=placed[:2]
        + (columns, columns, columns, P(TENSOR, None), P(), P(TENSOR), P(TENSOR), P())
        + placed[14:],
        check_vma=False,
    )
```

```python
import math

import jax
import jax.numpy as jnp
import numpy as np
from jax import lax
from jax.experimental import pallas as pl
from jax.experimental.pallas import tpu as pltpu
from jax.sharding import Mesh
from jax.sharding import PartitionSpec as P

AXES = ("zl", "y", "c", "zh", "x")
SIZES = (2, 4, 2, 2, 4)
DP = ("zl", "y", "c")
TENSOR = ("zh", "x")
GROUPS = ("zl", "y", "zh")

HEAD_DIM = 128
EPS = 1e-06
BASE = 50000.0
BF = jnp.bfloat16
F32 = jnp.float32
SCALE = 1.0 / math.sqrt(HEAD_DIM)
VMEM = 32 * 1024 * 1024
BIG = 56 * 1024 * 1024


def rope_tables(length):
    half = HEAD_DIM // 2
    frequency = np.power(
        np.float32(BASE), np.float32(-2.0) * np.arange(half, dtype=np.float32) / HEAD_DIM
    ).astype(np.float32)
    angles = np.arange(length, dtype=np.float32)[:, None] * frequency[None, :]
    cosine = np.cos(angles.astype(np.float64)).astype(np.float32)
    sine = np.sin(angles.astype(np.float64)).astype(np.float32)
    return np.concatenate([cosine, cosine, -sine, sine], 1)


def along(value, axis, shift):
    size = SIZES[AXES.index(axis)]
    return lax.ppermute(value, axis, [(i, (i + shift) % size) for i in range(size)])


def other_core(value):
    return lax.ppermute(value, "c", [(0, 1), (1, 0)])


def other_half_chip(value):
    return lax.ppermute(value, ("zl", "zh"), [(i, 3 - i) for i in range(4)])


def sum_x(value):
    return value + along(value, "x", 1) + along(value, "x", 2) + along(value, "x", 3)


def gather_x(value, awaited=None):
    half = value.shape[0] // 2
    after, before = along(value, "x", -1), along(value, "x", 1)
    far = [after[:half], before[half:]]
    if awaited is not None:
        far = tie(far, awaited)
    return [value, after, along(far[0], "x", -1), along(far[1], "x", 1), before]


def tie_kernel(*refs):
    del refs


def tie(values, awaited):
    anywhere = pl.BlockSpec(memory_space=pl.ANY)
    count = len(values)
    return pl.pallas_call(
        tie_kernel,
        in_specs=[anywhere] * (count + 1),
        out_specs=[anywhere] * count,
        out_shape=[jax.ShapeDtypeStruct(v.shape, v.dtype) for v in values],
        input_output_aliases={i: i for i in range(count)},
    )(*values, awaited)


def later(start, awaited):
    ends = awaited[(0,) * awaited.ndim].astype(F32) + awaited[(-1,) * awaited.ndim].astype(F32)
    return start + (ends != ends).astype(jnp.int32)


def send_x(pieces):
    return [
        pieces[0],
        along(pieces[1], "x", 1),
        along(pieces[2], "x", 2),
        along(pieces[3], "x", -1),
    ]


def deal_in(value, zh, awaited=None):
    half = value.shape[0] // 2
    got = []
    for k in (0, 1):
        pairs = [(a * 2 + b, (b ^ k) * 2 + a) for a in range(2) for b in range(2)]
        start = (zh ^ k) * half
        if awaited is not None:
            start = later(start, awaited)
        part = lax.dynamic_slice_in_dim(value, start, half, 0)
        got.append(lax.ppermute(part, ("c", "zh"), pairs))
    return jnp.stack(got, 0)


def deal_line(parts):
    return lax.all_to_all(parts, ("c", "x"), 0, 0, tiled=True)


def deal_out(dealt, same):
    got = dealt.transpose(1, 0, 2, 3).reshape(2, 1024, 256)
    moved = lax.ppermute(got, ("c", "zh"), [(1, 2), (2, 1)])
    got = jnp.where(same, got, moved)
    return got[0], got[1]


def other_half(weights, c, awaited):
    half = weights[0].shape[0] // 2
    start = later(c * half, awaited)
    parts = [lax.dynamic_slice_in_dim(w, start, half, 0) for w in weights]
    return other_half_chip(jnp.concatenate(parts, parts[0].ndim - 1))


def send_y(pieces):
    own, after, far, before = pieces
    half = far.shape[0] // 2
    up, down = along(far[:half], "y", 1), along(far[half:], "y", -1)
    add = lambda a, b: (a.astype(F32) + b.astype(F32)).astype(a.dtype)
    after = jnp.concatenate([add(after[:half], up), after[half:]], 0)
    before = jnp.concatenate([before[:half], add(before[half:], down)], 0)
    return [own, along(after, "y", 1), along(before, "y", -1)]


def to_shard(value, zl, same):
    low, high = value[:256], value[256:]
    near = jnp.where(zl == 0, low, high)
    far = jnp.where(zl == 0, high, low)
    order = [(i, k, m) for i in range(2) for k in range(2) for m in range(2)]
    index = lambda i, k, m: (i * 2 + k) * 2 + m
    stay = [(index(i, k, m), index(i, m, k)) for i, k, m in order if k != m]
    flip = [(index(i, k, m), index(1 - i, m, k)) for i, k, m in order]
    axes = ("zl", "c", "zh")
    got = lax.ppermute(near, axes, stay)
    return jnp.where(same, near, got), lax.ppermute(far, axes, flip)


def from_groups(piece):
    pair = jnp.stack([piece, lax.ppermute(piece, "zl", [(0, 1), (1, 0)])], 0)
    return [pair] + [along(pair, "y", -r) for r in (1, 2, 3)]


def settle(value):
    return lax.ppermute(value, ("c", "zh"), [(0, 2), (3, 1)])


def dot(left, right, dims):
    return lax.dot_general(left, right, (dims, ((), ())), preferred_element_type=F32)


NT = ((1,), (1,))
NN = ((1,), (0,))
TN = ((0,), (0,))


def call(kernel, grid, in_specs, out_specs, out_shape, scratch=(), flops=1, vmem=VMEM):
    return pl.pallas_call(
        kernel,
        grid_spec=pltpu.PrefetchScalarGridSpec(
            num_scalar_prefetch=1,
            grid=grid,
            in_specs=in_specs,
            out_specs=out_specs,
            scratch_shapes=scratch,
        ),
        out_shape=out_shape,
        compiler_params=pltpu.CompilerParams(vmem_limit_bytes=vmem),
        cost_estimate=pl.CostEstimate(flops=flops, bytes_accessed=1, transcendentals=0),
    )


def shape(*dims, dtype=BF):
    return jax.ShapeDtypeStruct(dims, dtype)


def whole(*dims):
    return pl.BlockSpec(dims, lambda i, p: (0,) * len(dims))


ANYWHERE = pl.BlockSpec(memory_space=pl.ANY)


def line_rows(place, r, rows=128):
    return pl.ds(pl.multiple_of(lax.rem(place[0] + r, 4) * rows, rows), rows)


def pick(flag, yes, no):
    return jnp.where(flag == 1, yes, no)


def pair_of(i, p):
    return jnp.where(i == 0, p[1], jnp.where(i == 1, 1 - p[1], i - 2))


def send_pair(i, p):
    other = jnp.where(i == 0, p[1], 1 - p[1])
    return jnp.where(p[2] == 1, other, jnp.maximum(i - 2, 0))


def keep_pair(i, p):
    other = jnp.where(i == 0, p[1], 1 - p[1])
    return jnp.where(p[2] == 1, jnp.maximum(i - 2, 0), other)


def role(i, p, first):
    return jnp.where(i < first, 1 - p[2], p[2])


def column_blocks(place, pieces):
    own, after, far_low, far_high, before = pieces
    for r, (first, second) in enumerate(
        ((own, own), (after, after), (far_low, far_high), (before, before))
    ):
        for k, piece in enumerate((first, second)):
            index = lax.rem(place[1] + k, 2) * 4 + lax.rem(place[0] + r, 4)
            yield pl.multiple_of(index * 256, 256), piece[k if r != 2 else 0]


def norm_kernel(place, own, after, far_low, far_high, before, gain, low, normed, inv):
    squares = jnp.zeros((low.shape[0], 1), F32)
    for column, here in column_blocks(place, (own, after, far_low, far_high, before)):
        low[:, pl.ds(column, 256)] = here
        here = here.astype(F32)
        squares += jnp.sum(here * here, axis=1, keepdims=True)
    root = lax.rsqrt(squares / low.shape[1] + EPS)
    inv[...] = root
    normed[...] = (low[...].astype(F32) * root * gain[...]).astype(BF)


def piece_specs(step, rows_of):
    return [pl.BlockSpec((n, step, 256), rows_of) for n in (2, 2, 1, 1, 2)]


def norm_rows(pieces, place, gain):
    rows, step = pieces[0].shape[1], 128
    full = lambda: pl.BlockSpec((step, 2048), lambda i, p: (i, 0))
    return call(
        norm_kernel,
        (rows // step,),
        piece_specs(step, lambda i, p: (0, i, 0)) + [whole(1, 2048)],
        [full(), full(), pl.BlockSpec((step, 1), lambda i, p: (i, 0))],
        [shape(rows, 2048), shape(rows, 2048), shape(rows, 1, dtype=F32)],
    )(place, *pieces, gain)


def place_kernel(place, own, after, far_low, far_high, before, low):
    for column, here in column_blocks(place, (own, after, far_low, far_high, before)):
        low[:, pl.ds(column, 256)] = here


def place_rows(pieces, place):
    rows = pieces[0].shape[1]
    step = rows // 4
    return call(
        place_kernel,
        (4,),
        piece_specs(step, lambda i, p: (0, lax.rem(i + p[0], 4), 0)),
        pl.BlockSpec((step, 2048), lambda i, p: (i, 0)),
        shape(rows, 2048),
    )(place, *pieces)


def project_kernel(place, rows_in, *refs):
    *own, near, far, awaited, send, keep, squares, columns = refs
    i = pl.program_id(0)
    lane = lax.broadcasted_iota(jnp.int32, columns.shape, 1)

    @pl.when(i == 0)
    def _():
        columns[...] = jnp.zeros_like(columns)

    def finish(raw):
        kept = role(i, place, 3)

        @pl.when(kept == 1)
        def _():
            keep[...] = raw

        @pl.when(kept == 0)
        def _():
            send[...] = raw

        total = jnp.sum(raw * raw, axis=1, keepdims=True)
        columns[...] += jnp.where(lane == lax.rem(i, 3), total, 0.0)

    @pl.when(i < 3)
    def _():
        half = near.shape[0]
        here = pl.ds(pl.multiple_of(place[1] * half, half), half)
        there = pl.ds(pl.multiple_of((1 - place[1]) * half, half), half)
        finish(dot(rows_in[:, here], near[...], NN) + dot(rows_in[:, there], far[...], NN))

    for j, weight in enumerate(own):

        @pl.when(i == 3 + j)
        def _(weight=weight):
            finish(dot(rows_in[...], weight[...], NN))

    @pl.when(i == 5)
    def _():
        squares[...] = columns[...].T


def project(rows_in, own, near, far, awaited, place):
    rows, width = rows_in.shape
    other = lambda i: jnp.minimum(i, 2)
    mine = lambda i: jnp.maximum(i - 3, 0)
    return call(
        project_kernel,
        (6,),
        [
            whole(rows, width),
            whole(width, 256),
            whole(width, 256),
            whole(width, 256),
            pl.BlockSpec((width // 2, 256), lambda i, p: (0, other(i))),
            pl.BlockSpec((width // 2, 256), lambda i, p: (0, other(i))),
            ANYWHERE,
        ],
        [
            pl.BlockSpec((rows, 256), lambda i, p: (0, jnp.where(p[2] == 1, other(i), mine(i)))),
            pl.BlockSpec((rows, 256), lambda i, p: (0, jnp.where(p[2] == 1, mine(i), other(i)))),
            whole(8, rows),
        ],
        [shape(rows, 768, dtype=F32), shape(rows, 768, dtype=F32), shape(8, rows, dtype=F32)],
        scratch=[pltpu.VMEM((rows, 8), F32)],
        vmem=BIG,
    )(place, rows_in, *own, near, far, awaited)


def columns_of(rows_two):
    rest = jnp.zeros((6, rows_two.shape[1]), F32)
    return jnp.concatenate([rows_two, rest], 0).T


def prep_kernel(place, raw_send, raw_keep, inv_rows, gains, table, first, second, out_send, out_keep):
    cosine, sine = table[:, :128], table[:, 128:]
    inv = columns_of(inv_rows[...])
    for part, (raw, out) in enumerate(((raw_keep, out_keep), (raw_send, out_send))):
        for i in range(2):
            for h in range(2):
                lo = i * 256 + h * 128
                normed = raw[:, lo : lo + 128] * inv[:, i : i + 1]
                out[:, 768 + lo : 896 + lo] = normed.astype(BF)
                normed = normed * gains[part * 2 + i : part * 2 + i + 1, h * 128 : h * 128 + 128]
                out[:, lo : lo + 128] = (
                    normed * cosine + pltpu.roll(normed, 64, 1) * sine
                ).astype(BF)
        out[:, 512:768] = raw[:, 512:768].astype(BF)


def prep(raw_send, raw_keep, inv_rows, gains, table, awaited, place):
    rows, step = raw_send.shape[0], 128
    spec = lambda width: pl.BlockSpec((step, width), lambda i, p: (i, 0))
    return call(
        prep_kernel,
        (rows // step,),
        [
            spec(768),
            spec(768),
            pl.BlockSpec((2, step), lambda i, p: (0, i)),
            whole(4, 256),
            pl.BlockSpec((step, 256), lambda i, p: (p[1] * 4 + i, 0)),
            ANYWHERE,
            ANYWHERE,
        ],
        [spec(1280), spec(1280)],
        [shape(rows, 1280), shape(rows, 1280)],
        vmem=BIG,
    )(place, raw_send, raw_keep, inv_rows, gains, table, *awaited)


def attend_kernel(place, mine, rest, bias, qkv, out_mine, out_rest, lse):
    rows = 256
    qkv[0:512, :] = mine[...]
    qkv[512:1024, :] = rest[...]
    for h in range(2):
        cols = slice(h * 128, h * 128 + 128)
        keys = qkv[:, 256 + h * 128 : 384 + h * 128]
        values = qkv[:, 512 + h * 128 : 640 + h * 128]
        for i in range(4):
            here = slice(i * rows, (i + 1) * rows)
            scores = dot(qkv[here, cols], keys, NT) * SCALE + bias[...]
            top = jnp.max(scores, axis=1, keepdims=True)
            weight = jnp.exp(scores - top)
            total = jnp.sum(weight, axis=1, keepdims=True)
            out = out_mine if i < 2 else out_rest
            out[i % 2 * rows : i % 2 * rows + rows, cols] = (
                dot(weight.astype(BF), values, NN) / total
            ).astype(BF)
            wide = jnp.broadcast_to(top + jnp.log(total), (rows, 8))
            lse[h : h + 1, here] = wide.T[0:1, :]


def attend(mine, rest, bias, place):
    return call(
        attend_kernel,
        (1,),
        [whole(512, 1280), whole(512, 1280), whole(1, 1024)],
        [whole(1024, 1280), whole(512, 256), whole(512, 256), whole(2, 1024)],
        [shape(1024, 1280), shape(512, 256), shape(512, 256), shape(2, 1024, dtype=F32)],
    )(place, mine, rest, bias)


def fill_other(place, near, far, other):
    half = near.shape[0]
    other[pl.ds(pl.multiple_of(place[1] * half, half), half), :] = near[...]
    other[pl.ds(pl.multiple_of((1 - place[1]) * half, half), half), :] = far[...]


def heads_to_rows_kernel(place, keep, send, own, near, far, first, second, a, b, c, d, other):
    fill_other(place, near, far, other)
    for r, out in enumerate((a, b, c, d)):
        here = line_rows(place, r)
        left, right = keep[here, :], send[here, :]
        part = dot(pick(place[2], left, right), own[...], NN)
        part += dot(pick(place[2], right, left), other[...], NN)
        out[...] = part.astype(BF)


def heads_to_rows(heads, rest, own, near, far, awaited, place):
    width = own.shape[1]
    step = width // 2
    tile = lambda n: pl.BlockSpec((n, step), lambda i, p: (0, i))
    return call(
        heads_to_rows_kernel,
        (2,),
        [whole(512, 256), whole(512, 256), tile(256), tile(128), tile(128), ANYWHERE, ANYWHERE],
        [tile(128)] * 4,
        [shape(128, width)] * 4,
        scratch=[pltpu.VMEM((256, step), BF)],
    )(place, heads, rest, own, near, far, *awaited)


def fill(rows, pieces):
    start = 0
    for piece in pieces:
        rows[start : start + piece.shape[0], :] = piece[...]
        start += piece.shape[0]


def rows_to_heads_kernel(
    place, own_rows, after, far_low, far_high, before, own, near, far,
    keep, send, rows, other,
):
    fill(rows, (own_rows, after, far_low, far_high, before))
    fill_other(place, near, far, other)
    mine = dot(rows[...], own[...], NT).astype(BF)
    rest = dot(rows[...], other[...], NT).astype(BF)
    for out, part in ((send, pick(place[2], rest, mine)), (keep, pick(place[2], mine, rest))):
        for r in range(4):
            out[line_rows(place, r), :] = part[r * 128 : r * 128 + 128]


def rows_to_heads(pieces, own, near, far, place):
    width = own.shape[1]
    return call(
        rows_to_heads_kernel,
        (1,),
        [whole(n, width) for n in (128, 128, 64, 64, 128, 256, 128, 128)],
        [whole(512, 256), whole(512, 256), whole(512, width)],
        [shape(512, 256), shape(512, 256), shape(512, width)],
        scratch=[pltpu.VMEM((256, width), BF)],
        vmem=BIG,
    )(place, *pieces, own, near, far)


def middle_kernel(place, a, b, c, d, low, gain, middle, normed, inv):
    total = sum((t[...].astype(F32) for t in (b, c, d)), a[...].astype(F32))
    total = low[...].astype(F32) + total
    middle[...] = total
    root = lax.rsqrt(jnp.mean(total * total, axis=1, keepdims=True) + EPS)
    inv[...] = root
    normed[...] = (total * root * gain[...]).astype(BF)


def middle_rows(terms, low, gain, place):
    width = low.shape[1]
    return call(
        middle_kernel,
        (1,),
        [whole(128, width)] * 4
        + [pl.BlockSpec((128, width), lambda i, p: (p[0], 0)), whole(1, width)],
        [whole(128, width), whole(128, width), whole(128, 1)],
        [shape(128, width, dtype=F32), shape(128, width), shape(128, 1, dtype=F32)],
    )(place, *terms, low, gain)


def middle_back_kernel(
    place, a, b, c, d, middle, inv, gain, cot, ready_a, ready_b, ready_c, d_middle, d_low, gain_part
):
    d_in = sum((t[...].astype(F32) for t in (b, c, d)), a[...].astype(F32))
    hat = middle[...] * inv[...]
    gain_part[...] = jnp.sum(d_in * hat, axis=0, keepdims=True)
    scaled = d_in * gain[...]
    mean = jnp.mean(scaled * hat, axis=1, keepdims=True)
    total = cot[...].astype(F32) + inv[...] * (scaled - hat * mean)
    d_middle[...] = total
    d_low[...] = total.astype(BF)


def middle_back(terms, middle, inv, gain, cot, ready, place):
    width = middle.shape[1]
    return call(
        middle_back_kernel,
        (1,),
        [whole(128, width)] * 5
        + [whole(128, 1), whole(1, width), whole(128, width)]
        + [ANYWHERE] * 3,
        [whole(128, width), whole(128, width), whole(1, width)],
        [shape(128, width, dtype=F32), shape(128, width), shape(1, width, dtype=F32)],
        vmem=BIG,
    )(place, *terms, middle, inv, gain, cot, *ready)


def cot_back_kernel(place, cot, own, near, far, out):
    def one(down):
        out[0] = dot(cot[...], down, NT)

    i = pl.program_id(0)
    pl.when(i == 0)(lambda: one(near[...].reshape(256, near.shape[2])))
    pl.when(i == 1)(lambda: one(far[...].reshape(256, far.shape[2])))
    pl.when(i >= 2)(lambda: one(own[...].reshape(256, own.shape[2])))


def own_pair(i, p):
    return (jnp.maximum(i - 2, 0), 0, 0)


def cot_back(cot, own, near, far, place):
    rows, width = cot.shape
    return call(
        cot_back_kernel,
        (4,),
        [
            whole(rows, width),
            pl.BlockSpec((2, 128, width), own_pair),
            whole(2, 128, width),
            whole(2, 128, width),
        ],
        pl.BlockSpec((1, rows, 256), lambda i, p: (i, 0, 0)),
        shape(4, rows, 256, dtype=F32),
        flops=5_000_000_000,
    )(place, cot, own, near, far)


def expert_kernel(
    place, own_rows, after, far_low, far_high, before, back, weights, own_gate, own_up, near, far,
    send, keep, rows, a, b, c, d, total, both_weights,
):
    i = pl.program_id(0)

    @pl.when(i == 0)
    def _():
        fill(rows, (own_rows, after, far_low, far_high, before))

    def two(gate, gate_start, up, up_start):
        for j in range(2):
            both_weights[:, j * 256 : j * 256 + 128] = gate[j, :, gate_start : gate_start + 128]
            both_weights[:, j * 256 + 128 : j * 256 + 256] = up[j, :, up_start : up_start + 128]
        lane = lax.broadcasted_iota(jnp.int32, weights.shape, 1)
        pre = dot(rows[...], both_weights[...], NN)
        grads, acts = [], []
        for j in range(2):
            named = lane == pair_of(i, place) * 2 + j
            weight = jnp.sum(jnp.where(named, weights[...], 0.0), axis=1, keepdims=True)
            gate = pre[:, j * 256 : j * 256 + 128]
            up = pre[:, j * 256 + 128 : j * 256 + 256]
            sig = 1.0 / (1.0 + jnp.exp(-gate))
            silu = gate * sig
            d_act = weight * back[0, :, j * 128 : j * 128 + 128]
            acts.append((weight * (silu * up)).astype(BF))
            grads.append((d_act * up * sig * (1.0 + gate * (1.0 - sig))).astype(BF))
            grads.append((d_act * silu).astype(BF))
        both = jnp.concatenate(grads, 1)
        hidden = jnp.concatenate([both] + acts, 1)
        kept = role(i, place, 2)

        @pl.when(kept == 1)
        def _():
            keep[0] = hidden

        @pl.when(kept == 0)
        def _():
            send[0] = hidden

        part = dot(both, both_weights[...], NT)

        @pl.when(i == 0)
        def _():
            total[...] = part

        @pl.when(i > 0)
        def _():
            total[...] += part

    pl.when(i == 0)(lambda: two(near, 0, near, 128))
    pl.when(i == 1)(lambda: two(far, 0, far, 128))
    pl.when(i >= 2)(lambda: two(own_gate, 0, own_up, 0))

    @pl.when(i == 3)
    def _():
        for r, out in enumerate((a, b, c, d)):
            out[...] = total[r * 128 : r * 128 + 128, :].astype(BF)


def expert_layer(pieces, back, weights, own_gate, own_up, near, far, place):
    rows, width = 512, pieces[0].shape[1]
    return call(
        expert_kernel,
        (4,),
        [whole(n, width) for n in (128, 128, 64, 64, 128)]
        + [
            pl.BlockSpec((1, rows, 256), lambda i, p: (i, 0, 0)),
            whole(rows, 4),
            pl.BlockSpec((2, width, 128), own_pair),
            pl.BlockSpec((2, width, 128), own_pair),
            whole(2, width, 256),
            whole(2, width, 256),
        ],
        [
            pl.BlockSpec((1, rows, 768), lambda i, p: (send_pair(i, p), 0, 0)),
            pl.BlockSpec((1, rows, 768), lambda i, p: (keep_pair(i, p), 0, 0)),
            whole(rows, width),
        ]
        + [whole(128, width)] * 4,
        [shape(2, rows, 768), shape(2, rows, 768), shape(rows, width)] + [shape(128, width)] * 4,
        scratch=[pltpu.VMEM((rows, width), F32), pltpu.VMEM((width, 512), BF)],
        vmem=44 * 1024 * 1024,
    )(place, *pieces, back, weights, own_gate, own_up, near, far)


def expert_out_kernel(place, send, keep, own, near, far, awaited, a, b, c, d, total):
    i = pl.program_id(0)

    def one(down):
        acts = pick(role(i, place, 2), keep[0], send[0])
        part = dot(acts, down, NN)

        @pl.when(i == 0)
        def _():
            total[...] = part

        @pl.when(i > 0)
        def _():
            total[...] += part

    pl.when(i == 0)(lambda: one(near[...].reshape(256, near.shape[2])))
    pl.when(i == 1)(lambda: one(far[...].reshape(256, far.shape[2])))
    pl.when(i >= 2)(lambda: one(own[...].reshape(256, own.shape[2])))

    @pl.when(i == 3)
    def _():
        for r, out in enumerate((a, b, c, d)):
            out[...] = total[r * 128 : r * 128 + 128, :].astype(BF)


def expert_out(send, keep, own, near, far, awaited, place):
    rows, width = 512, own.shape[2]
    return call(
        expert_out_kernel,
        (4,),
        [
            pl.BlockSpec((1, rows, 256), lambda i, p: (send_pair(i, p), 0, 2)),
            pl.BlockSpec((1, rows, 256), lambda i, p: (keep_pair(i, p), 0, 2)),
            pl.BlockSpec((2, 128, width), own_pair),
            whole(2, 128, width),
            whole(2, 128, width),
            ANYWHERE,
        ],
        [whole(128, width)] * 4,
        [shape(128, width)] * 4,
        scratch=[pltpu.VMEM((rows, width), F32)],
        flops=5_000_000_000,
    )(place, send, keep, own, near, far, awaited)


def attend_back_kernel(
    place, qkv, d_mine, d_rest, heads_mine, heads_rest, bias, lse, table_mine, table_rest,
    d_query, d_key, d_value, sums, key_sum, value_sum,
):
    rows = 256

    def unturn(grad, i):
        table = (table_mine if i < 2 else table_rest)[i % 2 * rows : i % 2 * rows + rows, :]
        return grad * table[:, :128] - pltpu.roll(grad, 64, 1) * table[:, 128:]

    masked = jnp.broadcast_to(bias[...], (8, 1024)).T[:, 0:1]
    for h in range(2):
        cols = slice(h * 128, h * 128 + 128)
        keys = qkv[:, 256 + h * 128 : 384 + h * 128]
        keys_turned = keys.T
        values = qkv[:, 512 + h * 128 : 640 + h * 128]
        for i in range(4):
            here = slice(i * rows, (i + 1) * rows)
            query = qkv[here, cols]
            inside = slice(i % 2 * rows, i % 2 * rows + rows)
            d_here = (d_mine if i < 2 else d_rest)[inside, cols]
            heads = (heads_mine if i < 2 else heads_rest)[inside, cols]
            scores = dot(keys, query, NT) * SCALE + masked
            probs = jnp.exp(scores - lse[h : h + 1, here])
            mean = d_here.astype(F32) * heads.astype(F32)
            mean = jnp.sum(mean.T, axis=0, keepdims=True)
            d_scores = (probs * (dot(values, d_here, NT) - mean)).astype(BF)
            value_part = dot(probs.astype(BF), d_here, NN)
            key_part = dot(d_scores, query, NN)
            if i == 0:
                value_sum[...] = value_part
                key_sum[...] = key_part
            else:
                value_sum[...] += value_part
                key_sum[...] += key_part
            d_turned = dot(keys_turned, d_scores, NN) * SCALE
            inner = jnp.sum(d_turned * query.astype(F32).T, axis=0, keepdims=True)
            if h == 0:
                sums[0:1, here] = inner
            else:
                sums[0:1, here] += inner
            d_query[here, cols] = unturn(d_turned.T, i)
        d_value[:, cols] = value_sum[...].astype(BF)
        for i in range(4):
            here = slice(i * rows, (i + 1) * rows)
            d_rot = key_sum[here, :] * SCALE
            inner = d_rot * qkv[here, 256 + h * 128 : 384 + h * 128].astype(F32)
            inner = jnp.sum(inner.T, axis=0, keepdims=True)
            if h == 0:
                sums[1:2, here] = inner
            else:
                sums[1:2, here] += inner
            d_key[here, cols] = unturn(d_rot, i)


def attend_back(qkv, d_mine, d_rest, heads_mine, heads_rest, bias, lse, table, place):
    return call(
        attend_back_kernel,
        (1,),
        [whole(1024, 1280)]
        + [whole(512, 256)] * 4
        + [whole(1, 1024), whole(2, 1024)]
        + [
            pl.BlockSpec((512, 256), lambda i, p: (p[1], 0)),
            pl.BlockSpec((512, 256), lambda i, p: (1 - p[1], 0)),
        ],
        [whole(1024, 256), whole(1024, 256), whole(1024, 256), whole(2, 1024)],
        [
            shape(1024, 256, dtype=F32),
            shape(1024, 256, dtype=F32),
            shape(1024, 256),
            shape(2, 1024, dtype=F32),
        ],
        scratch=[pltpu.VMEM((1024, 128), F32), pltpu.VMEM((1024, 128), F32)],
        vmem=BIG,
    )(place, qkv, d_mine, d_rest, heads_mine, heads_rest, bias, lse, table, table)


def raw_back_kernel(
    place, d_query, d_key, d_value, query_hat, key_hat, sums, inv_rows, gains, mine, rest, gain_parts
):
    step = pl.program_id(0)

    @pl.when(step == 0)
    def _():
        gain_parts[...] = jnp.zeros_like(gain_parts)

    mean, inv = columns_of(sums[...]), columns_of(inv_rows[...])
    parts = []
    for i, (grad, hat) in enumerate(((d_query, query_hat), (d_key, key_hat))):
        normed = hat[...].astype(F32)
        scaled = grad[...] * gains[i : i + 1, :]
        parts.append((inv[:, i : i + 1] * (scaled - normed * mean[:, i : i + 1])).astype(BF))
        gain_parts[i : i + 1, :] += jnp.sum(grad[...] * normed, axis=0, keepdims=True)
    total = jnp.concatenate(parts + [d_value[...]], 1)

    @pl.when(step < 2)
    def _():
        mine[...] = total

    @pl.when(step >= 2)
    def _():
        rest[...] = total


def raw_back(d_query, d_key, d_value, qkv, sums, inv_rows, gains, place):
    step = 256
    spec = lambda width, column=0: pl.BlockSpec((step, width), lambda i, p: (i, column))
    line = lambda: pl.BlockSpec((2, step), lambda i, p: (0, i))
    return call(
        raw_back_kernel,
        (4,),
        [
            spec(256),
            spec(256),
            spec(256),
            spec(256, 3),
            spec(256, 4),
            line(),
            line(),
            whole(2, 256),
        ],
        [
            pl.BlockSpec((step, 768), lambda i, p: (jnp.minimum(i, 1), 0)),
            pl.BlockSpec((step, 768), lambda i, p: (jnp.maximum(i - 2, 0), 0)),
            whole(2, 256),
        ],
        [shape(512, 768), shape(512, 768), shape(2, 256, dtype=F32)],
        vmem=BIG,
    )(place, d_query, d_key, d_value, qkv, qkv, sums, inv_rows, gains)


def back_kernel(place, *refs):
    rows_mine, rows_rest, d_mine, d_rest, raw_mine, raw_rest, raw_got = refs[:7]
    heads_mine, heads_rest, own_q, own_k, own_v, near, far, low, inv, gain_mlp, moe = refs[7:18]
    pieces, terms = refs[18:22], refs[22:26]
    mine, rest, total, d_own, d_other = refs[26:]
    i = pl.program_id(0)

    @pl.when(i == 0)
    def _():
        for r in range(4):
            mine[r * 128 : r * 128 + 128, :] = heads_mine[line_rows(place, r), :]
            rest[r * 128 : r * 128 + 128, :] = heads_rest[line_rows(place, r), :]
        d_own[...] = pick(place[2], raw_mine[...], raw_got[...])
        d_other[...] = pick(place[2], raw_got[...], raw_mine[...])

    qkv = dot(rows_mine[...], raw_mine[...], TN) + dot(rows_rest[...], raw_rest[...], TN)
    back = dot(d_mine[...], mine[...], TN) + dot(d_rest[...], rest[...], TN)
    grads = jnp.concatenate([qkv.astype(BF), back.astype(BF)], 1)
    for j, piece in enumerate(pieces):

        @pl.when(i // 2 == j)
        def _(piece=piece):
            piece[pl.ds(pl.multiple_of(lax.rem(i, 2) * 256, 256), 256), :] = grads

    other = jnp.where(i // 4 == place[1], near[...], far[...])
    own = jnp.concatenate([own_q[...], own_k[...], own_v[...]], 1)
    part = dot(d_own[...], own, NT) + dot(d_other[...], other, NT)
    total[...] = part
    gain = jnp.sum(part * (low[...].astype(F32) * inv[...]), axis=0, keepdims=True)
    zeros = jnp.zeros((14, gain.shape[1]), F32)
    gains = jnp.concatenate([gain, gain_mlp[...], zeros], 0).astype(BF)
    for r, out in enumerate(terms):
        out[0:128, :] = total[line_rows(place, r), :].astype(BF)
        out[128:144, :] = gains
    terms[2][144:272, :] = moe[...]


def back(
    rows_mine, rows_rest, d_mine, d_rest, raw_mine, raw_rest, raw_got, heads,
    own, near, far, low, inv, gain_mlp, moe, place,
):
    rows, width, step = 512, low.shape[1], 256
    block = lambda: pl.BlockSpec(
        (rows, step), lambda i, p: (0, lax.rem(p[3] + i // 2, 4) * 2 + lax.rem(i, 2))
    )
    half = lambda: pl.BlockSpec((step, 768), lambda i, p: (lax.rem(i, 4), 0))
    tile = lambda: pl.BlockSpec((step, 256), lambda i, p: (i, 0))
    column = lambda n: pl.BlockSpec((n, step), lambda i, p: (0, i))
    return call(
        back_kernel,
        (width // step,),
        [block(), block(), block(), block()]
        + [whole(rows, 768)] * 3
        + [whole(rows, 256)] * 2
        + [tile(), tile(), tile(), half(), half(), column(rows), whole(rows, 1), column(1), column(128)],
        [whole(512, 1024)] * 4 + [column(n) for n in (144, 144, 272, 144)],
        [shape(512, 1024)] * 4 + [shape(n, width) for n in (144, 144, 272, 144)],
        scratch=[
            pltpu.VMEM((rows, 256), BF),
            pltpu.VMEM((rows, 256), BF),
            pltpu.VMEM((rows, step), F32),
            pltpu.VMEM((rows, 768), BF),
            pltpu.VMEM((rows, 768), BF),
        ],
    )(
        place, rows_mine, rows_rest, d_mine, d_rest, raw_mine, raw_rest, raw_got, *heads,
        *own, near, far, low, inv, gain_mlp, moe,
    )


def last_rows_kernel(place, *refs):
    d_terms, moe_terms = refs[:4], refs[4:7]
    d_middle, middle, low, inv, gain = refs[7:12]
    parts, gains, rows = refs[-3:]
    total = sum((t[0:144].astype(F32) for t in d_terms[1:]), d_terms[0][...].astype(F32))
    gains[...] = total[128:130]
    d_in = total[:128]
    hat = low[...].astype(F32) * inv[...]
    scaled = d_in * gain[...]
    mean = jnp.mean(scaled * hat, axis=1, keepdims=True)
    rows[1] = (d_middle[...] + inv[...] * (scaled - hat * mean)).astype(BF)
    moe = sum((t[...].astype(F32) for t in moe_terms), d_terms[2][144:272].astype(F32))
    rows[0] = (middle[...] + moe).astype(BF)
    for i in range(8):
        parts[i] = rows[:, :, i * 256 : i * 256 + 256]


def last_rows(d_terms, moe_terms, d_middle, middle, low, inv, gain, awaited, place):
    width = low.shape[1]
    mine = lambda n: pl.BlockSpec((128, n), lambda i, p: (p[0], 0))
    return call(
        last_rows_kernel,
        (1,),
        [whole(n, width) for n in (144, 144, 272, 144)]
        + [whole(128, width)] * 5
        + [mine(width), mine(1), whole(1, width)]
        + [ANYWHERE] * len(awaited),
        [whole(8, 2, 128, 256), whole(2, width)],
        [shape(8, 2, 128, 256), shape(2, width, dtype=F32)],
        scratch=[pltpu.VMEM((2, 128, width), BF)],
        vmem=BIG,
    )(place, *d_terms, *moe_terms, d_middle, middle, low, inv, gain, *awaited)


def settle_attention_kernel(place, *refs):
    here, there = refs[:4], refs[4:8]
    query, key, value, back, small = refs[9:]
    i = pl.program_id(0)

    @pl.when(i == 0)
    def _():
        small[...] = jnp.zeros_like(small)

    def one(mine, rest):
        mine, rest = mine[0].astype(F32), rest[0].astype(F32)
        first = pick(place[1], rest[:128], mine[:128])
        second = pick(place[1], mine[:128], rest[:128])
        total = jnp.concatenate([first, second], 0)
        query[...] = total[:, :256]
        key[...] = total[:, 256:512]
        value[...] = total[:, 512:768]
        back[...] = total[:, 768:].T
        mine, rest = mine[128:], rest[128:]
        row = lax.broadcasted_iota(jnp.int32, mine.shape, 0)
        small[...] += jnp.where(row < 4, mine + rest, pick(place[2], mine, rest))

    for r in range(4):

        @pl.when(lax.rem(i // 2 + 4 - place[3], 4) == r)
        def _(r=r):
            one(here[r], there[r])


def settle_attention(here, there, awaited, place):
    piece = lambda: pl.BlockSpec((1, 144, 1024), lambda i, p: (lax.rem(i + p[4], 2), 0, 0))
    rows = lambda: pl.BlockSpec((256, 256), lambda i, p: (i, 0))
    return call(
        settle_attention_kernel,
        (8,),
        [piece() for _ in range(8)] + [ANYWHERE],
        [rows(), rows(), rows(), pl.BlockSpec((256, 256), lambda i, p: (0, i)), whole(16, 1024)],
        [shape(2048, 256, dtype=F32)] * 3
        + [shape(256, 2048, dtype=F32), shape(16, 1024, dtype=F32)],
    )(place, *here, *there, awaited)


def settle_experts_kernel(place, gu_mine, gu_got, down_mine, down_got, gate, up, down):
    total = pick(place[2], gu_mine[0], gu_got[0]).astype(F32)
    for j in range(2):
        gate[j] = total[:, j * 256 : j * 256 + 128]
        up[j] = total[:, j * 256 + 128 : j * 256 + 256]
    total = pick(place[2], down_mine[0], down_got[0]).astype(F32)
    down[...] = total.reshape(down.shape)


def settle_experts(gu_mine, gu_got, down_mine, down_got, place):
    def step(i, p, mine):
        return jnp.where(p[2] == mine, i, 0)

    def tall(mine):
        def index(i, p):
            j = step(i, p, mine)
            return (j // 4, lax.rem(j, 4), 0)

        return pl.BlockSpec((1, 512, 512), index)

    def flat(mine):
        def index(i, p):
            j = step(i, p, mine)
            return (j // 4, 0, lax.rem(j, 4))

        return pl.BlockSpec((1, 256, 512), index)

    thin = lambda: pl.BlockSpec((2, 512, 128), lambda i, p: (i // 4, lax.rem(i, 4), 0))
    return call(
        settle_experts_kernel,
        (8,),
        [tall(1), tall(0), flat(1), flat(0)],
        [thin(), thin(), pl.BlockSpec((2, 128, 512), lambda i, p: (i // 4, 0, lax.rem(i, 4)))],
        [shape(4, 2048, 128, dtype=F32)] * 2 + [shape(4, 128, 2048, dtype=F32)],
        flops=20_000_000_000,
    )(place, gu_mine, gu_got, down_mine, down_got)


def choice_weights(ids, gates, experts, capacity):
    named = ids[:, :, None] == jnp.arange(experts, dtype=jnp.int32)
    count = jnp.sum(named.astype(F32), axis=1)
    tokens = ids.shape[0]
    earlier = (
        jnp.arange(tokens, dtype=jnp.int32)[:, None] > jnp.arange(tokens, dtype=jnp.int32)[None, :]
    ).astype(BF)
    place = jnp.dot(earlier, count.astype(BF), preferred_element_type=F32)
    weight = jnp.sum(jnp.where(named, gates[:, :, None], 0.0), axis=1)
    return jnp.where(place < capacity, weight, 0.0)


def local(
    hidden_in,
    cotangent,
    sequence_order,
    seq_lengths,
    expert_ids,
    gate_weights,
    w_query,
    w_key,
    w_value,
    w_output,
    gain_attn,
    gain_query,
    gain_key,
    gain_mlp,
    w_gate,
    w_up,
    w_down,
):
    zl, y, c, zh, x = (lax.axis_index(a) for a in AXES)
    same = c == zh
    length = hidden_in.shape[1]
    half = length // 2
    experts = w_gate.shape[0]
    width = w_query.shape[0]
    place = jnp.stack([x, c, same.astype(jnp.int32), y, zl, zh]).astype(jnp.int32)
    sequence = (zl * SIZES[1] + y) * 2 + zh
    tokens_here = seq_lengths[sequence]
    ids_here = expert_ids[sequence]
    gates_here = gate_weights[sequence]

    x_dealt = deal_in(hidden_in[0], zh)
    qkv_own = [w_query, w_key, w_value]
    qkv_near = other_half(qkv_own, c, x_dealt)
    x_pieces = gather_x(x_dealt)
    cot_dealt = deal_in(cotangent[0], zh, x_pieces[1])
    gains_own = jnp.stack([gain_query, gain_key], 0)
    gains_other = other_half_chip(gains_own)

    table = jnp.asarray(rope_tables(length))
    positions = (jnp.arange(length, dtype=jnp.int32) + c * half) % length
    bias = jnp.where(positions < tokens_here, 0.0, -1e30).astype(F32)
    weight_all = choice_weights(ids_here, gates_here, experts, length * 2 // experts)
    weight_here = lax.dynamic_slice_in_dim(weight_all, c * half, half, 0)
    weight_here = lax.dynamic_slice_in_dim(
        jnp.concatenate([weight_here, weight_here], 0), x * (half // 4), half, 0
    )

    x_low, attn_in, inv_one = norm_rows(x_pieces, place, gain_attn[None, :])
    qkv_near, cot_first = tie([qkv_near, cot_dealt], attn_in)
    qkv_far = other_core(qkv_near)
    out_near = other_half([w_output], c, attn_in)
    raw_send, raw_keep, squares = project(attn_in, qkv_own, qkv_near, qkv_far, out_near, place)
    (gains_other,) = tie([gains_other], squares)
    gains_keep = jnp.where(same, gains_own, gains_other)
    gains_qk = jnp.concatenate([gains_keep, jnp.where(same, gains_other, gains_own)], 0)
    inv_qk = lax.rsqrt(sum_x(squares[:2]) / width + EPS)
    (out_near,) = tie([out_near], inv_qk)
    down_near = other_half([w_down], c, out_near)
    gu_near = other_half([w_gate, w_up], c, out_near)
    cot_pieces = gather_x(cot_first, inv_qk)
    ready_send, ready_keep = prep(
        raw_send,
        raw_keep,
        inv_qk,
        gains_qk,
        table,
        (cot_pieces[1], cot_pieces[4]),
        place,
    )
    ready_rest = other_core(ready_send)
    qkv, heads_mine, heads_rest, lse = attend(ready_keep, ready_rest, bias[None, :], place)
    heads_got = other_core(heads_rest)
    out_near, inv_tied = tie([out_near, inv_qk], heads_got)
    out_far = other_core(out_near)
    inv_qk_rest = other_core(inv_tied)
    cot = place_rows(cot_pieces, place)
    attn_terms = send_x(
        heads_to_rows(heads_mine, heads_got, w_output, out_near, out_far, (cot, heads_got), place)
    )
    attn_in, cot = tie([attn_in, cot], heads_got)
    attn_in_rest = other_core(attn_in)
    cot_rest = other_core(cot)

    middle, moe_own, inv_two = middle_rows(attn_terms, x_low, gain_mlp[None, :], place)
    moe_pieces = gather_x(moe_own)
    gu_near, down_near = tie([gu_near, down_near], moe_pieces[1])
    gu_near, down_near = tie([gu_near, down_near], moe_pieces[4])
    down_far = other_core(down_near)
    cot_down = cot_back(cot, w_down, down_near, down_far, place)
    gu_far = other_core(gu_near)
    hidden_send, hidden_keep, moe_in, *d_moe_terms = expert_layer(
        moe_pieces, cot_down, weight_here, w_gate, w_up, gu_near, gu_far, place
    )
    d_moe_terms = send_x(d_moe_terms)
    moe_terms = expert_out(
        hidden_send, hidden_keep, w_down, down_near, down_far, hidden_keep, place
    )
    hidden_all = jnp.concatenate([hidden_keep, other_core(hidden_send)], 1)
    moe_all = jnp.concatenate([moe_in, other_core(moe_in)], 0)
    cot_all = jnp.concatenate([cot, cot_rest], 0)
    grad_gate_up = jnp.einsum(
        "td,etf->edf", moe_all, hidden_all[:, :, :512], preferred_element_type=F32
    ).astype(BF)
    grad_down = jnp.einsum(
        "etf,td->efd", hidden_all[:, :, 512:], cot_all, preferred_element_type=F32
    ).astype(BF)

    d_middle, d_own, gain_mlp_part = middle_back(
        d_moe_terms,
        middle,
        inv_two,
        gain_mlp[None, :],
        cot,
        (grad_gate_up, grad_down, moe_terms[0]),
        place,
    )
    grad_gate_up, grad_down = lax.psum((grad_gate_up, grad_down), GROUPS)
    d_pieces = gather_x(d_own)
    d_heads_keep, d_heads_send, d_attn = rows_to_heads(
        d_pieces, w_output, out_near, out_far, place
    )
    d_heads_rest = other_core(d_heads_send)
    *moe_terms, d_attn = tie(list(moe_terms) + [d_attn], d_heads_rest)
    moe_after, moe_before = along(moe_terms[1], "x", 1), along(moe_terms[3], "x", -1)
    d_attn_rest = other_core(d_attn)
    d_query, d_key, d_value, sums = attend_back(
        qkv,
        d_heads_keep,
        d_heads_rest,
        heads_mine,
        heads_rest,
        bias[None, :],
        lse,
        table,
        place,
    )
    (sums,) = tie([sums], moe_after)
    (sums,) = tie([sums], moe_before)
    sums_rest = other_core(sums)
    sums = sums + jnp.concatenate([sums_rest[:, half:], sums_rest[:, :half]], 1)
    sums = sum_x(sums) / width
    raw_mine, raw_rest, gain_qk_parts = raw_back(
        d_query,
        d_key,
        d_value,
        qkv,
        sums,
        jnp.concatenate([inv_qk, inv_qk_rest], 1),
        gains_keep,
        place,
    )
    raw_got = other_core(raw_rest)
    pieces = back(
        attn_in,
        attn_in_rest,
        d_attn,
        d_attn_rest,
        raw_mine,
        raw_rest,
        raw_got,
        (heads_mine, heads_rest),
        qkv_own,
        qkv_near,
        qkv_far,
        x_low,
        inv_one,
        gain_mlp_part,
        moe_terms[2],
        place,
    )
    weight_terms = send_y(pieces[:4])
    d_in_terms = send_x(pieces[4:])
    moe_terms = [moe_terms[0], moe_after, moe_before]
    rows_dealt, gains = last_rows(
        d_in_terms,
        moe_terms,
        d_middle,
        middle,
        x_low,
        inv_one,
        gain_attn[None, :],
        weight_terms[1:],
        place,
    )
    dealt = deal_line(rows_dealt)
    grad_gate_up, grad_down = tie([grad_gate_up, grad_down], rows_dealt)
    total = sum((t.astype(F32) for t in weight_terms[1:]), weight_terms[0].astype(F32)).astype(BF)
    near, far = to_shard(total, zl, same)
    total = (near.astype(F32) + far.astype(F32)).astype(BF)
    first = c == 0
    got = other_core(jnp.where(first, total[128:], total[:128]))
    mine = jnp.where(first, total[:128], total[128:]).astype(F32) + got.astype(F32)
    small = jnp.concatenate([gains.reshape(-1), gain_qk_parts.reshape(-1)])
    small = (small + lax.ppermute(small, "zh", [(0, 1), (1, 0)])).reshape(9, 512)
    small = jnp.concatenate([small.reshape(-1), jnp.zeros((11776,), F32)]).reshape(16, 1024)
    (mine,) = tie([jnp.concatenate([mine, small], 0).astype(BF)], dealt)
    here = from_groups(mine)
    (dealt,) = tie([dealt], here[0])
    output, grad_input = deal_out(dealt, same)

    grad_gate, grad_up, grad_down = settle_experts(
        grad_gate_up, settle(grad_gate_up), grad_down, settle(grad_down), place
    )
    here = tie(list(here), grad_down)
    grad_query, grad_key, grad_value, grad_output, small = settle_attention(
        here, [other_core(t) for t in here], grad_down, place
    )
    small = small.reshape(-1)
    return (
        output[None],
        grad_input[None],
        grad_query,
        grad_key,
        grad_value,
        grad_output,
        small[:width],
        small[2 * width : 2 * width + 256],
        small[2 * width + 256 : 2 * width + 512],
        small[width : 2 * width],
        grad_gate,
        grad_up,
        grad_down,
    )


def solution(mesh):
    fine = Mesh(mesh.devices.reshape(SIZES), AXES)
    columns = P(None, TENSOR)
    placed = (
        P(DP, None, TENSOR),
        P(DP, None, TENSOR),
        P(),
        P(),
        P(),
        P(),
        columns,
        columns,
        columns,
        P(TENSOR, None),
        P(),
        P(TENSOR),
        P(TENSOR),
        P(),
        P(None, None, TENSOR),
        P(None, None, TENSOR),
        P(None, TENSOR, None),
    )
    return jax.shard_map(
        local,
        mesh=fine,
        in_specs=placed,
        out_specs=placed[:2]
        + (columns, columns, columns, P(TENSOR, None), P(), P(TENSOR), P(TENSOR), P())
        + placed[14:],
        check_vma=False,
    )
```

```python
import math

import jax
import jax.numpy as jnp
import numpy as np
from jax import lax
from jax.experimental import pallas as pl
from jax.experimental.pallas import tpu as pltpu
from jax.sharding import Mesh
from jax.sharding import PartitionSpec as P

AXES = ("zl", "y", "c", "zh", "x")
SIZES = (2, 4, 2, 2, 4)
DP = ("zl", "y", "c")
TENSOR = ("zh", "x")
GROUPS = ("zl", "y", "zh")

HEAD_DIM = 128
EPS = 1e-06
BASE = 50000.0
BF = jnp.bfloat16
F32 = jnp.float32
SCALE = 1.0 / math.sqrt(HEAD_DIM)
VMEM = 32 * 1024 * 1024
BIG = 56 * 1024 * 1024


def rope_tables(length):
    half = HEAD_DIM // 2
    frequency = np.power(
        np.float32(BASE), np.float32(-2.0) * np.arange(half, dtype=np.float32) / HEAD_DIM
    ).astype(np.float32)
    angles = np.arange(length, dtype=np.float32)[:, None] * frequency[None, :]
    cosine = np.cos(angles.astype(np.float64)).astype(np.float32)
    sine = np.sin(angles.astype(np.float64)).astype(np.float32)
    return np.concatenate([cosine, cosine, -sine, sine], 1)


def along(value, axis, shift):
    size = SIZES[AXES.index(axis)]
    return lax.ppermute(value, axis, [(i, (i + shift) % size) for i in range(size)])


def other_core(value):
    return lax.ppermute(value, "c", [(0, 1), (1, 0)])


def other_half_chip(value):
    return lax.ppermute(value, ("zl", "zh"), [(i, 3 - i) for i in range(4)])


def sum_x(value):
    return value + along(value, "x", 1) + along(value, "x", 2) + along(value, "x", 3)


def gather_x(value, awaited=None):
    half = value.shape[0] // 2
    after, before = along(value, "x", -1), along(value, "x", 1)
    far = [after[:half], before[half:]]
    if awaited is not None:
        far = tie(far, awaited)
    return [value, after, along(far[0], "x", -1), along(far[1], "x", 1), before]


def tie_kernel(*refs):
    del refs


def tie(values, awaited):
    anywhere = pl.BlockSpec(memory_space=pl.ANY)
    count = len(values)
    return pl.pallas_call(
        tie_kernel,
        in_specs=[anywhere] * (count + 1),
        out_specs=[anywhere] * count,
        out_shape=[jax.ShapeDtypeStruct(v.shape, v.dtype) for v in values],
        input_output_aliases={i: i for i in range(count)},
    )(*values, awaited)


def later(start, awaited):
    ends = awaited[(0,) * awaited.ndim].astype(F32) + awaited[(-1,) * awaited.ndim].astype(F32)
    return start + (ends != ends).astype(jnp.int32)


def send_x(pieces):
    return [
        pieces[0],
        along(pieces[1], "x", 1),
        along(pieces[2], "x", 2),
        along(pieces[3], "x", -1),
    ]


def deal_in(value, zh, awaited=None):
    half = value.shape[0] // 2
    got = []
    for k in (0, 1):
        pairs = [(a * 2 + b, (b ^ k) * 2 + a) for a in range(2) for b in range(2)]
        start = (zh ^ k) * half
        if awaited is not None:
            start = later(start, awaited)
        part = lax.dynamic_slice_in_dim(value, start, half, 0)
        got.append(lax.ppermute(part, ("c", "zh"), pairs))
    return jnp.stack(got, 0)


def deal_line(parts):
    return lax.all_to_all(parts, ("c", "x"), 0, 0, tiled=True)


def deal_out(dealt, same):
    got = dealt.transpose(1, 0, 2, 3).reshape(2, 1024, 256)
    moved = lax.ppermute(got, ("c", "zh"), [(1, 2), (2, 1)])
    got = jnp.where(same, got, moved)
    return got[0], got[1]


def other_half(weights, c, awaited):
    half = weights[0].shape[0] // 2
    start = later(c * half, awaited)
    parts = [lax.dynamic_slice_in_dim(w, start, half, 0) for w in weights]
    return other_half_chip(jnp.concatenate(parts, parts[0].ndim - 1))


def send_y(pieces):
    own, after, far, before = pieces
    half = far.shape[0] // 2
    up, down = along(far[:half], "y", 1), along(far[half:], "y", -1)
    add = lambda a, b: (a.astype(F32) + b.astype(F32)).astype(a.dtype)
    after = jnp.concatenate([add(after[:half], up), after[half:]], 0)
    before = jnp.concatenate([before[:half], add(before[half:], down)], 0)
    return [own, along(after, "y", 1), along(before, "y", -1)]


def to_shard(value, zl, same):
    low, high = value[:256], value[256:]
    near = jnp.where(zl == 0, low, high)
    far = jnp.where(zl == 0, high, low)
    order = [(i, k, m) for i in range(2) for k in range(2) for m in range(2)]
    index = lambda i, k, m: (i * 2 + k) * 2 + m
    stay = [(index(i, k, m), index(i, m, k)) for i, k, m in order if k != m]
    flip = [(index(i, k, m), index(1 - i, m, k)) for i, k, m in order]
    axes = ("zl", "c", "zh")
    got = lax.ppermute(near, axes, stay)
    return jnp.where(same, near, got), lax.ppermute(far, axes, flip)


def from_groups(piece):
    pair = jnp.stack([piece, lax.ppermute(piece, "zl", [(0, 1), (1, 0)])], 0)
    return [pair] + [along(pair, "y", -r) for r in (1, 2, 3)]


def settle(value):
    return lax.ppermute(value, ("c", "zh"), [(0, 2), (3, 1)])


def dot(left, right, dims):
    return lax.dot_general(left, right, (dims, ((), ())), preferred_element_type=F32)


NT = ((1,), (1,))
NN = ((1,), (0,))
TN = ((0,), (0,))


def call(kernel, grid, in_specs, out_specs, out_shape, scratch=(), flops=1, vmem=VMEM):
    return pl.pallas_call(
        kernel,
        grid_spec=pltpu.PrefetchScalarGridSpec(
            num_scalar_prefetch=1,
            grid=grid,
            in_specs=in_specs,
            out_specs=out_specs,
            scratch_shapes=scratch,
        ),
        out_shape=out_shape,
        compiler_params=pltpu.CompilerParams(vmem_limit_bytes=vmem),
        cost_estimate=pl.CostEstimate(flops=flops, bytes_accessed=1, transcendentals=0),
    )


def shape(*dims, dtype=BF):
    return jax.ShapeDtypeStruct(dims, dtype)


def whole(*dims):
    return pl.BlockSpec(dims, lambda i, p: (0,) * len(dims))


ANYWHERE = pl.BlockSpec(memory_space=pl.ANY)


def line_rows(place, r, rows=128):
    return pl.ds(pl.multiple_of(lax.rem(place[0] + r, 4) * rows, rows), rows)


def pick(flag, yes, no):
    return jnp.where(flag == 1, yes, no)


def pair_of(i, p):
    return jnp.where(i == 0, p[1], jnp.where(i == 1, 1 - p[1], i - 2))


def send_pair(i, p):
    other = jnp.where(i == 0, p[1], 1 - p[1])
    return jnp.where(p[2] == 1, other, jnp.maximum(i - 2, 0))


def keep_pair(i, p):
    other = jnp.where(i == 0, p[1], 1 - p[1])
    return jnp.where(p[2] == 1, jnp.maximum(i - 2, 0), other)


def role(i, p, first):
    return jnp.where(i < first, 1 - p[2], p[2])


def column_blocks(place, pieces):
    own, after, far_low, far_high, before = pieces
    for r, (first, second) in enumerate(
        ((own, own), (after, after), (far_low, far_high), (before, before))
    ):
        for k, piece in enumerate((first, second)):
            index = lax.rem(place[1] + k, 2) * 4 + lax.rem(place[0] + r, 4)
            yield pl.multiple_of(index * 256, 256), piece[k if r != 2 else 0]


def norm_kernel(place, own, after, far_low, far_high, before, gain, low, normed, inv):
    squares = jnp.zeros((low.shape[0], 1), F32)
    for column, here in column_blocks(place, (own, after, far_low, far_high, before)):
        low[:, pl.ds(column, 256)] = here
        here = here.astype(F32)
        squares += jnp.sum(here * here, axis=1, keepdims=True)
    root = lax.rsqrt(squares / low.shape[1] + EPS)
    inv[...] = root
    normed[...] = (low[...].astype(F32) * root * gain[...]).astype(BF)


def piece_specs(step, rows_of):
    return [pl.BlockSpec((n, step, 256), rows_of) for n in (2, 2, 1, 1, 2)]


def norm_rows(pieces, place, gain):
    rows, step = pieces[0].shape[1], 128
    full = lambda: pl.BlockSpec((step, 2048), lambda i, p: (i, 0))
    return call(
        norm_kernel,
        (rows // step,),
        piece_specs(step, lambda i, p: (0, i, 0)) + [whole(1, 2048)],
        [full(), full(), pl.BlockSpec((step, 1), lambda i, p: (i, 0))],
        [shape(rows, 2048), shape(rows, 2048), shape(rows, 1, dtype=F32)],
    )(place, *pieces, gain)


def place_kernel(place, own, after, far_low, far_high, before, low):
    for column, here in column_blocks(place, (own, after, far_low, far_high, before)):
        low[:, pl.ds(column, 256)] = here


def place_rows(pieces, place):
    rows = pieces[0].shape[1]
    step = rows // 4
    return call(
        place_kernel,
        (4,),
        piece_specs(step, lambda i, p: (0, lax.rem(i + p[0], 4), 0)),
        pl.BlockSpec((step, 2048), lambda i, p: (i, 0)),
        shape(rows, 2048),
    )(place, *pieces)


def project_kernel(place, rows_in, *refs):
    *own, near, far, awaited, send, keep, squares, columns = refs
    i = pl.program_id(0)
    lane = lax.broadcasted_iota(jnp.int32, columns.shape, 1)

    @pl.when(i == 0)
    def _():
        columns[...] = jnp.zeros_like(columns)

    def finish(raw):
        kept = role(i, place, 3)

        @pl.when(kept == 1)
        def _():
            keep[...] = raw

        @pl.when(kept == 0)
        def _():
            send[...] = raw

        total = jnp.sum(raw * raw, axis=1, keepdims=True)
        columns[...] += jnp.where(lane == lax.rem(i, 3), total, 0.0)

    @pl.when(i < 3)
    def _():
        half = near.shape[0]
        here = pl.ds(pl.multiple_of(place[1] * half, half), half)
        there = pl.ds(pl.multiple_of((1 - place[1]) * half, half), half)
        finish(dot(rows_in[:, here], near[...], NN) + dot(rows_in[:, there], far[...], NN))

    for j, weight in enumerate(own):

        @pl.when(i == 3 + j)
        def _(weight=weight):
            finish(dot(rows_in[...], weight[...], NN))

    @pl.when(i == 5)
    def _():
        squares[...] = columns[...].T


def project(rows_in, own, near, far, awaited, place):
    rows, width = rows_in.shape
    other = lambda i: jnp.minimum(i, 2)
    mine = lambda i: jnp.maximum(i - 3, 0)
    return call(
        project_kernel,
        (6,),
        [
            whole(rows, width),
            whole(width, 256),
            whole(width, 256),
            whole(width, 256),
            pl.BlockSpec((width // 2, 256), lambda i, p: (0, other(i))),
            pl.BlockSpec((width // 2, 256), lambda i, p: (0, other(i))),
            ANYWHERE,
        ],
        [
            pl.BlockSpec((rows, 256), lambda i, p: (0, jnp.where(p[2] == 1, other(i), mine(i)))),
            pl.BlockSpec((rows, 256), lambda i, p: (0, jnp.where(p[2] == 1, mine(i), other(i)))),
            whole(8, rows),
        ],
        [shape(rows, 768, dtype=F32), shape(rows, 768, dtype=F32), shape(8, rows, dtype=F32)],
        scratch=[pltpu.VMEM((rows, 8), F32)],
    )(place, rows_in, *own, near, far, awaited)


def columns_of(rows_two):
    rest = jnp.zeros((6, rows_two.shape[1]), F32)
    return jnp.concatenate([rows_two, rest], 0).T


def prep_kernel(place, raw_send, raw_keep, inv_rows, gains, table, first, second, out_send, out_keep):
    cosine, sine = table[:, :128], table[:, 128:]
    inv = columns_of(inv_rows[...])
    for part, (raw, out) in enumerate(((raw_keep, out_keep), (raw_send, out_send))):
        for i in range(2):
            for h in range(2):
                lo = i * 256 + h * 128
                normed = raw[:, lo : lo + 128] * inv[:, i : i + 1]
                out[:, 768 + lo : 896 + lo] = normed.astype(BF)
                normed = normed * gains[part * 2 + i : part * 2 + i + 1, h * 128 : h * 128 + 128]
                out[:, lo : lo + 128] = (
                    normed * cosine + pltpu.roll(normed, 64, 1) * sine
                ).astype(BF)
        out[:, 512:768] = raw[:, 512:768].astype(BF)


def prep(raw_send, raw_keep, inv_rows, gains, table, awaited, place):
    rows, step = raw_send.shape[0], 128
    spec = lambda width: pl.BlockSpec((step, width), lambda i, p: (i, 0))
    return call(
        prep_kernel,
        (rows // step,),
        [
            spec(768),
            spec(768),
            pl.BlockSpec((2, step), lambda i, p: (0, i)),
            whole(4, 256),
            pl.BlockSpec((step, 256), lambda i, p: (p[1] * 4 + i, 0)),
            ANYWHERE,
            ANYWHERE,
        ],
        [spec(1280), spec(1280)],
        [shape(rows, 1280), shape(rows, 1280)],
    )(place, raw_send, raw_keep, inv_rows, gains, table, *awaited)


def attend_kernel(place, mine, rest, bias, qkv, out_mine, out_rest, lse):
    rows = 256
    qkv[0:512, :] = mine[...]
    qkv[512:1024, :] = rest[...]
    for h in range(2):
        cols = slice(h * 128, h * 128 + 128)
        keys = qkv[:, 256 + h * 128 : 384 + h * 128]
        values = qkv[:, 512 + h * 128 : 640 + h * 128]
        for i in range(4):
            here = slice(i * rows, (i + 1) * rows)
            scores = dot(qkv[here, cols], keys, NT) * SCALE + bias[...]
            top = jnp.max(scores, axis=1, keepdims=True)
            weight = jnp.exp(scores - top)
            total = jnp.sum(weight, axis=1, keepdims=True)
            out = out_mine if i < 2 else out_rest
            out[i % 2 * rows : i % 2 * rows + rows, cols] = (
                dot(weight.astype(BF), values, NN) / total
            ).astype(BF)
            wide = jnp.broadcast_to(top + jnp.log(total), (rows, 8))
            lse[h : h + 1, here] = wide.T[0:1, :]


def attend(mine, rest, bias, place):
    return call(
        attend_kernel,
        (1,),
        [whole(512, 1280), whole(512, 1280), whole(1, 1024)],
        [whole(1024, 1280), whole(512, 256), whole(512, 256), whole(2, 1024)],
        [shape(1024, 1280), shape(512, 256), shape(512, 256), shape(2, 1024, dtype=F32)],
    )(place, mine, rest, bias)


def fill_other(place, near, far, other):
    half = near.shape[0]
    other[pl.ds(pl.multiple_of(place[1] * half, half), half), :] = near[...]
    other[pl.ds(pl.multiple_of((1 - place[1]) * half, half), half), :] = far[...]


def heads_to_rows_kernel(place, keep, send, own, near, far, first, second, a, b, c, d, other):
    fill_other(place, near, far, other)
    for r, out in enumerate((a, b, c, d)):
        here = line_rows(place, r)
        left, right = keep[here, :], send[here, :]
        part = dot(pick(place[2], left, right), own[...], NN)
        part += dot(pick(place[2], right, left), other[...], NN)
        out[...] = part.astype(BF)


def heads_to_rows(heads, rest, own, near, far, awaited, place):
    width = own.shape[1]
    step = width // 2
    tile = lambda n: pl.BlockSpec((n, step), lambda i, p: (0, i))
    return call(
        heads_to_rows_kernel,
        (2,),
        [whole(512, 256), whole(512, 256), tile(256), tile(128), tile(128), ANYWHERE, ANYWHERE],
        [tile(128)] * 4,
        [shape(128, width)] * 4,
        scratch=[pltpu.VMEM((256, step), BF)],
    )(place, heads, rest, own, near, far, *awaited)


def fill(rows, pieces):
    start = 0
    for piece in pieces:
        rows[start : start + piece.shape[0], :] = piece[...]
        start += piece.shape[0]


def rows_to_heads_kernel(
    place, own_rows, after, far_low, far_high, before, own, near, far,
    keep, send, rows, other,
):
    fill(rows, (own_rows, after, far_low, far_high, before))
    fill_other(place, near, far, other)
    mine = dot(rows[...], own[...], NT).astype(BF)
    rest = dot(rows[...], other[...], NT).astype(BF)
    for out, part in ((send, pick(place[2], rest, mine)), (keep, pick(place[2], mine, rest))):
        for r in range(4):
            out[line_rows(place, r), :] = part[r * 128 : r * 128 + 128]


def rows_to_heads(pieces, own, near, far, place):
    width = own.shape[1]
    return call(
        rows_to_heads_kernel,
        (1,),
        [whole(n, width) for n in (128, 128, 64, 64, 128, 256, 128, 128)],
        [whole(512, 256), whole(512, 256), whole(512, width)],
        [shape(512, 256), shape(512, 256), shape(512, width)],
        scratch=[pltpu.VMEM((256, width), BF)],
        vmem=BIG,
    )(place, *pieces, own, near, far)


def middle_kernel(place, a, b, c, d, low, gain, middle, normed, inv):
    total = sum((t[...].astype(F32) for t in (b, c, d)), a[...].astype(F32))
    total = low[...].astype(F32) + total
    middle[...] = total
    root = lax.rsqrt(jnp.mean(total * total, axis=1, keepdims=True) + EPS)
    inv[...] = root
    normed[...] = (total * root * gain[...]).astype(BF)


def middle_rows(terms, low, gain, place):
    width = low.shape[1]
    return call(
        middle_kernel,
        (1,),
        [whole(128, width)] * 4
        + [pl.BlockSpec((128, width), lambda i, p: (p[0], 0)), whole(1, width)],
        [whole(128, width), whole(128, width), whole(128, 1)],
        [shape(128, width, dtype=F32), shape(128, width), shape(128, 1, dtype=F32)],
    )(place, *terms, low, gain)


def middle_back_kernel(
    place, a, b, c, d, middle, inv, gain, cot, ready_a, ready_b, ready_c, d_middle, d_low, gain_part
):
    d_in = sum((t[...].astype(F32) for t in (b, c, d)), a[...].astype(F32))
    hat = middle[...] * inv[...]
    gain_part[...] = jnp.sum(d_in * hat, axis=0, keepdims=True)
    scaled = d_in * gain[...]
    mean = jnp.mean(scaled * hat, axis=1, keepdims=True)
    total = cot[...].astype(F32) + inv[...] * (scaled - hat * mean)
    d_middle[...] = total
    d_low[...] = total.astype(BF)


def middle_back(terms, middle, inv, gain, cot, ready, place):
    width = middle.shape[1]
    return call(
        middle_back_kernel,
        (1,),
        [whole(128, width)] * 5
        + [whole(128, 1), whole(1, width), whole(128, width)]
        + [ANYWHERE] * 3,
        [whole(128, width), whole(128, width), whole(1, width)],
        [shape(128, width, dtype=F32), shape(128, width), shape(1, width, dtype=F32)],
        vmem=BIG,
    )(place, *terms, middle, inv, gain, cot, *ready)


def cot_back_kernel(place, cot, own, near, far, out):
    def one(down):
        out[0] = dot(cot[...], down, NT)

    i = pl.program_id(0)
    pl.when(i == 0)(lambda: one(near[...].reshape(256, near.shape[2])))
    pl.when(i == 1)(lambda: one(far[...].reshape(256, far.shape[2])))
    pl.when(i >= 2)(lambda: one(own[...].reshape(256, own.shape[2])))


def own_pair(i, p):
    return (jnp.maximum(i - 2, 0), 0, 0)


def cot_back(cot, own, near, far, place):
    rows, width = cot.shape
    return call(
        cot_back_kernel,
        (4,),
        [
            whole(rows, width),
            pl.BlockSpec((2, 128, width), own_pair),
            whole(2, 128, width),
            whole(2, 128, width),
        ],
        pl.BlockSpec((1, rows, 256), lambda i, p: (i, 0, 0)),
        shape(4, rows, 256, dtype=F32),
        flops=5_000_000_000,
    )(place, cot, own, near, far)


def expert_kernel(
    place, own_rows, after, far_low, far_high, before, back, weights, own_gate, own_up, near, far,
    send, keep, rows, a, b, c, d, total, both_weights,
):
    i = pl.program_id(0)

    @pl.when(i == 0)
    def _():
        fill(rows, (own_rows, after, far_low, far_high, before))

    def two(gate, gate_start, up, up_start):
        for j in range(2):
            both_weights[:, j * 256 : j * 256 + 128] = gate[j, :, gate_start : gate_start + 128]
            both_weights[:, j * 256 + 128 : j * 256 + 256] = up[j, :, up_start : up_start + 128]
        lane = lax.broadcasted_iota(jnp.int32, weights.shape, 1)
        pre = dot(rows[...], both_weights[...], NN)
        grads, acts = [], []
        for j in range(2):
            named = lane == pair_of(i, place) * 2 + j
            weight = jnp.sum(jnp.where(named, weights[...], 0.0), axis=1, keepdims=True)
            gate = pre[:, j * 256 : j * 256 + 128]
            up = pre[:, j * 256 + 128 : j * 256 + 256]
            sig = 1.0 / (1.0 + jnp.exp(-gate))
            silu = gate * sig
            d_act = weight * back[0, :, j * 128 : j * 128 + 128]
            acts.append((weight * (silu * up)).astype(BF))
            grads.append((d_act * up * sig * (1.0 + gate * (1.0 - sig))).astype(BF))
            grads.append((d_act * silu).astype(BF))
        both = jnp.concatenate(grads, 1)
        hidden = jnp.concatenate([both] + acts, 1)
        kept = role(i, place, 2)

        @pl.when(kept == 1)
        def _():
            keep[0] = hidden

        @pl.when(kept == 0)
        def _():
            send[0] = hidden

        part = dot(both, both_weights[...], NT)

        @pl.when(i == 0)
        def _():
            total[...] = part

        @pl.when(i > 0)
        def _():
            total[...] += part

    pl.when(i == 0)(lambda: two(near, 0, near, 128))
    pl.when(i == 1)(lambda: two(far, 0, far, 128))
    pl.when(i >= 2)(lambda: two(own_gate, 0, own_up, 0))

    @pl.when(i == 3)
    def _():
        for r, out in enumerate((a, b, c, d)):
            out[...] = total[r * 128 : r * 128 + 128, :].astype(BF)


def expert_layer(pieces, back, weights, own_gate, own_up, near, far, place):
    rows, width = 512, pieces[0].shape[1]
    return call(
        expert_kernel,
        (4,),
        [whole(n, width) for n in (128, 128, 64, 64, 128)]
        + [
            pl.BlockSpec((1, rows, 256), lambda i, p: (i, 0, 0)),
            whole(rows, 4),
            pl.BlockSpec((2, width, 128), own_pair),
            pl.BlockSpec((2, width, 128), own_pair),
            whole(2, width, 256),
            whole(2, width, 256),
        ],
        [
            pl.BlockSpec((1, rows, 768), lambda i, p: (send_pair(i, p), 0, 0)),
            pl.BlockSpec((1, rows, 768), lambda i, p: (keep_pair(i, p), 0, 0)),
            whole(rows, width),
        ]
        + [whole(128, width)] * 4,
        [shape(2, rows, 768), shape(2, rows, 768), shape(rows, width)] + [shape(128, width)] * 4,
        scratch=[pltpu.VMEM((rows, width), F32), pltpu.VMEM((width, 512), BF)],
        vmem=44 * 1024 * 1024,
    )(place, *pieces, back, weights, own_gate, own_up, near, far)


def expert_out_kernel(place, send, keep, own, near, far, awaited, a, b, c, d, total):
    i = pl.program_id(0)

    def one(down):
        acts = pick(role(i, place, 2), keep[0], send[0])
        part = dot(acts, down, NN)

        @pl.when(i == 0)
        def _():
            total[...] = part

        @pl.when(i > 0)
        def _():
            total[...] += part

    pl.when(i == 0)(lambda: one(near[...].reshape(256, near.shape[2])))
    pl.when(i == 1)(lambda: one(far[...].reshape(256, far.shape[2])))
    pl.when(i >= 2)(lambda: one(own[...].reshape(256, own.shape[2])))

    @pl.when(i == 3)
    def _():
        for r, out in enumerate((a, b, c, d)):
            out[...] = total[r * 128 : r * 128 + 128, :].astype(BF)


def expert_out(send, keep, own, near, far, awaited, place):
    rows, width = 512, own.shape[2]
    return call(
        expert_out_kernel,
        (4,),
        [
            pl.BlockSpec((1, rows, 256), lambda i, p: (send_pair(i, p), 0, 2)),
            pl.BlockSpec((1, rows, 256), lambda i, p: (keep_pair(i, p), 0, 2)),
            pl.BlockSpec((2, 128, width), own_pair),
            whole(2, 128, width),
            whole(2, 128, width),
            ANYWHERE,
        ],
        [whole(128, width)] * 4,
        [shape(128, width)] * 4,
        scratch=[pltpu.VMEM((rows, width), F32)],
        flops=5_000_000_000,
    )(place, send, keep, own, near, far, awaited)


def attend_back_kernel(
    place, qkv, d_mine, d_rest, heads_mine, heads_rest, bias, lse, table_mine, table_rest,
    d_query, d_key, d_value, sums, key_sum, value_sum,
):
    rows = 256

    def unturn(grad, i):
        table = (table_mine if i < 2 else table_rest)[i % 2 * rows : i % 2 * rows + rows, :]
        return grad * table[:, :128] - pltpu.roll(grad, 64, 1) * table[:, 128:]

    masked = jnp.broadcast_to(bias[...], (8, 1024)).T[:, 0:1]
    for h in range(2):
        cols = slice(h * 128, h * 128 + 128)
        keys = qkv[:, 256 + h * 128 : 384 + h * 128]
        keys_turned = keys.T
        values = qkv[:, 512 + h * 128 : 640 + h * 128]
        for i in range(4):
            here = slice(i * rows, (i + 1) * rows)
            query = qkv[here, cols]
            inside = slice(i % 2 * rows, i % 2 * rows + rows)
            d_here = (d_mine if i < 2 else d_rest)[inside, cols]
            heads = (heads_mine if i < 2 else heads_rest)[inside, cols]
            scores = dot(keys, query, NT) * SCALE + masked
            probs = jnp.exp(scores - lse[h : h + 1, here])
            mean = d_here.astype(F32) * heads.astype(F32)
            mean = jnp.sum(mean.T, axis=0, keepdims=True)
            d_scores = (probs * (dot(values, d_here, NT) - mean)).astype(BF)
            value_part = dot(probs.astype(BF), d_here, NN)
            key_part = dot(d_scores, query, NN)
            if i == 0:
                value_sum[...] = value_part
                key_sum[...] = key_part
            else:
                value_sum[...] += value_part
                key_sum[...] += key_part
            d_turned = dot(keys_turned, d_scores, NN) * SCALE
            inner = jnp.sum(d_turned * query.astype(F32).T, axis=0, keepdims=True)
            if h == 0:
                sums[0:1, here] = inner
            else:
                sums[0:1, here] += inner
            d_query[here, cols] = unturn(d_turned.T, i)
        d_value[:, cols] = value_sum[...].astype(BF)
        for i in range(4):
            here = slice(i * rows, (i + 1) * rows)
            d_rot = key_sum[here, :] * SCALE
            inner = d_rot * qkv[here, 256 + h * 128 : 384 + h * 128].astype(F32)
            inner = jnp.sum(inner.T, axis=0, keepdims=True)
            if h == 0:
                sums[1:2, here] = inner
            else:
                sums[1:2, here] += inner
            d_key[here, cols] = unturn(d_rot, i)


def attend_back(qkv, d_mine, d_rest, heads_mine, heads_rest, bias, lse, table, place):
    return call(
        attend_back_kernel,
        (1,),
        [whole(1024, 1280)]
        + [whole(512, 256)] * 4
        + [whole(1, 1024), whole(2, 1024)]
        + [
            pl.BlockSpec((512, 256), lambda i, p: (p[1], 0)),
            pl.BlockSpec((512, 256), lambda i, p: (1 - p[1], 0)),
        ],
        [whole(1024, 256), whole(1024, 256), whole(1024, 256), whole(2, 1024)],
        [
            shape(1024, 256, dtype=F32),
            shape(1024, 256, dtype=F32),
            shape(1024, 256),
            shape(2, 1024, dtype=F32),
        ],
        scratch=[pltpu.VMEM((1024, 128), F32), pltpu.VMEM((1024, 128), F32)],
        vmem=BIG,
    )(place, qkv, d_mine, d_rest, heads_mine, heads_rest, bias, lse, table, table)


def raw_back_kernel(
    place, d_query, d_key, d_value, query_hat, key_hat, sums, inv_rows, gains, mine, rest, gain_parts
):
    step = pl.program_id(0)

    @pl.when(step == 0)
    def _():
        gain_parts[...] = jnp.zeros_like(gain_parts)

    mean, inv = columns_of(sums[...]), columns_of(inv_rows[...])
    parts = []
    for i, (grad, hat) in enumerate(((d_query, query_hat), (d_key, key_hat))):
        normed = hat[...].astype(F32)
        scaled = grad[...] * gains[i : i + 1, :]
        parts.append((inv[:, i : i + 1] * (scaled - normed * mean[:, i : i + 1])).astype(BF))
        gain_parts[i : i + 1, :] += jnp.sum(grad[...] * normed, axis=0, keepdims=True)
    total = jnp.concatenate(parts + [d_value[...]], 1)

    @pl.when(step < 2)
    def _():
        mine[...] = total

    @pl.when(step >= 2)
    def _():
        rest[...] = total


def raw_back(d_query, d_key, d_value, qkv, sums, inv_rows, gains, place):
    step = 256
    spec = lambda width, column=0: pl.BlockSpec((step, width), lambda i, p: (i, column))
    line = lambda: pl.BlockSpec((2, step), lambda i, p: (0, i))
    return call(
        raw_back_kernel,
        (4,),
        [
            spec(256),
            spec(256),
            spec(256),
            spec(256, 3),
            spec(256, 4),
            line(),
            line(),
            whole(2, 256),
        ],
        [
            pl.BlockSpec((step, 768), lambda i, p: (jnp.minimum(i, 1), 0)),
            pl.BlockSpec((step, 768), lambda i, p: (jnp.maximum(i - 2, 0), 0)),
            whole(2, 256),
        ],
        [shape(512, 768), shape(512, 768), shape(2, 256, dtype=F32)],
    )(place, d_query, d_key, d_value, qkv, qkv, sums, inv_rows, gains)


def back_kernel(place, *refs):
    rows_mine, rows_rest, d_mine, d_rest, raw_mine, raw_rest, raw_got = refs[:7]
    heads_mine, heads_rest, own_q, own_k, own_v, near, far, low, inv, gain_mlp, moe = refs[7:18]
    pieces, terms = refs[19:22], refs[22:26]
    mine, rest, total, d_own, d_other = refs[26:]
    i = pl.program_id(0)

    @pl.when(i == 0)
    def _():
        for r in range(4):
            mine[r * 128 : r * 128 + 128, :] = heads_mine[line_rows(place, r), :]
            rest[r * 128 : r * 128 + 128, :] = heads_rest[line_rows(place, r), :]
        d_own[...] = pick(place[2], raw_mine[...], raw_got[...])
        d_other[...] = pick(place[2], raw_got[...], raw_mine[...])

    @pl.when(i // 2 != 2)
    def _():
        qkv = dot(rows_mine[...], raw_mine[...], TN) + dot(rows_rest[...], raw_rest[...], TN)
        back = dot(d_mine[...], mine[...], TN) + dot(d_rest[...], rest[...], TN)
        grads = jnp.concatenate([qkv.astype(BF), back.astype(BF)], 1)
        for j, piece in zip((0, 1, 3), pieces):

            @pl.when(i // 2 == j)
            def _(piece=piece):
                piece[pl.ds(pl.multiple_of(lax.rem(i, 2) * 256, 256), 256), :] = grads

    other = jnp.where(i // 4 == place[1], near[...], far[...])
    own = jnp.concatenate([own_q[...], own_k[...], own_v[...]], 1)
    part = dot(d_own[...], own, NT) + dot(d_other[...], other, NT)
    total[...] = part
    gain = jnp.sum(part * (low[...].astype(F32) * inv[...]), axis=0, keepdims=True)
    zeros = jnp.zeros((14, gain.shape[1]), F32)
    gains = jnp.concatenate([gain, gain_mlp[...], zeros], 0).astype(BF)
    for r, out in enumerate(terms):
        out[0:128, :] = total[line_rows(place, r), :].astype(BF)
        out[128:144, :] = gains
    terms[2][144:272, :] = moe[...]


def far_back_kernel(
    place, rows_mine, rows_rest, d_mine, d_rest, raw_mine, raw_rest, heads_mine, heads_rest,
    out, mine, rest,
):
    @pl.when(pl.program_id(0) == 0)
    def _():
        for r in range(4):
            mine[r * 128 : r * 128 + 128, :] = heads_mine[line_rows(place, r), :]
            rest[r * 128 : r * 128 + 128, :] = heads_rest[line_rows(place, r), :]

    qkv = dot(rows_mine[...], raw_mine[...], TN) + dot(rows_rest[...], raw_rest[...], TN)
    back = dot(d_mine[...], mine[...], TN) + dot(d_rest[...], rest[...], TN)
    out[...] = jnp.concatenate([qkv.astype(BF), back.astype(BF)], 1)


def far_back(rows_mine, rows_rest, d_mine, d_rest, raw_mine, raw_rest, heads, place):
    block = lambda: pl.BlockSpec((512, 256), lambda i, p: (0, lax.rem(p[3] + 2, 4) * 2 + i))
    return call(
        far_back_kernel,
        (2,),
        [block(), block(), block(), block()] + [whole(512, 768)] * 2 + [whole(512, 256)] * 2,
        pl.BlockSpec((256, 1024), lambda i, p: (i, 0)),
        shape(512, 1024),
        scratch=[pltpu.VMEM((512, 256), BF), pltpu.VMEM((512, 256), BF)],
    )(place, rows_mine, rows_rest, d_mine, d_rest, raw_mine, raw_rest, *heads)


def back(
    rows_mine, rows_rest, d_mine, d_rest, raw_mine, raw_rest, raw_got, heads,
    own, near, far, low, inv, gain_mlp, moe, awaited, place,
):
    rows, width, step = 512, low.shape[1], 256
    block = lambda: pl.BlockSpec(
        (rows, step), lambda i, p: (0, lax.rem(p[3] + i // 2, 4) * 2 + lax.rem(i, 2))
    )
    half = lambda: pl.BlockSpec((step, 768), lambda i, p: (lax.rem(i, 4), 0))
    tile = lambda: pl.BlockSpec((step, 256), lambda i, p: (i, 0))
    column = lambda n: pl.BlockSpec((n, step), lambda i, p: (0, i))
    return call(
        back_kernel,
        (width // step,),
        [block(), block(), block(), block()]
        + [whole(rows, 768)] * 3
        + [whole(rows, 256)] * 2
        + [tile(), tile(), tile(), half(), half(), column(rows), whole(rows, 1), column(1), column(128), ANYWHERE],
        [whole(512, 1024)] * 3 + [column(n) for n in (144, 144, 272, 144)],
        [shape(512, 1024)] * 3 + [shape(n, width) for n in (144, 144, 272, 144)],
        scratch=[
            pltpu.VMEM((rows, 256), BF),
            pltpu.VMEM((rows, 256), BF),
            pltpu.VMEM((rows, step), F32),
            pltpu.VMEM((rows, 768), BF),
            pltpu.VMEM((rows, 768), BF),
        ],
        flops=20_000_000_000,
    )(
        place, rows_mine, rows_rest, d_mine, d_rest, raw_mine, raw_rest, raw_got, *heads,
        *own, near, far, low, inv, gain_mlp, moe, awaited,
    )


def last_rows_kernel(place, *refs):
    d_terms, moe_terms = refs[:4], refs[4:7]
    d_middle, middle, low, inv, gain = refs[7:12]
    parts, gains, rows = refs[-3:]
    total = sum((t[0:144].astype(F32) for t in d_terms[1:]), d_terms[0][...].astype(F32))
    gains[...] = total[128:130]
    d_in = total[:128]
    hat = low[...].astype(F32) * inv[...]
    scaled = d_in * gain[...]
    mean = jnp.mean(scaled * hat, axis=1, keepdims=True)
    rows[1] = (d_middle[...] + inv[...] * (scaled - hat * mean)).astype(BF)
    moe = sum((t[...].astype(F32) for t in moe_terms), d_terms[2][144:272].astype(F32))
    rows[0] = (middle[...] + moe).astype(BF)
    for i in range(8):
        parts[i] = rows[:, :, i * 256 : i * 256 + 256]


def last_rows(d_terms, moe_terms, d_middle, middle, low, inv, gain, awaited, place):
    width = low.shape[1]
    mine = lambda n: pl.BlockSpec((128, n), lambda i, p: (p[0], 0))
    return call(
        last_rows_kernel,
        (1,),
        [whole(n, width) for n in (144, 144, 272, 144)]
        + [whole(128, width)] * 5
        + [mine(width), mine(1), whole(1, width)]
        + [ANYWHERE] * len(awaited),
        [whole(8, 2, 128, 256), whole(2, width)],
        [shape(8, 2, 128, 256), shape(2, width, dtype=F32)],
        scratch=[pltpu.VMEM((2, 128, width), BF)],
        vmem=BIG,
    )(place, *d_terms, *moe_terms, d_middle, middle, low, inv, gain, *awaited)


def settle_attention_kernel(place, *refs):
    here, there = refs[:4], refs[4:8]
    query, key, value, back, small = refs[9:]
    i = pl.program_id(0)

    @pl.when(i == 0)
    def _():
        small[...] = jnp.zeros_like(small)

    def one(mine, rest):
        mine, rest = mine[0].astype(F32), rest[0].astype(F32)
        first = pick(place[1], rest[:128], mine[:128])
        second = pick(place[1], mine[:128], rest[:128])
        total = jnp.concatenate([first, second], 0)
        query[...] = total[:, :256]
        key[...] = total[:, 256:512]
        value[...] = total[:, 512:768]
        back[...] = total[:, 768:].T
        mine, rest = mine[128:], rest[128:]
        row = lax.broadcasted_iota(jnp.int32, mine.shape, 0)
        small[...] += jnp.where(row < 4, mine + rest, pick(place[2], mine, rest))

    for r in range(4):

        @pl.when(lax.rem(i // 2 + 4 - place[3], 4) == r)
        def _(r=r):
            one(here[r], there[r])


def settle_attention(here, there, awaited, place):
    piece = lambda: pl.BlockSpec((1, 144, 1024), lambda i, p: (lax.rem(i + p[4], 2), 0, 0))
    rows = lambda: pl.BlockSpec((256, 256), lambda i, p: (i, 0))
    return call(
        settle_attention_kernel,
        (8,),
        [piece() for _ in range(8)] + [ANYWHERE],
        [rows(), rows(), rows(), pl.BlockSpec((256, 256), lambda i, p: (0, i)), whole(16, 1024)],
        [shape(2048, 256, dtype=F32)] * 3
        + [shape(256, 2048, dtype=F32), shape(16, 1024, dtype=F32)],
    )(place, *here, *there, awaited)


def settle_experts_kernel(place, gu_mine, gu_got, down_mine, down_got, gate, up, down):
    total = pick(place[2], gu_mine[0], gu_got[0]).astype(F32)
    for j in range(2):
        gate[j] = total[:, j * 256 : j * 256 + 128]
        up[j] = total[:, j * 256 + 128 : j * 256 + 256]
    total = pick(place[2], down_mine[0], down_got[0]).astype(F32)
    down[...] = total.reshape(down.shape)


def settle_experts(gu_mine, gu_got, down_mine, down_got, place):
    def step(i, p, mine):
        return jnp.where(p[2] == mine, i, 0)

    def tall(mine):
        def index(i, p):
            j = step(i, p, mine)
            return (j // 4, lax.rem(j, 4), 0)

        return pl.BlockSpec((1, 512, 512), index)

    def flat(mine):
        def index(i, p):
            j = step(i, p, mine)
            return (j // 4, 0, lax.rem(j, 4))

        return pl.BlockSpec((1, 256, 512), index)

    thin = lambda: pl.BlockSpec((2, 512, 128), lambda i, p: (i // 4, lax.rem(i, 4), 0))
    return call(
        settle_experts_kernel,
        (8,),
        [tall(1), tall(0), flat(1), flat(0)],
        [thin(), thin(), pl.BlockSpec((2, 128, 512), lambda i, p: (i // 4, 0, lax.rem(i, 4)))],
        [shape(4, 2048, 128, dtype=F32)] * 2 + [shape(4, 128, 2048, dtype=F32)],
        flops=20_000_000_000,
    )(place, gu_mine, gu_got, down_mine, down_got)


def choice_weights(ids, gates, experts, capacity):
    named = ids[:, :, None] == jnp.arange(experts, dtype=jnp.int32)
    count = jnp.sum(named.astype(F32), axis=1)
    tokens = ids.shape[0]
    earlier = (
        jnp.arange(tokens, dtype=jnp.int32)[:, None] > jnp.arange(tokens, dtype=jnp.int32)[None, :]
    ).astype(BF)
    place = jnp.dot(earlier, count.astype(BF), preferred_element_type=F32)
    weight = jnp.sum(jnp.where(named, gates[:, :, None], 0.0), axis=1)
    return jnp.where(place < capacity, weight, 0.0)


def local(
    hidden_in,
    cotangent,
    sequence_order,
    seq_lengths,
    expert_ids,
    gate_weights,
    w_query,
    w_key,
    w_value,
    w_output,
    gain_attn,
    gain_query,
    gain_key,
    gain_mlp,
    w_gate,
    w_up,
    w_down,
):
    zl, y, c, zh, x = (lax.axis_index(a) for a in AXES)
    same = c == zh
    length = hidden_in.shape[1]
    half = length // 2
    experts = w_gate.shape[0]
    width = w_query.shape[0]
    place = jnp.stack([x, c, same.astype(jnp.int32), y, zl, zh]).astype(jnp.int32)
    sequence = (zl * SIZES[1] + y) * 2 + zh
    tokens_here = seq_lengths[sequence]
    ids_here = expert_ids[sequence]
    gates_here = gate_weights[sequence]

    x_dealt = deal_in(hidden_in[0], zh)
    qkv_own = [w_query, w_key, w_value]
    qkv_near = other_half(qkv_own, c, x_dealt)
    x_pieces = gather_x(x_dealt)
    cot_dealt = deal_in(cotangent[0], zh, x_pieces[1])
    gains_own = jnp.stack([gain_query, gain_key], 0)
    gains_other = other_half_chip(gains_own)

    table = jnp.asarray(rope_tables(length))
    positions = (jnp.arange(length, dtype=jnp.int32) + c * half) % length
    bias = jnp.where(positions < tokens_here, 0.0, -1e30).astype(F32)
    weight_all = choice_weights(ids_here, gates_here, experts, length * 2 // experts)
    weight_here = lax.dynamic_slice_in_dim(weight_all, c * half, half, 0)
    weight_here = lax.dynamic_slice_in_dim(
        jnp.concatenate([weight_here, weight_here], 0), x * (half // 4), half, 0
    )

    x_low, attn_in, inv_one = norm_rows(x_pieces, place, gain_attn[None, :])
    qkv_near, cot_first = tie([qkv_near, cot_dealt], attn_in)
    qkv_far = other_core(qkv_near)
    out_near = other_half([w_output], c, attn_in)
    raw_send, raw_keep, squares = project(attn_in, qkv_own, qkv_near, qkv_far, out_near, place)
    (gains_other,) = tie([gains_other], squares)
    gains_keep = jnp.where(same, gains_own, gains_other)
    gains_qk = jnp.concatenate([gains_keep, jnp.where(same, gains_other, gains_own)], 0)
    inv_qk = lax.rsqrt(sum_x(squares[:2]) / width + EPS)
    (out_near,) = tie([out_near], inv_qk)
    down_near = other_half([w_down], c, out_near)
    gu_near = other_half([w_gate, w_up], c, out_near)
    cot_pieces = gather_x(cot_first, inv_qk)
    ready_send, ready_keep = prep(
        raw_send,
        raw_keep,
        inv_qk,
        gains_qk,
        table,
        (cot_pieces[1], cot_pieces[4]),
        place,
    )
    ready_rest = other_core(ready_send)
    qkv, heads_mine, heads_rest, lse = attend(ready_keep, ready_rest, bias[None, :], place)
    heads_got = other_core(heads_rest)
    out_near, inv_tied = tie([out_near, inv_qk], heads_got)
    out_far = other_core(out_near)
    inv_qk_rest = other_core(inv_tied)
    cot = place_rows(cot_pieces, place)
    attn_terms = send_x(
        heads_to_rows(heads_mine, heads_got, w_output, out_near, out_far, (cot, heads_got), place)
    )
    attn_in, cot = tie([attn_in, cot], heads_got)
    attn_in_rest = other_core(attn_in)
    cot_rest = other_core(cot)

    middle, moe_own, inv_two = middle_rows(attn_terms, x_low, gain_mlp[None, :], place)
    moe_pieces = gather_x(moe_own)
    gu_near, down_near = tie([gu_near, down_near], moe_pieces[1])
    gu_near, down_near = tie([gu_near, down_near], moe_pieces[4])
    down_far = other_core(down_near)
    cot_down = cot_back(cot, w_down, down_near, down_far, place)
    gu_far = other_core(gu_near)
    hidden_send, hidden_keep, moe_in, *d_moe_terms = expert_layer(
        moe_pieces, cot_down, weight_here, w_gate, w_up, gu_near, gu_far, place
    )
    d_moe_terms = send_x(d_moe_terms)
    moe_terms = expert_out(
        hidden_send, hidden_keep, w_down, down_near, down_far, hidden_keep, place
    )
    hidden_all = jnp.concatenate([hidden_keep, other_core(hidden_send)], 1)
    moe_all = jnp.concatenate([moe_in, other_core(moe_in)], 0)
    cot_all = jnp.concatenate([cot, cot_rest], 0)
    grad_gate_up = jnp.einsum(
        "td,etf->edf", moe_all, hidden_all[:, :, :512], preferred_element_type=F32
    ).astype(BF)
    grad_down = jnp.einsum(
        "etf,td->efd", hidden_all[:, :, 512:], cot_all, preferred_element_type=F32
    ).astype(BF)

    d_middle, d_own, gain_mlp_part = middle_back(
        d_moe_terms,
        middle,
        inv_two,
        gain_mlp[None, :],
        cot,
        (grad_gate_up, grad_down, moe_terms[0]),
        place,
    )
    grad_gate_up, grad_down = lax.psum((grad_gate_up, grad_down), GROUPS)
    d_pieces = gather_x(d_own)
    d_heads_keep, d_heads_send, d_attn = rows_to_heads(
        d_pieces, w_output, out_near, out_far, place
    )
    d_heads_rest = other_core(d_heads_send)
    *moe_terms, d_attn = tie(list(moe_terms) + [d_attn], d_heads_rest)
    moe_after, moe_before = along(moe_terms[1], "x", 1), along(moe_terms[3], "x", -1)
    d_attn_rest = other_core(d_attn)
    d_query, d_key, d_value, sums = attend_back(
        qkv,
        d_heads_keep,
        d_heads_rest,
        heads_mine,
        heads_rest,
        bias[None, :],
        lse,
        table,
        place,
    )
    (sums,) = tie([sums], moe_after)
    (sums,) = tie([sums], moe_before)
    sums_rest = other_core(sums)
    sums = sums + jnp.concatenate([sums_rest[:, half:], sums_rest[:, :half]], 1)
    sums = sum_x(sums) / width
    raw_mine, raw_rest, gain_qk_parts = raw_back(
        d_query,
        d_key,
        d_value,
        qkv,
        sums,
        jnp.concatenate([inv_qk, inv_qk_rest], 1),
        gains_keep,
        place,
    )
    raw_got = other_core(raw_rest)
    far_piece = far_back(
        attn_in,
        attn_in_rest,
        d_attn,
        d_attn_rest,
        raw_mine,
        raw_rest,
        (heads_mine, heads_rest),
        place,
    )
    pieces = back(
        attn_in,
        attn_in_rest,
        d_attn,
        d_attn_rest,
        raw_mine,
        raw_rest,
        raw_got,
        (heads_mine, heads_rest),
        qkv_own,
        qkv_near,
        qkv_far,
        x_low,
        inv_one,
        gain_mlp_part,
        moe_terms[2],
        far_piece,
        place,
    )
    weight_terms = send_y([pieces[0], pieces[1], far_piece, pieces[2]])
    d_in_terms = send_x(pieces[3:])
    moe_terms = [moe_terms[0], moe_after, moe_before]
    rows_dealt, gains = last_rows(
        d_in_terms,
        moe_terms,
        d_middle,
        middle,
        x_low,
        inv_one,
        gain_attn[None, :],
        weight_terms[1:],
        place,
    )
    dealt = deal_line(rows_dealt)
    grad_gate_up, grad_down = tie([grad_gate_up, grad_down], rows_dealt)
    total = sum((t.astype(F32) for t in weight_terms[1:]), weight_terms[0].astype(F32)).astype(BF)
    near, far = to_shard(total, zl, same)
    total = (near.astype(F32) + far.astype(F32)).astype(BF)
    first = c == 0
    got = other_core(jnp.where(first, total[128:], total[:128]))
    mine = jnp.where(first, total[:128], total[128:]).astype(F32) + got.astype(F32)
    small = jnp.concatenate([gains.reshape(-1), gain_qk_parts.reshape(-1)])
    small = (small + lax.ppermute(small, "zh", [(0, 1), (1, 0)])).reshape(9, 512)
    small = jnp.concatenate([small.reshape(-1), jnp.zeros((11776,), F32)]).reshape(16, 1024)
    (mine,) = tie([jnp.concatenate([mine, small], 0).astype(BF)], dealt)
    here = from_groups(mine)
    (dealt,) = tie([dealt], here[0])
    output, grad_input = deal_out(dealt, same)

    grad_gate, grad_up, grad_down = settle_experts(
        grad_gate_up, settle(grad_gate_up), grad_down, settle(grad_down), place
    )
    here = tie(list(here), grad_down)
    grad_query, grad_key, grad_value, grad_output, small = settle_attention(
        here, [other_core(t) for t in here], grad_down, place
    )
    small = small.reshape(-1)
    return (
        output[None],
        grad_input[None],
        grad_query,
        grad_key,
        grad_value,
        grad_output,
        small[:width],
        small[2 * width : 2 * width + 256],
        small[2 * width + 256 : 2 * width + 512],
        small[width : 2 * width],
        grad_gate,
        grad_up,
        grad_down,
    )


def solution(mesh):
    fine = Mesh(mesh.devices.reshape(SIZES), AXES)
    columns = P(None, TENSOR)
    placed = (
        P(DP, None, TENSOR),
        P(DP, None, TENSOR),
        P(),
        P(),
        P(),
        P(),
        columns,
        columns,
        columns,
        P(TENSOR, None),
        P(),
        P(TENSOR),
        P(TENSOR),
        P(),
        P(None, None, TENSOR),
        P(None, None, TENSOR),
        P(None, TENSOR, None),
    )
    return jax.shard_map(
        local,
        mesh=fine,
        in_specs=placed,
        out_specs=placed[:2]
        + (columns, columns, columns, P(TENSOR, None), P(), P(TENSOR), P(TENSOR), P())
        + placed[14:],
        check_vma=False,
    )
```
